32 devices in a mesh: dp: 16 (over z, y, core), tensor: 2 (over x).
Axes of the slice: x: 2, y: 2, z: 4, core: 2. Of those that a mesh axis runs over, the one named last changes fastest.
Arguments:
- residual_in: bfloat16 [4096, 2048], P(('dp', 'tensor')), may hold values from -6 to 6
- seg_ids: int32 [4096], P('dp'), may hold values from -1 to 2, as said below
- attn_gain: bfloat16 [2048], P('dp'), may hold values from 0.099609375 to 1.8984375
- w_qkv: bfloat16 [3, 2048, 2048], P(None, 'dp', 'tensor'), may hold values from -0.125 to 0.125
- w_out: bfloat16 [2048, 2048], P('tensor', 'dp'), may hold values from -2 to 2
- ffn_gain: bfloat16 [2048], P('dp'), may hold values from 0.099609375 to 1.8984375
- w_gate_up: bfloat16 [2, 2048, 8192], P(None, 'dp', 'tensor'), may hold values from -0.125 to 0.125
- w_down: bfloat16 [8192, 2048], P('tensor', 'dp'), may hold values from -0.0625 to 0.0625
- cotangent: bfloat16 [4096, 2048], P(('dp', 'tensor')), may hold values from -6 to 6
Outputs:
- block_out: bfloat16 [4096, 2048], P(('dp', 'tensor'))
- input_grad: float32 [4096, 2048], P(('dp', 'tensor'))
- attn_gain_grad: float32 [2048], P('dp')
- w_qkv_grad: float32 [3, 2048, 2048], P(None, 'dp', 'tensor')
- w_out_grad: float32 [2048, 2048], P('tensor', 'dp')
- ffn_gain_grad: float32 [2048], P('dp')
- w_gate_up_grad: float32 [2, 2048, 8192], P(None, 'dp', 'tensor')
- w_down_grad: float32 [8192, 2048], P('tensor', 'dp')
The draws below stay inside these ranges and needn't reach their ends.
Inputs may be any that keep to these rules, and one draw needn't show every extreme that they name: `seg_ids`: each aligned group of 256 rows (the rows of one dp index) holds one to three sequences as runs of non-decreasing ids, followed by padding rows of -1 up to the group's end; a sequence always covers rows 127 and 128 of its group; in one group a single sequence fills all 256 rows.
All inputs are finite; a program needn't handle non-finite values.
Results may differ from the reference program's by a relative error of at most 0.012.
The reference program's roundings to bfloat16 on the way count: a program that leaves them out, or rounds other values in their place, can miss the bound.
Values may be sent and summed in bfloat16 or wider, within the bound.
A program may use at most 320 MiB of HBM per device.

```python
import jax
import jax.numpy as jnp
from jax import lax

D = 2048
H = 32
HD = 64
FF = 8192
TOK_DEV = 128
BLOCK = 128
HH = 2048
TOKENS = 4096


def draw_seg_ids(key, part):
    key = jax.random.fold_in(key, 7)
    group_rows = 2 * TOK_DEV
    groups = TOKENS // group_rows
    blocks = group_rows // BLOCK
    subkeys = jax.random.split(key, 5)
    used_rows = jax.random.randint(subkeys[0], (groups,), blocks // 2 + 1, blocks + 1) * BLOCK
    whole_group = jax.random.randint(subkeys[1], (), 0, groups)
    seq_start = jax.random.randint(subkeys[2], (groups,), 0, TOK_DEV)
    seq_split = jax.random.randint(subkeys[3], (groups,), TOK_DEV + 1, used_rows + 1)
    seq_end = jax.random.randint(subkeys[4], (groups,), seq_split, used_rows + 1)
    is_chosen = jnp.arange(groups) == whole_group
    seq_start = jnp.where(is_chosen, 0, seq_start)
    seq_split = jnp.where(is_chosen, group_rows, seq_split)
    seq_end = jnp.where(is_chosen, group_rows, seq_end)
    row_index = jnp.arange(group_rows)[None, :]
    doc_label = (row_index >= seq_start[:, None]).astype(jnp.int32) + (row_index >= seq_split[:, None]).astype(jnp.int32)
    return jnp.where(row_index < seq_end[:, None], doc_label, -1).reshape(-1).astype(jnp.int32)


def strengthened(entries, key, source, target, shards_of, factor):
    owner, partner = [(jnp.arange(entries.shape[position]) // (entries.shape[position] // shards_of)).reshape([-1 if axis == position else 1 for axis in range(entries.ndim)]) for position in (source, target)]
    chosen = jax.random.permutation(key, shards_of)[partner]
    strong = (owner == chosen) | (owner == (partner + shards_of // 2) % shards_of)
    return jnp.where(strong, factor * entries, entries)


def block_levels(stream_key, dims, cuts, least, top_value):
    gain = 1.0
    for dim, parts in cuts:
        heights = jax.random.uniform(jax.random.fold_in(jax.random.fold_in(stream_key, 6), dim), (parts,), jnp.float32, least / len(cuts), top_value / len(cuts))
        gain = gain * jnp.repeat(jnp.exp(heights), dims[dim] // parts).reshape((-1,) + (1,) * (len(dims) - 1 - dim))
    return gain


def scatter_about(own_key, shape, scale, bound, shards=(), kind=jnp.bfloat16):
    entries = jax.random.normal(own_key, shape, jnp.float32) * scale
    if len(shards) > 0:
        entries = block_levels(own_key, shape, shards, -0.22, 0.18) * entries
    return jnp.clip(entries, min=-bound, max=bound).astype(kind)


def gaussian_with(key, shape, scale, bound, shards, heavy, held_as=jnp.bfloat16):
    values = scale * jax.random.normal(key, shape, jnp.float32)
    if shards:
        values = values * block_levels(key, shape, shards, -0.22, 0.18)
    return jnp.clip(strengthened(values, jax.random.fold_in(key, 3), *heavy), -bound, bound).astype(held_as)


def setup_inputs(seed: int = 0) -> dict:
    key_of = jax.random.split(jax.random.key(seed), 10)
    return {
        "residual_in": scatter_about(key_of[0], (TOKENS, D), 1.0, 6.0, ((0, 32),)),
        "seg_ids": draw_seg_ids(jax.random.fold_in(key_of[9], 71), 0),
        "attn_gain": jnp.clip(1.0 + 0.18 * jax.random.normal(key_of[2], (D,), jnp.float32), 0.099609375, 1.8984375).astype(jnp.bfloat16),
        "w_qkv": scatter_about(key_of[3], (3, D, HH), D ** -0.5, 0.125, ((1, 16), (2, 2))),
        "w_out": scatter_about(key_of[4], (HH, D), (max(HH // 256, 1)) ** -0.5, 2.0, ((0, 2), (1, 16))),
        "ffn_gain": jnp.clip(1.0 + 0.18 * jax.random.normal(key_of[5], (D,), jnp.float32), 0.099609375, 1.8984375).astype(jnp.bfloat16),
        "w_gate_up": scatter_about(key_of[6], (2, D, FF), D ** -0.5, 0.125, ((1, 16), (2, 2))),
        "w_down": scatter_about(key_of[7], (FF, D), FF ** -0.5, 0.0625, ((0, 2), (1, 16))),
        "cotangent": gaussian_with(key_of[8], (TOKENS, D), 1.0, 6.0, ((0, 32),), (0, 1, 32, 2.75)),
    }


EPSILON = 1e-05
ROPE_BASE = 130000.0
PRECISE = lax.Precision.HIGHEST

@jax.custom_vjp
def low(v):
    return lax.optimization_barrier(v.astype(jnp.bfloat16)).astype(jnp.float32)

@jax.custom_vjp
def low_back(v):
    return v

def low_keep(v):
    return (low(v), None)

def low_pass(kept, grad):
    return (grad,)

def back_keep(v):
    return (v, None)

def back_low(kept, grad):
    return (low(grad),)
low.defvjp(low_keep, low_pass)
low_back.defvjp(back_keep, back_low)

def positions(segments):
    row_index = jnp.arange(segments.shape[1], dtype=jnp.int32)[None, :]
    previous = jnp.concatenate([segments[:, :1] - 1, segments[:, :-1]], axis=1)
    run_start = lax.cummax(jnp.where(segments != previous, row_index, 0), axis=1)
    return (row_index - run_start).astype(jnp.int32)

def rope_tables(places, head_dim):
    half_dim = head_dim // 2
    frequency = ROPE_BASE ** (-(jnp.arange(half_dim, dtype=jnp.float32) * 2.0 / head_dim))
    angles = places.astype(jnp.float32)[:, None, None] * frequency[None, None, :]
    return (jnp.cos(angles), jnp.sin(angles))

def rotate(field, cosine, sine_table):
    half_dim = field.shape[-1] // 2
    lower_half = field[..., :half_dim]
    upper_half = field[..., half_dim:]
    return jnp.concatenate([lower_half * cosine - upper_half * sine_table, upper_half * cosine + lower_half * sine_table], axis=-1)

def normalize(field):
    return field * lax.rsqrt(lax.optimization_barrier(jnp.mean(field * field, axis=-1, keepdims=True)) + EPSILON)

def attend(block):
    queries, key_rows, value_rows, segments = block
    row_index = jnp.arange(queries.shape[0])
    allowed = (segments[:, None] == segments[None, :]) & (row_index[:, None] >= row_index[None, :])
    scores = jnp.einsum('qhd,khd->hqk', queries, key_rows, precision=PRECISE) * queries.shape[-1] ** (-0.5)
    scores = jnp.where(allowed[None], low_back(scores), -1e+30)
    weights = jax.nn.softmax(scores, axis=-1)
    return jnp.einsum('hqk,khd->qhd', low(weights), value_rows, precision=PRECISE)

def forward(residual, attn_gain, w_qkv, w_out, ffn_gain, w_gate_up, w_down, segments):
    row_count = residual.shape[0]
    normed = low(normalize(residual) * attn_gain)
    projected = jnp.einsum('rd,cde->cre', normed, w_qkv, precision=PRECISE)
    cosine, sine_table = rope_tables(positions(segments).reshape(-1), HD)
    head_shape = (row_count, H, HD)
    queries = low(rotate(low_back(projected[0]).reshape(head_shape), cosine, sine_table))
    key_rows = low(rotate(low_back(projected[1]).reshape(head_shape), cosine, sine_table))
    value_rows = low(low_back(projected[2])).reshape(head_shape)
    grouped = (segments.shape[0], segments.shape[1], H, HD)
    attended = lax.map(jax.checkpoint(attend), (queries.reshape(grouped), key_rows.reshape(grouped), value_rows.reshape(grouped), segments))
    attended = low(low_back(attended.reshape(row_count, H * HD)))
    mixed = residual + low_back(jnp.dot(attended, w_out, precision=PRECISE))
    normed_ffn = low(normalize(mixed) * ffn_gain)
    gate_up = jnp.einsum('rd,cde->cre', normed_ffn, w_gate_up, precision=PRECISE)
    hidden = low(jax.nn.silu(low_back(gate_up[0])) * low_back(gate_up[1]))
    return mixed + low_back(jnp.dot(hidden, w_down, precision=PRECISE))

def reference(residual_in, seg_ids, attn_gain, w_qkv, w_out, ffn_gain, w_gate_up, w_down, cotangent):
    segments = seg_ids.reshape(-1, 2 * TOK_DEV)
    live_rows = (seg_ids >= 0).astype(jnp.float32)
    primals = tuple((operand.astype(jnp.float32) for operand in (residual_in, attn_gain, w_qkv, w_out, ffn_gain, w_gate_up, w_down)))

    def wrapped(*operands):
        return forward(*operands, segments)
    result, pullback = jax.vjp(wrapped, *primals)
    gradients = pullback(cotangent.astype(jnp.float32) * live_rows[:, None])
    return (result.astype(jnp.bfloat16), gradients[0], gradients[1], gradients[2], gradients[3], gradients[4], gradients[5], gradients[6])
```

```python
import functools

import jax
import jax.numpy as jnp
from jax import lax
from jax.experimental import pallas as pl
from jax.experimental.pallas import tpu as pltpu
from jax.sharding import PartitionSpec as P

HD = 64
EPSILON = 1e-05
ROPE_BASE = 130000.0
MESH = pl.DeviceIdType.MESH
ANY = pl.BlockSpec(memory_space=pl.ANY)
VM = pl.BlockSpec(memory_space=pltpu.VMEM)
F32 = jnp.float32
BF16 = jnp.bfloat16
LANES = 128
NT = (((1,), (1,)), ((), ()))
TN = (((0,), (0,)), ((), ()))
NN = (((1,), (0,)), ((), ()))


def dot(a, b, dims=NN):
    return lax.dot_general(a, b, dims, preferred_element_type=F32)


def when(cond, action):
    if cond is None:
        action()
    else:
        pl.when(cond)(action)


class Net:
    def __init__(self, dp, send_sems, local_sems):
        self.n = dp // 4
        self.dp_index = lax.axis_index("dp")
        self.x = lax.axis_index("tensor")
        self.z = self.dp_index // 4
        self.y = (self.dp_index // 2) % 2
        self.c = self.dp_index % 2
        self.send_sems = send_sems
        self.local_sems = local_sems
        self.sent = 0
        self.moved = 0
        self.pending = []
        self.kept = []

    def place(self, z, y, c):
        return (z * 2 + y) * 2 + c

    def device(self, z=None, y=None, c=None, x=None):
        z = self.z if z is None else z
        y = self.y if y is None else y
        c = self.c if c is None else c
        x = self.x if x is None else x
        return (self.place(z, y, c), x)

    def greet(self, devices):
        barrier = pltpu.get_barrier_semaphore()
        for device in devices:
            pl.semaphore_signal(barrier, inc=1, device_id=device, device_id_type=MESH)
        pl.semaphore_wait(barrier, len(devices))

    def send(self, src, dst, recv_sem, device, cond=None):
        sem = self.send_sems.at[self.sent]
        self.sent += 1
        copy = pltpu.make_async_remote_copy(
            src_ref=src, dst_ref=dst, send_sem=sem, recv_sem=recv_sem, device_id=device, device_id_type=MESH
        )
        when(cond, copy.start)
        self.pending.append((cond, copy))

    def recv(self, dst, recv_sem):
        pltpu.make_async_remote_copy(
            src_ref=dst, dst_ref=dst, send_sem=self.send_sems.at[0], recv_sem=recv_sem,
            device_id=self.device(c=1 - self.c), device_id_type=MESH,
        ).wait_recv()

    def local(self, src, dst, cond=None):
        sem = self.local_sems.at[self.moved]
        self.moved += 1
        copy = pltpu.make_async_copy(src, dst, sem)
        when(cond, copy.start)
        self.kept.append((cond, copy))
        return copy

    def settle(self, copy):
        self.kept = [entry for entry in self.kept if entry[1] is not copy]
        copy.wait()

    def drain(self):
        assert self.sent <= self.send_sems.shape[0] and self.moved <= self.local_sems.shape[0]
        for cond, copy in self.pending:
            when(cond, copy.wait_send)
        for cond, copy in self.kept:
            when(cond, copy.wait)


class Gather:
    def __init__(self, net, own, at, sems):
        self.net, self.own, self.at = net, own, at
        self.sems = sems

    def spread(self, block, src, ysend=True):
        net = self.net
        here = net.place(block, net.y, net.c)
        net.send(src, self.at(here), self.sems.at[1, block], net.device(y=1 - net.y))
        net.send(src, self.at(here), self.sems.at[2 + net.y, block], net.device(c=1 - net.c))

    def start(self):
        net = self.net
        here = self.at(net.dp_index)
        net.send(self.own, here, self.sems.at[0, net.z], net.device(z=net.z + 1), net.z < net.n - 1)
        net.send(self.own, here, self.sems.at[0, net.z], net.device(z=net.z - 1), net.z > 0)
        self.spread(net.z, self.own)
        self.kept = net.local(self.own, here)

    def step(self, s):
        net = self.net
        for sign in (1, -1):
            block = net.z - s * sign
            valid = jnp.logical_and(block >= 0, block < net.n)
            nxt = net.z + sign
            more = jnp.logical_and(nxt >= 0, nxt < net.n)
            here = self.at(net.place(block, net.y, net.c))

            @pl.when(valid)
            def _():
                net.recv(here, self.sems.at[0, block])

            net.send(here, here, self.sems.at[0, block], net.device(z=nxt), jnp.logical_and(valid, more))
            net.send(here, here, self.sems.at[1, block], net.device(y=1 - net.y), valid)
            net.send(here, here, self.sems.at[2 + net.y, block], net.device(c=1 - net.c), valid)

    def cross(self, block):
        net = self.net
        there = self.at(net.place(block, 1 - net.y, net.c))
        net.recv(there, self.sems.at[1, block])
        net.send(there, there, self.sems.at[3 - net.y, block], net.device(c=1 - net.c))

    def cross_step(self, s):
        net = self.net
        for sign in (1, -1):
            block = net.z - s * sign
            valid = jnp.logical_and(block >= 0, block < net.n)
            there = self.at(net.place(block, 1 - net.y, net.c))

            @pl.when(valid)
            def _():
                net.recv(there, self.sems.at[1, block])

            net.send(there, there, self.sems.at[3 - net.y, block], net.device(c=1 - net.c), valid)

    def finish(self, block):
        net = self.net
        for y in (0, 1):
            net.recv(self.at(net.place(block, y, 1 - net.c)), self.sems.at[2 + y, block])


class Exchange:
    def __init__(self, net, part, at, sems):
        self.net, self.part, self.at = net, part, at
        self.sems = sems

    def start(self):
        net = self.net
        here = self.at(net.dp_index)
        for d in list(range(1, net.n)):
            to = (net.z + d) % net.n
            net.send(self.part(to), here, self.sems.at[0, net.z], net.device(z=to))
        own = self.part(net.z)
        net.send(own, here, self.sems.at[1, net.z], net.device(y=1 - net.y))
        net.send(own, here, self.sems.at[2 + net.y, net.z], net.device(c=1 - net.c))
        self.kept = net.local(own, here)

    def step(self, block):
        net = self.net
        here = self.at(net.place(block, net.y, net.c))
        net.recv(here, self.sems.at[0, block])
        net.send(here, here, self.sems.at[1, block], net.device(y=1 - net.y))
        net.send(here, here, self.sems.at[2 + net.y, block], net.device(c=1 - net.c))

    cross = Gather.cross
    finish = Gather.finish


class Rows:
    def __init__(self, net, own, full, sems):
        self.net, self.own, self.full = net, own, full
        self.sems = sems

    def start(self):
        net = self.net
        here = self.full.at[net.z, net.x]
        net.send(self.own, here, self.sems.at[0, net.z], net.device(z=net.z + 1), net.z < net.n - 1)
        net.send(self.own, here, self.sems.at[0, net.z], net.device(z=net.z - 1), net.z > 0)
        net.send(self.own, here, self.sems.at[1, net.z], net.device(x=1 - net.x))
        self.kept = net.local(self.own, here)

    def step(self, s):
        net = self.net
        for sign in (1, -1):
            block = net.z - s * sign
            valid = jnp.logical_and(block >= 0, block < net.n)
            nxt = net.z + sign
            more = jnp.logical_and(nxt >= 0, nxt < net.n)
            here = self.full.at[block, net.x]

            @pl.when(valid)
            def _():
                net.recv(here, self.sems.at[0, block])

            net.send(here, here, self.sems.at[0, block], net.device(z=nxt), jnp.logical_and(valid, more))
            net.send(here, here, self.sems.at[1, block], net.device(x=1 - net.x), valid)

    def finish(self):
        net = self.net
        for block in range(net.n):
            net.recv(self.full.at[block, 1 - net.x], self.sems.at[1, block])


class Reduce:
    def __init__(self, net, part, from_c, from_y, result, sems):
        self.net, self.part, self.from_c, self.from_y, self.result = net, part, from_c, from_y, result
        self.cs, self.ys, self.zs = sems

    def add(self, total, term):
        def body(r):
            span = pl.ds(r, 16)
            total[span] = (total[span].astype(F32) + term[span].astype(F32)).astype(BF16)

        loop(total.shape[0], 16, body)

    def start(self, i):
        net = self.net
        net.send(self.part.at[i, 1 - net.c], self.from_c.at[i], self.cs.at[i], net.device(c=1 - net.c))

    def step_c(self, i):
        net = self.net
        net.recv(self.from_c.at[i], self.cs.at[i])
        for y in (0, 1):
            self.add(self.part.at[i, net.c, y], self.from_c.at[i, y])
        net.send(self.part.at[i, net.c, 1 - net.y], self.from_y.at[i], self.ys.at[i], net.device(y=1 - net.y))

    def step_y(self, i, matrix, to):
        net = self.net
        net.recv(self.from_y.at[i], self.ys.at[i])
        self.add(self.part.at[i, net.c, net.y], self.from_y.at[i])
        src = self.part.at[i, net.c, net.y]
        dst = self.result.at[matrix, net.z]
        away = to != net.z
        net.send(src, dst, self.zs.at[matrix, net.z], net.device(z=to), away)
        net.local(src, dst, jnp.logical_not(away))

    def finish(self, matrix):
        net = self.net
        for d in range(1, net.n):
            block = (net.z + d) % net.n
            net.recv(self.result.at[matrix, block], self.zs.at[matrix, block])


def loop(total, step, body):
    @pl.loop(0, total // step)
    def _(i):
        body(pl.multiple_of(i * step, step))


def turn(field, cosine, sine, lane):
    half = HD // 2
    partner = jnp.where(lane % HD < half, pltpu.roll(field, LANES - half, 1), pltpu.roll(field, half, 1))
    return field * cosine + partner * sine


def head_masks():
    lane = lax.broadcasted_iota(jnp.int32, (1, LANES), 1)
    return (lane < HD).astype(BF16), (lane >= HD).astype(BF16)


def both(field, masks):
    return jnp.concatenate([field * masks[0], field * masks[1]], axis=0)


def pick(stacked, rows):
    lane = lax.broadcasted_iota(jnp.int32, (1, LANES), 1)
    return jnp.where(lane < HD, stacked[:rows], stacked[rows:])


def softmax(queries2, key_rows, allowed):
    scores = dot(queries2, key_rows, NT) * HD ** (-0.5)
    scores = jnp.where(allowed > 0, scores, -1e30)
    raised = jnp.exp(scores - jnp.max(scores, axis=-1, keepdims=True))
    return raised / jnp.sum(raised, axis=-1, keepdims=True)


def attention_kernel(
    dp,
    residual, cotangent, seg_col, seg_row, gains, freq, wa, wf,
    wa_out, wf_out, grad_out, normed_ffn_out, normed_out, attended_out, qkv_out, mixed_out, tables_out, gains_out,
    weights, pre, all_gains, allowed, grad_own, normed_all, ffn_own, partial, to_x, from_x,
    send_sems, local_sems, gain_sems, q_sems, o_sems, f_sems, g_sems, n_sems, x_sems,
):
    net = Net(dp, send_sems, local_sems)
    n = net.n
    rows, width = residual.shape
    block, cols = wa.shape[1:]
    group = 2 * rows
    part = wf.shape[2] // n
    me, x = net.dp_index, net.x
    net.greet([((me + k) % dp, x) for k in range(1, dp)] + [(me, 1 - x)])

    for k in range(1, dp):
        net.send(gains, all_gains.at[me], gain_sems.at[me], ((me + k) % dp, x))
    all_gains[me] = gains[...]

    def at_weights(first, count):
        return lambda index: weights.at[pl.ds(first, count), pl.ds(pl.multiple_of(index * block, block), block)]

    qkv = Gather(net, wa.at[pl.ds(0, 3)], at_weights(0, 3), q_sems)
    out = Gather(net, wa.at[pl.ds(3, 1)], at_weights(3, 1), o_sems)
    ffn = Exchange(
        net,
        lambda to: wf.at[:, :, pl.ds(pl.multiple_of(to * part, part), part)],
        lambda index: wf_out.at[:, pl.ds(pl.multiple_of(index * block, block), block)],
        f_sems,
    )
    grads = Rows(net, grad_own, grad_out, g_sems)
    ffn_rows = Rows(net, ffn_own, normed_ffn_out, n_sems)
    qkv.start()

    def mask_body(r):
        span = pl.ds(r, 16)
        live = (seg_col[x, span] >= 0).astype(F32)
        grad_own[span] = (cotangent[span].astype(F32) * live).astype(BF16)

    loop(rows, 16, mask_body)

    row_seg = jnp.concatenate([seg_col[0], seg_col[1]], axis=0)
    row_id = lax.broadcasted_iota(jnp.int32, (group, group), 0)
    col_id = lax.broadcasted_iota(jnp.int32, (group, group), 1)
    mask = jnp.logical_and(row_seg == seg_row[...], row_id >= col_id).astype(F32)
    allowed[...] = mask
    places = jnp.sum(mask, axis=1, keepdims=True) - 1.0
    lane = lax.broadcasted_iota(jnp.int32, (group, LANES), 1)
    angles = places * freq[...]
    tables_out[0] = jnp.cos(angles)
    tables_out[1] = jnp.where(lane % HD < HD // 2, -jnp.sin(angles), jnp.sin(angles))

    for k in range(1, dp):
        source = (me + k) % dp
        net.recv(all_gains.at[source], gain_sems.at[source])
    for i in range(dp):
        gains_out[:, i * block : (i + 1) * block] = all_gains[i]

    def norm_body(r):
        value = residual[pl.ds(r, 16)].astype(F32)
        unit = value * lax.rsqrt(jnp.mean(value * value, axis=-1, keepdims=True) + EPSILON)
        to = pl.multiple_of(x * rows + r, 16)
        normed_all[pl.ds(to, 16)] = (unit * gains_out[0:1]).astype(BF16)

    loop(rows, 16, norm_body)
    own_rows = normed_all.at[pl.ds(pl.multiple_of(x * rows, rows), rows)]
    other_rows = normed_all.at[pl.ds(pl.multiple_of((1 - x) * rows, rows), rows)]
    net.send(own_rows, own_rows, x_sems.at[0], net.device(x=1 - x))

    depth = width // n

    def project(b, first):
        qkv.finish(b)
        base = pl.multiple_of(b * depth, depth)

        def body(col):
            for m in range(3):
                term = dot(normed_all[:, pl.ds(base, depth)], weights[m, pl.ds(base, depth), pl.ds(col, 256)])
                to = pl.ds(pl.multiple_of(m * cols + col, 256), 256)
                pre[:, to] = term if first else pre[:, to] + term

        loop(cols, 256, body)

    qkv.step(1)
    qkv.cross(net.z)
    grads.start()
    for s in range(2, n):
        qkv.step(s)
        if s == 2:
            out.start()
            ffn.start()
        qkv.cross_step(s - 1)
    qkv.cross_step(n - 1)
    net.recv(other_rows, x_sems.at[0])
    net.settle(qkv.kept)
    for k in range(n):
        project((net.z + k) % n, k == 0)
    out.cross(net.z)
    for s in range(1, n):
        out.step(s)
        out.cross_step(s)
    masks = head_masks()

    def head_body(col):
        cosine, sine = tables_out[0], tables_out[1]
        queries = turn(pre[:, pl.ds(col, LANES)], cosine, sine, lane).astype(BF16)
        key_rows = turn(pre[:, pl.ds(pl.multiple_of(cols + col, LANES), LANES)], cosine, sine, lane).astype(BF16)
        value_rows = pre[:, pl.ds(pl.multiple_of(2 * cols + col, LANES), LANES)].astype(BF16)
        qkv_out[0, :, pl.ds(col, LANES)] = queries
        qkv_out[1, :, pl.ds(col, LANES)] = key_rows
        qkv_out[2, :, pl.ds(col, LANES)] = value_rows
        may = jnp.concatenate([allowed[...], allowed[...]], axis=0)
        probs = softmax(both(queries, masks), key_rows, may).astype(BF16)
        attended_out[:, pl.ds(col, LANES)] = pick(dot(probs, value_rows), group).astype(BF16)

    loop(cols, LANES, head_body)
    for k in range(1, n):
        ffn.step((net.z + k) % n)
    for k in range(n):
        out.finish((net.z + k) % n)
    net.settle(out.kept)
    kept_weights = net.local(weights, wa_out)

    def out_body(col):
        term = dot(attended_out[...], weights[3, pl.ds(col, 256), :], NT)
        partial[0, :, pl.ds(col, 256)] = term[:rows]
        partial[1, :, pl.ds(col, 256)] = term[rows:]

    loop(width, 256, out_body)

    def to_body(r):
        to_x[pl.ds(r, 16)] = partial[1 - x, pl.ds(r, 16)].astype(BF16)

    loop(rows, 16, to_body)
    net.send(to_x, from_x, x_sems.at[1], net.device(x=1 - x))
    for s in range(1, n):
        grads.step(s)
    net.recv(from_x, x_sems.at[1])

    def mix_body(r):
        span = pl.ds(r, 16)
        value = residual[span].astype(F32) + partial[x, span] + from_x[span].astype(F32)
        mixed_out[span] = value
        unit = value * lax.rsqrt(jnp.mean(value * value, axis=-1, keepdims=True) + EPSILON)
        ffn_own[span] = (unit * gains_out[8:9]).astype(BF16)

    loop(rows, 16, mix_body)
    ffn_rows.start()
    net.local(normed_all, normed_out)
    for s in range(1, n):
        ffn_rows.step(s)
    for k in range(n):
        ffn.cross((net.z + k) % n)
    for k in range(n):
        ffn.finish((net.z + k) % n)
    grads.finish()
    ffn_rows.finish()
    net.drain()


class RowSum:
    def __init__(self, net, part, from_x, from_z, sems):
        self.net, self.part, self.from_x, self.from_z = net, part, from_x, from_z
        self.xs, self.zs = sems

    def start(self, b):
        net = self.net
        net.send(self.part(b, 1 - net.x), self.from_x.at[b], self.xs.at[b], net.device(x=1 - net.x))

    def step(self, b, own):
        net = self.net
        net.recv(self.from_x.at[b], self.xs.at[b])
        total, term = self.part(b, net.x), self.from_x.at[b]

        def body(r):
            span = pl.ds(r, 16)
            total[span] = (total[span].astype(F32) + term[span].astype(F32)).astype(BF16)

        loop(total.shape[0], 16, body)
        if not own:
            net.send(total, self.from_z.at[net.z], self.zs.at[net.z], net.device(z=b))

    def finish(self):
        net = self.net
        for d in range(1, net.n):
            b = (net.z + d) % net.n
            net.recv(self.from_z.at[b], self.zs.at[b])

    def total(self, span):
        net = self.net
        value = self.part(net.z, net.x)[span].astype(F32)
        for d in range(1, net.n):
            value = value + self.from_z[(net.z + d) % net.n, span].astype(F32)
        return value


def norm_back(grad, value, gain):
    scale = lax.rsqrt(jnp.mean(value * value, axis=-1, keepdims=True) + EPSILON)
    unit = value * scale
    scaled = grad * gain
    back = scale * (scaled - unit * jnp.mean(scaled * unit, axis=-1, keepdims=True))
    return back, grad * unit


def weight_item(red, i, left, right, base, depth, block):
    def body(col):
        term = dot(left[:, pl.ds(base, depth)], right[:, pl.ds(col, 256)], TN).astype(BF16)
        for y in (0, 1):
            for c in (0, 1):
                at = (y * 2 + c) * block
                red.part[i, c, y, :, pl.ds(col, 256)] = term[at : at + block]

    loop(right.shape[1], 256, body)


def ffn_kernel(
    dp,
    mixed, gains, normed_hbm, grad_hbm, wf,
    result, block_out, mixed_grad, gain_part,
    weights, normed, grad, hidden, gate_up_grad, back, back_x, back_z, add_x, add_z, part, from_c, from_y,
    send_sems, local_sems, bx_sems, bz_sems, ax_sems, az_sems, rc_sems, ry_sems, rz_sems,
):
    net = Net(dp, send_sems, local_sems)
    n = net.n
    rows, width = mixed.shape
    cols = wf.shape[2]
    block = width // dp
    depth = width // n
    pair = 2 * rows
    loads = [net.local(normed_hbm, normed), net.local(wf, weights), net.local(grad_hbm, grad)]
    net.greet(
        [net.device(z=(net.z + d) % n) for d in range(1, n)]
        + [net.device(y=1 - net.y), net.device(c=1 - net.c), net.device(x=1 - net.x)]
    )
    gate_grad, up_grad = gate_up_grad.at[:, pl.ds(0, cols)], gate_up_grad.at[:, pl.ds(cols, cols)]
    add = gate_up_grad
    backs = RowSum(net, lambda b, half: back.at[b, half], back_x, back_z, (bx_sems, bz_sems))
    adds = RowSum(
        net, lambda b, half: add.at[pl.ds(pl.multiple_of((b * 2 + half) * rows, rows), rows)], add_x, add_z, (ax_sems, az_sems)
    )
    red = Reduce(net, part, from_c, from_y, result, (rc_sems, ry_sems, rz_sems))
    for load in loads:
        net.settle(load)

    order = sorted(range(n), key=lambda d: -min(d, n - d))

    def chunk(b):
        here = pl.ds(pl.multiple_of(b * pair, pair), pair)

        def hidden_body(col):
            span = pl.ds(col, 256)
            gate = dot(normed[here], weights[0, :, span])
            up = dot(normed[here], weights[1, :, span])
            hidden_grad = dot(grad[here], weights[2, :, span])
            sigmoid = 1.0 / (1.0 + jnp.exp(-gate))
            active = gate * sigmoid
            hidden[here, span] = (active * up).astype(BF16)
            gate_grad[here, span] = (hidden_grad * up * sigmoid * (1.0 + gate * (1.0 - sigmoid))).astype(BF16)
            up_grad[here, span] = (hidden_grad * active).astype(BF16)

        loop(cols, 256, hidden_body)

        def back_body(col):
            span = pl.ds(col, 256)
            term = dot(gate_grad[here], weights[0, span, :], NT) + dot(up_grad[here], weights[1, span, :], NT)
            term = term.astype(BF16)
            back[b, 0, :, span] = term[:rows]
            back[b, 1, :, span] = term[rows:]

        loop(width, 256, back_body)
        backs.start(b)

    def add_chunk(b):
        here = pl.ds(pl.multiple_of(b * pair, pair), pair)

        def body(col):
            span = pl.ds(col, 256)
            term = dot(hidden[here], weights[2, span, :], NT).astype(BF16)
            add[here, span] = term

        loop(width, 256, body)
        adds.start(b)

    for k, d in enumerate(order):
        chunk((net.z + d) % n)
        if k > 0:
            backs.step((net.z + order[k - 1]) % n, order[k - 1] == 0)
    items = []
    for d in order:
        b = (net.z + d) % n
        for m in (2, 0, 1):
            i = len(items)
            left, right = ((normed, gate_grad), (normed, up_grad), (grad, hidden))[m]
            weight_item(red, i, left, right, pl.multiple_of(b * depth, depth), depth, block)
            red.start(i)
            if i > 0:
                red.step_c(i - 1)
            if i == 1:
                backs.step((net.z + order[-1]) % n, order[-1] == 0)
            items.append((m, b))
    red.step_c(len(items) - 1)
    for k, d in enumerate(order):
        add_chunk((net.z + d) % n)
        if k > 0:
            adds.step((net.z + order[k - 1]) % n, order[k - 1] == 0)
    backs.finish()
    gain_part[...] = jnp.zeros_like(gain_part)

    def mixed_body(r):
        span = pl.ds(r, 16)
        own = pl.ds(pl.multiple_of((net.z * 2 + net.x) * rows + r, 16), 16)
        term, gain_term = norm_back(backs.total(span), mixed[span], gains[8:9])
        mixed_grad[span] = grad[own].astype(F32) + term
        gain_part[...] += gain_term[:8] + gain_term[8:]

    loop(rows, 16, mixed_body)
    adds.step((net.z + order[-1]) % n, order[-1] == 0)
    for i, (m, b) in enumerate(items):
        red.step_y(i, m, b)
    adds.finish()

    def block_body(r):
        span = pl.ds(r, 16)
        block_out[span] = (mixed[span] + adds.total(span)).astype(BF16)

    loop(rows, 16, block_body)
    for m in range(3):
        red.finish(m)
    net.drain()


def back_kernel(
    dp,
    residual, seg_col, seg_row, gains, tables, normed, attended, qkv, mixed_grad, ffn_part, wa,
    result, input_grad, gain_out,
    weights, allowed, mixed_all, attended_grad, qkv_grad, partial, to_x, from_x, gain_to, gain_from, gain_sum, gain_x,
    part, from_c, from_y,
    send_sems, local_sems, x_sems, gain_sems, rc_sems, ry_sems, rz_sems,
):
    net = Net(dp, send_sems, local_sems)
    n = net.n
    me, x = net.dp_index, net.x
    rows, width = residual.shape
    group = 2 * rows
    cols = wa.shape[2]
    block = width // dp
    depth = width // n
    load_out = net.local(wa.at[3], weights.at[3])
    load_qkv = net.local(wa.at[pl.ds(0, 3)], weights.at[pl.ds(0, 3)])
    net.greet([((me + k) % dp, x) for k in range(1, dp)] + [(me, 1 - x)])
    red = Reduce(net, part, from_c, from_y, result, (rc_sems, ry_sems, rz_sems))

    def low_body(r):
        to = pl.multiple_of(x * rows + r, 16)
        mixed_all[pl.ds(to, 16)] = mixed_grad[pl.ds(r, 16)].astype(BF16)

    loop(rows, 16, low_body)
    own_rows = mixed_all.at[pl.ds(pl.multiple_of(x * rows, rows), rows)]
    other_rows = mixed_all.at[pl.ds(pl.multiple_of((1 - x) * rows, rows), rows)]
    net.send(own_rows, own_rows, x_sems.at[0], net.device(x=1 - x))
    row_seg = jnp.concatenate([seg_col[0], seg_col[1]], axis=0)
    row_id = lax.broadcasted_iota(jnp.int32, (group, group), 0)
    col_id = lax.broadcasted_iota(jnp.int32, (group, group), 1)
    allowed[...] = jnp.logical_and(row_seg == seg_row[...], row_id >= col_id).astype(F32)
    net.settle(load_out)
    net.recv(other_rows, x_sems.at[0])

    def attended_body(col):
        span = pl.ds(col, 256)
        attended_grad[:, span] = dot(mixed_all[...], weights[3, :, span]).astype(BF16)

    loop(cols, 256, attended_body)
    order = sorted(range(n), key=lambda d: -min(d, n - d))
    items = []

    def emit(m, left, right):
        for d in order:
            b = (net.z + d) % n
            i = len(items)
            weight_item(red, i, left, right, pl.multiple_of(b * depth, depth), depth, block)
            red.start(i)
            if i > 0:
                red.step_c(i - 1)
            items.append((m, b))

    emit(3, mixed_all, attended)
    masks = head_masks()
    lane = lax.broadcasted_iota(jnp.int32, (group, LANES), 1)

    def head_body(col):
        span = pl.ds(col, LANES)
        cosine, sine = tables[0], tables[1]
        queries, key_rows, value_rows = qkv[0, :, span], qkv[1, :, span], qkv[2, :, span]
        out_grad = attended_grad[:, span]
        queries2, out_grad2 = both(queries, masks), both(out_grad, masks)
        may = jnp.concatenate([allowed[...], allowed[...]], axis=0)
        probs = softmax(queries2, key_rows, may)
        value_grad = dot(probs.astype(BF16), out_grad2, TN)
        prob_grad = dot(out_grad2, value_rows, NT)
        score_grad = probs * (prob_grad - jnp.sum(probs * prob_grad, axis=-1, keepdims=True))
        score_grad = score_grad.astype(BF16)
        query_grad = pick(dot(score_grad, key_rows), group) * HD ** (-0.5)
        key_grad = dot(score_grad, queries2, TN) * HD ** (-0.5)
        qkv_grad[0, :, span] = turn(query_grad, cosine, -sine, lane).astype(BF16)
        qkv_grad[1, :, span] = turn(key_grad, cosine, -sine, lane).astype(BF16)
        qkv_grad[2, :, span] = value_grad.astype(BF16)

    loop(cols, LANES, head_body)
    net.settle(load_qkv)

    def normed_body(col):
        span = pl.ds(col, 256)
        term = dot(qkv_grad[0], weights[0, span, :], NT)
        term += dot(qkv_grad[1], weights[1, span, :], NT)
        term += dot(qkv_grad[2], weights[2, span, :], NT)
        partial[0, :, span] = term[:rows]
        partial[1, :, span] = term[rows:]

    def to_body(r):
        to_x[pl.ds(r, 16)] = partial[1 - x, pl.ds(r, 16)].astype(BF16)

    for m in range(3):
        emit(m, normed, qkv_grad.at[m])
    red.step_c(len(items) - 1)
    loop(width, 256, normed_body)
    loop(rows, 16, to_body)
    net.send(to_x, from_x, x_sems.at[1], net.device(x=1 - x))
    half = len(items) // 2
    for i in range(half):
        red.step_y(i, *items[i])
    net.recv(from_x, x_sems.at[1])
    gain_sum[...] = jnp.zeros_like(gain_sum)

    def input_body(r):
        span = pl.ds(r, 16)
        grad = partial[x, span] + from_x[span].astype(F32)
        term, gain_term = norm_back(grad, residual[span].astype(F32), gains[0:1])
        input_grad[span] = mixed_grad[span] + term
        gain_sum[...] += gain_term[:8] + gain_term[8:]

    loop(rows, 16, input_body)
    for i in range(dp):
        gain_to[i, 0:8] = gain_sum[:, i * block : (i + 1) * block]
        gain_to[i, 8:16] = ffn_part[:, i * block : (i + 1) * block]
    for k in range(1, dp):
        to = (me + k) % dp
        net.send(gain_to.at[to], gain_from.at[me], gain_sems.at[me], (to, x))
    for i in range(half, len(items)):
        red.step_y(i, *items[i])
    total = gain_to[me]
    for k in range(1, dp):
        source = (me + k) % dp
        net.recv(gain_from.at[source], gain_sems.at[source])
        total = total + gain_from[source]
    gain_x[0] = total
    net.send(gain_x.at[0], gain_x.at[1], x_sems.at[2], net.device(x=1 - x))
    for m in range(4):
        red.finish(m)
    net.recv(gain_x.at[1], x_sems.at[2])
    gain_out[...] = gain_x[0] + gain_x[1]
    net.drain()


def call(kernel, collective_id, sends, locals_, vmem, outs, out_specs, scratch, sems):
    def typed(entry):
        return (entry[:-1], F32) if entry[-1] is F32 else (entry, BF16)

    dma = pltpu.SemaphoreType.DMA
    return lambda in_specs, *args: pl.pallas_call(
        kernel,
        out_shape=[jax.ShapeDtypeStruct(*typed(entry)) for entry in outs],
        in_specs=in_specs,
        out_specs=out_specs,
        scratch_shapes=[pltpu.VMEM(*typed(entry)) for entry in scratch] + [dma((sends,)), dma((locals_,))] + [dma(entry) for entry in sems],
        compiler_params=pltpu.CompilerParams(collective_id=collective_id, has_side_effects=True, vmem_limit_bytes=vmem),
    )(*args)


def shards(dp, residual, seg_ids, attn_gain, w_qkv, w_out, ffn_gain, w_gate_up, w_down, cotangent):
    n = dp // 4
    rows, width = residual.shape
    group = seg_ids.shape[0]
    block, cols = w_qkv.shape[1:]
    part = w_gate_up.shape[2] // n
    wa = jnp.concatenate([w_qkv, w_out.T[None]], axis=0)
    wf = jnp.concatenate([w_gate_up, w_down.T[None]], axis=0)
    seg_col = seg_ids.reshape(2, rows, 1)
    seg_row = seg_ids.reshape(1, group)
    gains = jnp.concatenate(
        [jnp.broadcast_to(gain.astype(F32)[None], (8, block)) for gain in (attn_gain, ffn_gain)], axis=0
    )
    pairs = jnp.arange(LANES, dtype=jnp.int32) % (HD // 2)
    freq = (ROPE_BASE ** (-(pairs.astype(F32) * 2.0 / HD)))[None]
    mib = 1024 * 1024

    first = call(
        functools.partial(attention_kernel, dp), 1, 192, 8, 60 * mib,
        [
            (4, width, cols), (3, width, part), (n, 2, rows, width), (n, 2, rows, width), (group, width),
            (group, cols), (3, group, cols), (rows, width, F32), (2, group, LANES, F32), (16, width, F32),
        ],
        [ANY] * 5 + [VM] * 5,
        [
            (4, width, cols), (group, 3 * cols, F32), (dp, 16, block, F32), (group, group, F32),
            (rows, width), (group, width), (rows, width), (2, rows, width, F32), (rows, width), (rows, width),
        ],
        [(dp,), (4, n), (4, n), (4, n), (2, n), (2, n), (2,)],
    )
    (weights, ffn_weights, grad_all, normed_ffn, normed, attended, qkv, mixed, tables, all_gains) = first(
        [VM] * 6 + [ANY] * 2, residual, cotangent, seg_col, seg_row, gains, freq, wa, wf
    )
    every = n * 2 * rows
    items = 3 * n
    second = call(
        functools.partial(ffn_kernel, dp), 2, 128, 24, 63 * mib,
        [(3, n, block, part), (rows, width), (rows, width, F32), (8, width, F32)],
        [ANY] + [VM] * 3,
        [
            (3, width, part), (every, width), (every, width), (every, part), (every, 2 * part),
            (n, 2, rows, width), (n, rows, width), (n, rows, width), (n, rows, width), (n, rows, width),
            (items, 2, 2, block, part), (items, 2, block, part), (items, block, part),
        ],
        [(n,), (n,), (n,), (n,), (items,), (items,), (3, n)],
    )
    ffn_result, block_out, mixed_grad, ffn_part = second(
        [VM] * 2 + [ANY] * 3, mixed, all_gains, normed_ffn.reshape(every, width), grad_all.reshape(every, width), ffn_weights
    )
    items = 4 * n
    third = call(
        functools.partial(back_kernel, dp), 3, 128, 24, 63 * mib,
        [(4, n, block, cols), (rows, width, F32), (16, block, F32)],
        [ANY, VM, VM],
        [
            (4, width, cols), (group, group, F32), (group, width), (group, cols), (3, group, cols),
            (2, rows, width, F32), (rows, width), (rows, width),
            (dp, 16, block, F32), (dp, 16, block, F32), (8, width, F32), (2, 16, block, F32),
            (items, 2, 2, block, cols), (items, 2, block, cols), (items, block, cols),
        ],
        [(3,), (dp,), (items,), (items,), (4, n)],
    )
    result, input_grad, gain_grads = third(
        [VM] * 10 + [ANY], residual, seg_col, seg_row, all_gains, tables, normed, attended, qkv, mixed_grad, ffn_part, weights
    )
    gain_grads = jnp.sum(gain_grads.reshape(2, 8, block), axis=1)
    total = jnp.sum(result.astype(F32), axis=1)
    gate_up_grad = ffn_result[:2].astype(F32).transpose(0, 2, 1, 3).reshape(2, block, n * part)
    down_grad = ffn_result[2].astype(F32).transpose(0, 2, 1).reshape(n * part, block)
    return (
        block_out, input_grad, gain_grads[0], total[:3], total[3].T, gain_grads[1], gate_up_grad, down_grad,
    )


def positions(segments):
    row_index = jnp.arange(segments.shape[1], dtype=jnp.int32)[None, :]
    previous = jnp.concatenate([segments[:, :1] - 1, segments[:, :-1]], axis=1)
    run_start = lax.cummax(jnp.where(segments != previous, row_index, 0), axis=1)
    return row_index - run_start


def rope_tables(places, head_dim):
    half_dim = head_dim // 2
    frequency = ROPE_BASE ** (-(jnp.arange(half_dim, dtype=jnp.float32) * 2.0 / head_dim))
    angles = places.astype(jnp.float32)[:, None, None] * frequency[None, None, :]
    return (jnp.cos(angles), jnp.sin(angles))


def rotate(field, cosine, sine_table):
    half_dim = field.shape[-1] // 2
    lower_half = field[..., :half_dim]
    upper_half = field[..., half_dim:]
    return jnp.concatenate(
        [
            lower_half * cosine - upper_half * sine_table,
            upper_half * cosine + lower_half * sine_table,
        ],
        axis=-1,
    )


def unrotate(field, cosine, sine_table):
    half_dim = field.shape[-1] // 2
    lower_half = field[..., :half_dim]
    upper_half = field[..., half_dim:]
    return jnp.concatenate(
        [
            lower_half * cosine + upper_half * sine_table,
            upper_half * cosine - lower_half * sine_table,
        ],
        axis=-1,
    )


def attention_scores(queries, key_rows, allowed):
    scores = jnp.einsum(
        "qhd,khd->hqk", queries, key_rows, preferred_element_type=jnp.float32
    ) * queries.shape[-1] ** (-0.5)
    return jnp.where(allowed[None], scores, -1e30)


def plain_shards(residual_in, seg_ids, attn_gain, w_qkv, w_out, ffn_gain, w_gate_up, w_down, cotangent):
    rows_local = residual_in.shape[0]
    group_rows = seg_ids.shape[0]
    offset = lax.axis_index("tensor") * rows_local
    live_rows = (lax.dynamic_slice_in_dim(seg_ids, offset, rows_local) >= 0).astype(jnp.float32)
    residual = residual_in.astype(jnp.float32)
    contract_rows = (((0,), (0,)), ((), ()))
    contract_cols = (((1,), (1,)), ((), ()))
    gain_attn, qkv_full, out_full = (
        lax.all_gather(attn_gain, "dp", axis=0, tiled=True),
        lax.all_gather(w_qkv, "dp", axis=1, tiled=True),
        lax.all_gather(w_out, "dp", axis=1, tiled=True),
    )
    norm_attn = lax.rsqrt(jnp.mean(residual * residual, axis=-1, keepdims=True) + EPSILON)
    unit_attn = residual * norm_attn
    normed = (unit_attn * gain_attn.astype(jnp.float32)).astype(jnp.bfloat16)
    normed_all = lax.all_gather(normed, "tensor", axis=0, tiled=True)
    projected = jnp.einsum("rd,cde->cre", normed_all, qkv_full, preferred_element_type=jnp.float32)
    head_count = qkv_full.shape[2] // HD
    head_shape = (group_rows, head_count, HD)
    cosine, sine_table = rope_tables(positions(seg_ids[None, :])[0], HD)
    queries = rotate(projected[0].reshape(head_shape), cosine, sine_table).astype(jnp.bfloat16)
    key_rows = rotate(projected[1].reshape(head_shape), cosine, sine_table).astype(jnp.bfloat16)
    value_rows = projected[2].reshape(head_shape).astype(jnp.bfloat16)
    row_index = jnp.arange(group_rows)
    allowed = (seg_ids[:, None] == seg_ids[None, :]) & (row_index[:, None] >= row_index[None, :])
    scores = attention_scores(queries, key_rows, allowed)
    row_top = jnp.max(scores, axis=-1, keepdims=True)
    log_total = row_top + jnp.log(jnp.sum(jnp.exp(scores - row_top), axis=-1, keepdims=True))
    weights = jnp.exp(scores - log_total).astype(jnp.bfloat16)
    attended = jnp.einsum("hqk,khd->qhd", weights, value_rows, preferred_element_type=jnp.float32)
    attended = attended.reshape(group_rows, head_count * HD).astype(jnp.bfloat16)
    mixed = residual + lax.psum_scatter(
        jnp.dot(attended, out_full, preferred_element_type=jnp.float32),
        "tensor",
        scatter_dimension=0,
        tiled=True,
    )
    gain_ffn, gate_up_full, down_full = (
        lax.all_gather(ffn_gain, "dp", axis=0, tiled=True),
        lax.all_gather(w_gate_up, "dp", axis=1, tiled=True),
        lax.all_gather(w_down, "dp", axis=1, tiled=True),
    )
    norm_ffn = lax.rsqrt(jnp.mean(mixed * mixed, axis=-1, keepdims=True) + EPSILON)
    unit_ffn = mixed * norm_ffn
    normed_ffn = (unit_ffn * gain_ffn.astype(jnp.float32)).astype(jnp.bfloat16)
    normed_ffn_all = lax.all_gather(normed_ffn, "tensor", axis=0, tiled=True)
    gate_up = jnp.einsum(
        "rd,cde->cre", normed_ffn_all, gate_up_full, preferred_element_type=jnp.float32
    )
    gate_pre = gate_up[0]
    up_pre = gate_up[1]
    sigmoid_gate = jax.nn.sigmoid(gate_pre)
    activated = gate_pre * sigmoid_gate
    hidden = (activated * up_pre).astype(jnp.bfloat16)
    output = mixed + lax.psum_scatter(
        jnp.dot(hidden, down_full, preferred_element_type=jnp.float32).astype(jnp.bfloat16),
        "tensor",
        scatter_dimension=0,
        tiled=True,
    ).astype(jnp.float32)
    grad_out = cotangent.astype(jnp.float32) * live_rows[:, None]
    grad_all = lax.all_gather(grad_out.astype(jnp.bfloat16), "tensor", axis=0, tiled=True)
    down_grad = lax.dot_general(hidden, grad_all, contract_rows, preferred_element_type=jnp.float32)
    hidden_grad = lax.dot_general(
        grad_all, down_full, contract_cols, preferred_element_type=jnp.float32
    )
    gate_grads = jnp.stack(
        [
            hidden_grad * up_pre * sigmoid_gate * (1.0 + gate_pre * (1.0 - sigmoid_gate)),
            hidden_grad * activated,
        ]
    ).astype(jnp.bfloat16)
    gate_up_grad = jnp.einsum(
        "rd,cre->cde", normed_ffn_all, gate_grads, preferred_element_type=jnp.float32
    )
    normed_ffn_grad = lax.psum_scatter(
        jnp.einsum("cre,cde->rd", gate_grads, gate_up_full, preferred_element_type=jnp.float32),
        "tensor",
        scatter_dimension=0,
        tiled=True,
    )
    ffn_gain_part = jnp.sum(normed_ffn_grad * unit_ffn, axis=0)
    scaled_ffn = normed_ffn_grad * gain_ffn.astype(jnp.float32)
    mixed_grad = grad_out + norm_ffn * (
        scaled_ffn - unit_ffn * jnp.mean(scaled_ffn * unit_ffn, axis=-1, keepdims=True)
    )
    mixed_all = lax.all_gather(mixed_grad.astype(jnp.bfloat16), "tensor", axis=0, tiled=True)
    out_grad = lax.dot_general(
        attended, mixed_all, contract_rows, preferred_element_type=jnp.float32
    )
    attended_grad = lax.dot_general(
        mixed_all, out_full, contract_cols, preferred_element_type=jnp.float32
    )
    attended_grad = attended_grad.astype(jnp.bfloat16).reshape(head_shape)
    probabilities = jnp.exp(attention_scores(queries, key_rows, allowed) - log_total)
    value_grad = jnp.einsum(
        "hqk,qhd->khd",
        probabilities.astype(jnp.bfloat16),
        attended_grad,
        preferred_element_type=jnp.float32,
    )
    prob_grad = jnp.einsum(
        "qhd,khd->hqk", attended_grad, value_rows, preferred_element_type=jnp.float32
    )
    score_grad = (
        probabilities * (prob_grad - jnp.sum(probabilities * prob_grad, axis=-1, keepdims=True))
    ).astype(jnp.bfloat16)
    scale_factor = HD ** (-0.5)
    query_grad = (
        jnp.einsum("hqk,khd->qhd", score_grad, key_rows, preferred_element_type=jnp.float32)
        * scale_factor
    )
    key_grad = (
        jnp.einsum("hqk,qhd->khd", score_grad, queries, preferred_element_type=jnp.float32)
        * scale_factor
    )
    qkv_grads = jnp.stack(
        [
            unrotate(query_grad, cosine, sine_table),
            unrotate(key_grad, cosine, sine_table),
            value_grad,
        ]
    )
    qkv_grads = qkv_grads.reshape(3, group_rows, head_count * HD).astype(jnp.bfloat16)
    qkv_grad = jnp.einsum("rd,cre->cde", normed_all, qkv_grads, preferred_element_type=jnp.float32)
    normed_grad = lax.psum_scatter(
        jnp.einsum("cre,cde->rd", qkv_grads, qkv_full, preferred_element_type=jnp.float32),
        "tensor",
        scatter_dimension=0,
        tiled=True,
    )
    attn_gain_part = jnp.sum(normed_grad * unit_attn, axis=0)
    scaled_attn = normed_grad * gain_attn.astype(jnp.float32)
    input_grad = mixed_grad + norm_attn * (
        scaled_attn - unit_attn * jnp.mean(scaled_attn * unit_attn, axis=-1, keepdims=True)
    )
    (
        query_total,
        key_total,
        value_total,
        out_total,
        attn_gain_total,
        gate_total,
        up_total,
        down_total,
        ffn_gain_total,
    ) = (
        lax.psum_scatter(qkv_grad[0], "dp", scatter_dimension=0, tiled=True),
        lax.psum_scatter(qkv_grad[1], "dp", scatter_dimension=0, tiled=True),
        lax.psum_scatter(qkv_grad[2], "dp", scatter_dimension=0, tiled=True),
        lax.psum_scatter(out_grad, "dp", scatter_dimension=1, tiled=True),
        lax.psum_scatter(attn_gain_part, "dp", scatter_dimension=0, tiled=True),
        lax.psum_scatter(gate_up_grad[0], "dp", scatter_dimension=0, tiled=True),
        lax.psum_scatter(gate_up_grad[1], "dp", scatter_dimension=0, tiled=True),
        lax.psum_scatter(down_grad, "dp", scatter_dimension=1, tiled=True),
        lax.psum_scatter(ffn_gain_part, "dp", scatter_dimension=0, tiled=True),
    )
    gate_up_total = jnp.stack([gate_total, up_total])
    qkv_total = jnp.stack([query_total, key_total, value_total])
    attn_gain_sum, ffn_gain_sum = lax.psum((attn_gain_total, ffn_gain_total), "tensor")
    return (
        output.astype(jnp.bfloat16),
        input_grad,
        attn_gain_sum,
        qkv_total,
        out_total,
        ffn_gain_sum,
        gate_up_total,
        down_total,
    )


def solution(mesh):
    in_specs = (
        P(("dp", "tensor"), None),
        P("dp"),
        P("dp"),
        P(None, "dp", "tensor"),
        P("tensor", "dp"),
        P("dp"),
        P(None, "dp", "tensor"),
        P("tensor", "dp"),
        P(("dp", "tensor"), None),
    )
    out_specs = (
        P(("dp", "tensor"), None),
        P(("dp", "tensor"), None),
        P("dp"),
        P(None, "dp", "tensor"),
        P("tensor", "dp"),
        P("dp"),
        P(None, "dp", "tensor"),
        P("tensor", "dp"),
    )
    dp = mesh.shape["dp"]
    local = functools.partial(shards, dp) if dp == 16 else plain_shards
    return jax.shard_map(local, mesh=mesh, in_specs=in_specs, out_specs=out_specs, check_vma=False)
```

```python
import functools

import jax
import jax.numpy as jnp
from jax import lax
from jax.experimental import pallas as pl
from jax.experimental.pallas import tpu as pltpu
from jax.sharding import PartitionSpec as P

HD = 64
EPSILON = 1e-05
ROPE_BASE = 130000.0
MESH = pl.DeviceIdType.MESH
ANY = pl.BlockSpec(memory_space=pl.ANY)
VM = pl.BlockSpec(memory_space=pltpu.VMEM)
F32 = jnp.float32
BF16 = jnp.bfloat16
LANES = 128
NT = (((1,), (1,)), ((), ()))
TN = (((0,), (0,)), ((), ()))
NN = (((1,), (0,)), ((), ()))


def dot(a, b, dims=NN):
    return lax.dot_general(a, b, dims, preferred_element_type=F32)


def when(cond, action):
    if cond is None:
        action()
    else:
        pl.when(cond)(action)


class Net:
    def __init__(self, dp, send_sems, local_sems):
        self.n = dp // 4
        self.dp_index = lax.axis_index("dp")
        self.x = lax.axis_index("tensor")
        self.z = self.dp_index // 4
        self.y = (self.dp_index // 2) % 2
        self.c = self.dp_index % 2
        self.send_sems = send_sems
        self.local_sems = local_sems
        self.sent = 0
        self.moved = 0
        self.pending = []
        self.kept = []

    def place(self, z, y, c):
        return (z * 2 + y) * 2 + c

    def device(self, z=None, y=None, c=None, x=None):
        z = self.z if z is None else z
        y = self.y if y is None else y
        c = self.c if c is None else c
        x = self.x if x is None else x
        return (self.place(z, y, c), x)

    def greet(self, devices):
        barrier = pltpu.get_barrier_semaphore()
        for device in devices:
            pl.semaphore_signal(barrier, inc=1, device_id=device, device_id_type=MESH)
        pl.semaphore_wait(barrier, len(devices))

    def send(self, src, dst, recv_sem, device, cond=None):
        sem = self.send_sems.at[self.sent]
        self.sent += 1
        copy = pltpu.make_async_remote_copy(
            src_ref=src, dst_ref=dst, send_sem=sem, recv_sem=recv_sem, device_id=device, device_id_type=MESH
        )
        when(cond, copy.start)
        self.pending.append((cond, copy))
        return self.pending[-1]

    def recv(self, dst, recv_sem):
        pltpu.make_async_remote_copy(
            src_ref=dst, dst_ref=dst, send_sem=self.send_sems.at[0], recv_sem=recv_sem,
            device_id=self.device(c=1 - self.c), device_id_type=MESH,
        ).wait_recv()

    def local(self, src, dst, cond=None):
        sem = self.local_sems.at[self.moved]
        self.moved += 1
        copy = pltpu.make_async_copy(src, dst, sem)
        when(cond, copy.start)
        self.kept.append((cond, copy))
        return self.kept[-1]

    def settle(self, entry):
        for entries, wait in ((self.kept, "wait"), (self.pending, "wait_send")):
            for k, known in enumerate(entries):
                if known is entry:
                    when(entry[0], getattr(entry[1], wait))
                    del entries[k]
                    return

    def drain(self):
        assert self.sent <= self.send_sems.shape[0] and self.moved <= self.local_sems.shape[0]
        for cond, copy in self.pending:
            when(cond, copy.wait_send)
        for cond, copy in self.kept:
            when(cond, copy.wait)


class Gather:
    def __init__(self, net, own, at, sems):
        self.net, self.own, self.at = net, own, at
        self.sems = sems

    def spread(self, block, src, ysend=True):
        net = self.net
        here = net.place(block, net.y, net.c)
        net.send(src, self.at(here), self.sems.at[1, block], net.device(y=1 - net.y))
        net.send(src, self.at(here), self.sems.at[2 + net.y, block], net.device(c=1 - net.c))

    def start(self):
        net = self.net
        here = self.at(net.dp_index)
        net.send(self.own, here, self.sems.at[0, net.z], net.device(z=net.z + 1), net.z < net.n - 1)
        net.send(self.own, here, self.sems.at[0, net.z], net.device(z=net.z - 1), net.z > 0)
        self.spread(net.z, self.own)
        self.kept = net.local(self.own, here)

    def step(self, s):
        net = self.net
        for sign in (1, -1):
            block = net.z - s * sign
            valid = jnp.logical_and(block >= 0, block < net.n)
            nxt = net.z + sign
            more = jnp.logical_and(nxt >= 0, nxt < net.n)
            here = self.at(net.place(block, net.y, net.c))

            @pl.when(valid)
            def _():
                net.recv(here, self.sems.at[0, block])

            net.send(here, here, self.sems.at[0, block], net.device(z=nxt), jnp.logical_and(valid, more))
            net.send(here, here, self.sems.at[1, block], net.device(y=1 - net.y), valid)
            net.send(here, here, self.sems.at[2 + net.y, block], net.device(c=1 - net.c), valid)

    def cross(self, block):
        net = self.net
        there = self.at(net.place(block, 1 - net.y, net.c))
        net.recv(there, self.sems.at[1, block])
        net.send(there, there, self.sems.at[3 - net.y, block], net.device(c=1 - net.c))

    def cross_step(self, s):
        net = self.net
        for sign in (1, -1):
            block = net.z - s * sign
            valid = jnp.logical_and(block >= 0, block < net.n)
            there = self.at(net.place(block, 1 - net.y, net.c))

            @pl.when(valid)
            def _():
                net.recv(there, self.sems.at[1, block])

            net.send(there, there, self.sems.at[3 - net.y, block], net.device(c=1 - net.c), valid)

    def finish(self, block):
        net = self.net
        for y in (0, 1):
            net.recv(self.at(net.place(block, y, 1 - net.c)), self.sems.at[2 + y, block])


class Exchange:
    def __init__(self, net, part, at, sems):
        self.net, self.part, self.at = net, part, at
        self.sems = sems

    def start(self):
        net = self.net
        here = self.at(net.dp_index)
        for d in list(range(1, net.n)):
            to = (net.z + d) % net.n
            net.send(self.part(to), here, self.sems.at[0, net.z], net.device(z=to))
        own = self.part(net.z)
        net.send(own, here, self.sems.at[1, net.z], net.device(y=1 - net.y))
        net.send(own, here, self.sems.at[2 + net.y, net.z], net.device(c=1 - net.c))
        self.kept = net.local(own, here)

    def step(self, block):
        net = self.net
        here = self.at(net.place(block, net.y, net.c))
        net.recv(here, self.sems.at[0, block])
        net.send(here, here, self.sems.at[1, block], net.device(y=1 - net.y))
        net.send(here, here, self.sems.at[2 + net.y, block], net.device(c=1 - net.c))

    cross = Gather.cross
    finish = Gather.finish


class Rows:
    def __init__(self, net, own, full, sems):
        self.net, self.own, self.full = net, own, full
        self.sems = sems

    def start(self):
        net = self.net
        here = self.full.at[net.z, net.x]
        net.send(self.own, here, self.sems.at[0, net.z], net.device(z=net.z + 1), net.z < net.n - 1)
        net.send(self.own, here, self.sems.at[0, net.z], net.device(z=net.z - 1), net.z > 0)
        net.send(self.own, here, self.sems.at[1, net.z], net.device(x=1 - net.x))
        self.kept = net.local(self.own, here)

    def step(self, s):
        net = self.net
        for sign in (1, -1):
            block = net.z - s * sign
            valid = jnp.logical_and(block >= 0, block < net.n)
            nxt = net.z + sign
            more = jnp.logical_and(nxt >= 0, nxt < net.n)
            here = self.full.at[block, net.x]

            @pl.when(valid)
            def _():
                net.recv(here, self.sems.at[0, block])

            net.send(here, here, self.sems.at[0, block], net.device(z=nxt), jnp.logical_and(valid, more))
            net.send(here, here, self.sems.at[1, block], net.device(x=1 - net.x), valid)

    def finish(self):
        net = self.net
        for block in range(net.n):
            net.recv(self.full.at[block, 1 - net.x], self.sems.at[1, block])


class Reduce:
    def __init__(self, net, part, from_c, from_y, result, line, sems, total):
        self.net, self.part, self.from_c, self.from_y = net, part, from_c, from_y
        self.result, self.totals = result
        self.line = line
        self.cs, self.ys, self.zs, self.ls, self.free = sems
        self.slots = part.shape[0]
        self.total = total
        self.items = []
        self.out = {}
        self.done_c = self.done_y = self.done_z = 0

    def add(self, total, term):
        def body(r):
            span = pl.ds(r, 16)
            total[span] = (total[span].astype(F32) + term[span].astype(F32)).astype(BF16)

        loop(total.shape[0], 16, body)

    def credit(self, which, device):
        pl.semaphore_signal(self.free.at[which], inc=1, device_id=device, device_id_type=MESH)

    def item(self, matrix, to, left, right, depth, block):
        net = self.net
        i = len(self.items)
        slot = i % self.slots
        self.items.append((matrix, to))
        assert self.done_z > i - self.slots
        for entry in self.out.pop(i - self.slots, ()):
            net.settle(entry)

        def body(col):
            term = dot(left, right[:, pl.ds(col, 256)], TN).astype(BF16)
            for y in (0, 1):
                for c in (0, 1):
                    at = (y * 2 + c) * block
                    self.part[slot, c, y, :, pl.ds(col, 256)] = term[at : at + block]

        loop(right.shape[1], 256, body)
        if i >= self.slots:
            pl.semaphore_wait(self.free.at[0], 1)
        self.out[i] = [
            net.send(self.part.at[slot, 1 - net.c], self.from_c.at[slot], self.cs.at[slot], net.device(c=1 - net.c))
        ]

    def step_c(self):
        net = self.net
        i = self.done_c
        self.done_c += 1
        slot = i % self.slots
        net.recv(self.from_c.at[slot], self.cs.at[slot])
        for y in (0, 1):
            self.add(self.part.at[slot, net.c, y], self.from_c.at[slot, y])
        if i + self.slots < self.total:
            self.credit(0, net.device(c=1 - net.c))
        if i >= self.slots:
            pl.semaphore_wait(self.free.at[1], 1)
        self.out[i].append(
            net.send(self.part.at[slot, net.c, 1 - net.y], self.from_y.at[slot], self.ys.at[slot], net.device(y=1 - net.y))
        )

    def step_y(self):
        net = self.net
        i = self.done_y
        self.done_y += 1
        slot = i % self.slots
        matrix, to = self.items[i]
        net.recv(self.from_y.at[slot], self.ys.at[slot])
        self.add(self.part.at[slot, net.c, net.y], self.from_y.at[slot])
        if i + self.slots < self.total:
            self.credit(1, net.device(y=1 - net.y))
        matrices = self.result.shape[0]
        if matrix >= matrices:
            return
        src = self.part.at[slot, net.c, net.y]
        dst = self.result.at[matrix, net.z]
        away = to != net.z
        self.out[i].append(net.send(src, dst, self.zs.at[matrix, net.z], net.device(z=to), away))
        self.out[i].append(net.local(src, dst, jnp.logical_not(away)))
        self.done_z += 1

    def step_z(self):
        net = self.net
        i = self.done_z
        self.done_z += 1
        assert i < self.done_y
        matrix, to = self.items[i]
        m = matrix - self.result.shape[0]
        total = self.part.at[i % self.slots, net.c, net.y]
        behind = jnp.where(to > net.z, net.z > 0, net.z < net.n - 1)
        place = self.line(m, to)

        @pl.when(jnp.logical_and(to != net.z, behind))
        def _():
            net.recv(place, self.ls.at[m, to])
            self.add(total, place)

        side = jnp.where(to > net.z, 0, 1)
        nxt = jnp.where(to > net.z, net.z + 1, net.z - 1)
        there = net.device(z=nxt)
        last = jnp.logical_and(to != net.z, to == nxt)
        self.out[i].append(net.send(total, place, self.ls.at[m, to], there, jnp.logical_and(to != net.z, to != nxt)))
        self.out[i].append(net.send(total, self.totals.at[m, side], self.ls.at[m, net.n + side], there, last))
        self.out[i].append(net.local(total, self.totals.at[m, 2], to == net.z))

    def finish(self):
        net = self.net
        for matrix in range(self.result.shape[0]):
            for d in range(1, net.n):
                block = (net.z + d) % net.n
                net.recv(self.result.at[matrix, block], self.zs.at[matrix, block])
        for m in range(self.totals.shape[0]):
            for side, cond in ((0, net.z > 0), (1, net.z < net.n - 1)):

                @pl.when(cond)
                def _():
                    net.recv(self.totals.at[m, side], self.ls.at[m, net.n + side])


def loop(total, step, body):
    @pl.loop(0, total // step)
    def _(i):
        body(pl.multiple_of(i * step, step))


def turn(field, cosine, sine, lane):
    half = HD // 2
    partner = jnp.where(lane % HD < half, pltpu.roll(field, LANES - half, 1), pltpu.roll(field, half, 1))
    return field * cosine + partner * sine


def head_masks():
    lane = lax.broadcasted_iota(jnp.int32, (1, LANES), 1)
    return (lane < HD).astype(BF16), (lane >= HD).astype(BF16)


def both(field, masks):
    return jnp.concatenate([field * masks[0], field * masks[1]], axis=0)


def pick(stacked, rows):
    lane = lax.broadcasted_iota(jnp.int32, (1, LANES), 1)
    return jnp.where(lane < HD, stacked[:rows], stacked[rows:])


def softmax(queries2, key_rows, allowed):
    scores = dot(queries2, key_rows, NT) * HD ** (-0.5)
    scores = jnp.where(allowed > 0, scores, -1e30)
    raised = jnp.exp(scores - jnp.max(scores, axis=-1, keepdims=True))
    return raised / jnp.sum(raised, axis=-1, keepdims=True)


def attention_kernel(
    dp,
    residual, cotangent, seg_col, seg_row, gains, freq, wa, wf,
    wa_out, wf_out, grad_out, normed_ffn_out, normed_out, attended_out, qkv_out, mixed_out, tables_out, gains_out,
    weights, pre, all_gains, allowed, grad_own, normed_all, ffn_own, partial, to_x, from_x,
    send_sems, local_sems, gain_sems, q_sems, o_sems, f_sems, g_sems, n_sems, x_sems,
):
    net = Net(dp, send_sems, local_sems)
    n = net.n
    rows, width = residual.shape
    block, cols = wa.shape[1:]
    group = 2 * rows
    part = wf.shape[2] // n
    me, x = net.dp_index, net.x
    net.greet([((me + k) % dp, x) for k in range(1, dp)] + [(me, 1 - x)])

    for k in range(1, dp):
        net.send(gains, all_gains.at[me], gain_sems.at[me], ((me + k) % dp, x))
    all_gains[me] = gains[...]

    def at_weights(first, count):
        return lambda index: weights.at[pl.ds(first, count), pl.ds(pl.multiple_of(index * block, block), block)]

    qkv = Gather(net, wa.at[pl.ds(0, 3)], at_weights(0, 3), q_sems)
    out = Gather(net, wa.at[pl.ds(3, 1)], at_weights(3, 1), o_sems)
    ffn = Exchange(
        net,
        lambda to: wf.at[:, :, pl.ds(pl.multiple_of(to * part, part), part)],
        lambda index: wf_out.at[:, pl.ds(pl.multiple_of(index * block, block), block)],
        f_sems,
    )
    grads = Rows(net, grad_own, grad_out, g_sems)
    ffn_rows = Rows(net, ffn_own, normed_ffn_out, n_sems)
    qkv.start()

    def mask_body(r):
        span = pl.ds(r, 16)
        live = (seg_col[x, span] >= 0).astype(F32)
        grad_own[span] = (cotangent[span].astype(F32) * live).astype(BF16)

    loop(rows, 16, mask_body)

    row_seg = jnp.concatenate([seg_col[0], seg_col[1]], axis=0)
    row_id = lax.broadcasted_iota(jnp.int32, (group, group), 0)
    col_id = lax.broadcasted_iota(jnp.int32, (group, group), 1)
    mask = jnp.logical_and(row_seg == seg_row[...], row_id >= col_id).astype(F32)
    allowed[...] = mask
    places = jnp.sum(mask, axis=1, keepdims=True) - 1.0
    lane = lax.broadcasted_iota(jnp.int32, (group, LANES), 1)
    angles = places * freq[...]
    tables_out[0] = jnp.cos(angles)
    tables_out[1] = jnp.where(lane % HD < HD // 2, -jnp.sin(angles), jnp.sin(angles))

    for k in range(1, dp):
        source = (me + k) % dp
        net.recv(all_gains.at[source], gain_sems.at[source])
    for i in range(dp):
        gains_out[:, i * block : (i + 1) * block] = all_gains[i]

    def norm_body(r):
        value = residual[pl.ds(r, 16)].astype(F32)
        unit = value * lax.rsqrt(jnp.mean(value * value, axis=-1, keepdims=True) + EPSILON)
        to = pl.multiple_of(x * rows + r, 16)
        normed_all[pl.ds(to, 16)] = (unit * gains_out[0:1]).astype(BF16)

    loop(rows, 16, norm_body)
    own_rows = normed_all.at[pl.ds(pl.multiple_of(x * rows, rows), rows)]
    other_rows = normed_all.at[pl.ds(pl.multiple_of((1 - x) * rows, rows), rows)]
    net.send(own_rows, own_rows, x_sems.at[0], net.device(x=1 - x))

    depth = width // n

    def project(b, first):
        qkv.finish(b)
        base = pl.multiple_of(b * depth, depth)

        def body(col):
            for m in range(3):
                term = dot(normed_all[:, pl.ds(base, depth)], weights[m, pl.ds(base, depth), pl.ds(col, 256)])
                to = pl.ds(pl.multiple_of(m * cols + col, 256), 256)
                pre[:, to] = term if first else pre[:, to] + term

        loop(cols, 256, body)

    qkv.step(1)
    qkv.cross(net.z)
    grads.start()
    for s in range(2, n):
        qkv.step(s)
        if s == 2:
            out.start()
            ffn.start()
        qkv.cross_step(s - 1)
    qkv.cross_step(n - 1)
    net.recv(other_rows, x_sems.at[0])
    net.settle(qkv.kept)
    for k in range(n):
        project((net.z + k) % n, k == 0)
    out.cross(net.z)
    for s in range(1, n):
        out.step(s)
        out.cross_step(s)
    masks = head_masks()

    def head_body(col):
        cosine, sine = tables_out[0], tables_out[1]
        queries = turn(pre[:, pl.ds(col, LANES)], cosine, sine, lane).astype(BF16)
        key_rows = turn(pre[:, pl.ds(pl.multiple_of(cols + col, LANES), LANES)], cosine, sine, lane).astype(BF16)
        value_rows = pre[:, pl.ds(pl.multiple_of(2 * cols + col, LANES), LANES)].astype(BF16)
        qkv_out[0, :, pl.ds(col, LANES)] = queries
        qkv_out[1, :, pl.ds(col, LANES)] = key_rows
        qkv_out[2, :, pl.ds(col, LANES)] = value_rows
        may = jnp.concatenate([allowed[...], allowed[...]], axis=0)
        probs = softmax(both(queries, masks), key_rows, may).astype(BF16)
        attended_out[:, pl.ds(col, LANES)] = pick(dot(probs, value_rows), group).astype(BF16)

    loop(cols, LANES, head_body)
    for k in range(1, n):
        ffn.step((net.z + k) % n)
    for k in range(n):
        out.finish((net.z + k) % n)
    net.settle(out.kept)
    kept_weights = net.local(weights, wa_out)

    def out_body(col):
        term = dot(attended_out[...], weights[3, pl.ds(col, 256), :], NT)
        partial[0, :, pl.ds(col, 256)] = term[:rows]
        partial[1, :, pl.ds(col, 256)] = term[rows:]

    loop(width, 256, out_body)

    def to_body(r):
        to_x[pl.ds(r, 16)] = partial[1 - x, pl.ds(r, 16)].astype(BF16)

    loop(rows, 16, to_body)
    net.send(to_x, from_x, x_sems.at[1], net.device(x=1 - x))
    for s in range(1, n):
        grads.step(s)
    net.recv(from_x, x_sems.at[1])

    def mix_body(r):
        span = pl.ds(r, 16)
        value = residual[span].astype(F32) + partial[x, span] + from_x[span].astype(F32)
        mixed_out[span] = value
        unit = value * lax.rsqrt(jnp.mean(value * value, axis=-1, keepdims=True) + EPSILON)
        ffn_own[span] = (unit * gains_out[8:9]).astype(BF16)

    loop(rows, 16, mix_body)
    ffn_rows.start()
    net.local(normed_all, normed_out)
    for s in range(1, n):
        ffn_rows.step(s)
    for k in range(n):
        ffn.cross((net.z + k) % n)
    for k in range(n):
        ffn.finish((net.z + k) % n)
    grads.finish()
    ffn_rows.finish()
    net.drain()


def far_first(net):
    n = net.n
    table = [sorted(range(n), key=lambda b: (-abs(b - z), -b)) for z in range(n)]
    return [sum(jnp.where(net.z == z, table[z][k], 0) for z in range(n)) for k in range(n)]


class RowSum:
    def __init__(self, net, order, part, from_x, from_z, sems):
        self.net, self.order, self.part, self.from_x, self.from_z = net, order, part, from_x, from_z
        self.xs, self.zs = sems
        self.sent = []
        self.done_x = self.done_z = 0

    def start(self, b):
        net = self.net
        self.sent.append(
            net.send(self.part(b, 1 - net.x), self.from_x.at[b], self.xs.at[b], net.device(x=1 - net.x))
        )

    def add(self, total, term):
        def body(r):
            span = pl.ds(r, 16)
            total[span] = (total[span].astype(F32) + term[span].astype(F32)).astype(BF16)

        loop(total.shape[0], 16, body)

    def step_x(self):
        net = self.net
        b = self.order[self.done_x]
        self.done_x += 1
        net.recv(self.from_x.at[b], self.xs.at[b])
        self.add(self.part(b, net.x), self.from_x.at[b])

    def step_z(self):
        net = self.net
        b = self.order[self.done_z]
        self.done_z += 1
        total = self.part(b, net.x)
        behind = jnp.where(b > net.z, net.z > 0, net.z < net.n - 1)

        @pl.when(jnp.logical_and(b != net.z, behind))
        def _():
            net.recv(self.from_z.at[b], self.zs.at[b])
            self.add(total, self.from_z.at[b])

        slot = jnp.where(b == net.z - 1, net.n, b)
        to = jnp.where(b > net.z, net.z + 1, net.z - 1)
        self.sent.append(net.send(total, self.from_z.at[slot], self.zs.at[slot], net.device(z=to), b != net.z))

    def finish(self):
        net = self.net
        total = self.part(net.z, net.x)
        for slot, cond in ((net.z, net.z > 0), (net.n, net.z < net.n - 1)):

            @pl.when(cond)
            def _():
                net.recv(self.from_z.at[slot], self.zs.at[slot])
                self.add(total, self.from_z.at[slot])


def norm_back(grad, value, gain):
    scale = lax.rsqrt(jnp.mean(value * value, axis=-1, keepdims=True) + EPSILON)
    unit = value * scale
    scaled = grad * gain
    back = scale * (scaled - unit * jnp.mean(scaled * unit, axis=-1, keepdims=True))
    return back, grad * unit


def ffn_kernel(
    dp,
    mixed, residual, gains, seg_col, seg_row, tables, normed_ffn_hbm, grad_hbm, wf, normed_hbm, attended_hbm, qkv_hbm, wa,
    result, totals, block_out, input_grad, gain_out,
    weights, grad, hidden, gate_up_grad, back, back_x, back_z, part, from_c, from_y,
    mixed_all, allowed, from_x, gain_sum, ffn_sum, gain_to, gain_from, gain_x,
    send_sems, local_sems, bx_sems, bz_sems, rc_sems, ry_sems, rz_sems, rl_sems, x_sems, gain_sems, free,
):
    net = Net(dp, send_sems, local_sems)
    n, me, x = net.n, net.dp_index, net.x
    rows, width = mixed.shape
    cols = wf.shape[2]
    every = grad.shape[0]
    block = width // dp
    depth = width // n
    pair = 2 * rows
    assert width == 2 * cols and width == 2 * every and wa.shape[2] == cols

    def features(half):
        return weights.at[3, pl.ds(half * every, every)]

    loads = [net.local(normed_ffn_hbm.at[:, pl.ds(half * cols, cols)], features(half)) for half in (0, 1)]
    loads += [net.local(wf.at[m], weights.at[m]) for m in range(3)] + [net.local(grad_hbm, grad)]
    net.greet(
        [((me + k) % dp, x) for k in range(1, dp)] + [(me, 1 - x)]
    )
    order = far_first(net)
    beside = jnp.where(net.z > 0, 1, 0) + jnp.where(net.z < n - 1, 1, 0)
    gate_grad, up_grad = gate_up_grad.at[:, pl.ds(0, cols)], gate_up_grad.at[:, pl.ds(cols, cols)]
    add = gate_up_grad
    backs = RowSum(net, order, lambda b, half: back.at[b, half], back_x, back_z, (bx_sems, bz_sems))
    adds = RowSum(
        net, order, lambda b, half: add.at[pl.ds(pl.multiple_of((b * 2 + half) * rows, rows), rows)],
        back_x, back_z, (bx_sems, bz_sems),
    )
    red = Reduce(
        net, part, from_c, from_y, (result, totals),
        lambda m, to: weights.at[3, pl.ds(pl.multiple_of((m * n + to) * block, block), block)],
        (rc_sems, ry_sems, rz_sems, rl_sems, free), 7 * n,
    )
    for load in loads:
        net.settle(load)

    def chunk(b):
        here = pl.ds(pl.multiple_of(b * pair, pair), pair)

        def hidden_body(col):
            span = pl.ds(col, 256)

            def project(m):
                return dot(features(0)[here], weights[m, pl.ds(0, cols), span]) + dot(
                    features(1)[here], weights[m, pl.ds(cols, cols), span]
                )

            gate, up = project(0), project(1)
            hidden_grad = dot(grad[here], weights[2, :, span])
            sigmoid = 1.0 / (1.0 + jnp.exp(-gate))
            active = gate * sigmoid
            hidden[here, span] = (active * up).astype(BF16)
            gate_grad[here, span] = (hidden_grad * up * sigmoid * (1.0 + gate * (1.0 - sigmoid))).astype(BF16)
            up_grad[here, span] = (hidden_grad * active).astype(BF16)

        loop(cols, 256, hidden_body)

        def back_body(col):
            span = pl.ds(col, 256)
            term = dot(gate_grad[here], weights[0, span, :], NT) + dot(up_grad[here], weights[1, span, :], NT)
            term = term.astype(BF16)
            back[b, 0, :, span] = term[:rows]
            back[b, 1, :, span] = term[rows:]

        loop(width, 256, back_body)
        backs.start(b)

    def add_chunk(b):
        here = pl.ds(pl.multiple_of(b * pair, pair), pair)

        def body(col):
            span = pl.ds(col, 256)
            add[here, span] = dot(hidden[here], weights[2, span, :], NT).astype(BF16)

        loop(width, 256, body)

    def ffn_items(b):
        base = b * depth
        col = pl.ds(pl.multiple_of(base % cols, depth), depth)
        row = pl.ds(pl.multiple_of(base // cols * every, every), every)
        own = pl.ds(pl.multiple_of(base, depth), depth)
        for m in (2, 0, 1):
            left = grad[:, own] if m == 2 else weights[3, row, col]
            red.item(m, b, left, (gate_grad, up_grad, hidden)[m], depth, block)
            if len(red.items) > 1:
                red.step_c()

    for k in range(n):
        chunk(order[k])
        if k > 0:
            backs.step_x()
        if k > 1:
            backs.step_z()
    ffn_items(order[0])
    backs.step_x()
    backs.step_z()
    ffn_items(order[1])
    backs.step_z()
    red.step_y()
    for k in range(2, n):
        ffn_items(order[k])
        red.step_y()
    red.step_c()
    load_out = net.local(wa.at[3], weights.at[3])
    backs.finish()
    ffn_sum[...] = jnp.zeros_like(ffn_sum)

    def mixed_body(r):
        span = pl.ds(r, 16)
        own = pl.ds(pl.multiple_of((net.z * 2 + x) * rows + r, 16), 16)
        term, gain_term = norm_back(back[net.z, x, span].astype(F32), mixed[span], gains[8:9])
        value = grad[own].astype(F32) + term
        input_grad[span] = value
        mixed_all[pl.ds(pl.multiple_of(x * rows + r, 16), 16)] = value.astype(BF16)
        ffn_sum[...] += gain_term[:8] + gain_term[8:]

    loop(rows, 16, mixed_body)
    own_rows = mixed_all.at[pl.ds(pl.multiple_of(x * rows, rows), rows)]
    other_rows = mixed_all.at[pl.ds(pl.multiple_of((1 - x) * rows, rows), rows)]
    net.send(own_rows, own_rows, x_sems.at[0], net.device(x=1 - x))
    pl.semaphore_signal(free.at[2], inc=1, device_id=net.device(x=1 - x), device_id_type=MESH)
    for cond, z in ((net.z > 0, net.z - 1), (net.z < n - 1, net.z + 1)):

        @pl.when(cond)
        def _():
            pl.semaphore_signal(free.at[3], inc=1, device_id=net.device(z=z), device_id_type=MESH)

    for k in range(n):
        add_chunk(order[k])
        red.step_y()
    pl.semaphore_wait(free.at[2], 1)
    load_qkv = net.local(wa.at[pl.ds(0, 3)], weights.at[pl.ds(0, 3)])
    load_parts = [net.local(qkv_hbm.at[m], hidden.at[pl.ds(m * pair, pair)]) for m in range(3)]
    load_attended = net.local(attended_hbm, hidden.at[pl.ds(3 * pair, pair)])
    load_normed = net.local(normed_hbm, grad.at[pl.ds(0, pair)])
    queries_of, keys_of, values_of = [hidden.at[pl.ds(m * pair, pair)] for m in range(3)]
    attended = hidden.at[pl.ds(3 * pair, pair)]
    normed = grad.at[pl.ds(0, pair)]
    grads_of = [
        grad.at[pl.ds(2 * pair, pair), pl.ds(0, cols)],
        grad.at[pl.ds(2 * pair, pair), pl.ds(cols, cols)],
        grad.at[pl.ds(3 * pair, pair), pl.ds(0, cols)],
    ]
    attended_grad = grad.at[pl.ds(3 * pair, pair), pl.ds(cols, cols)]

    row_seg = jnp.concatenate([seg_col[0], seg_col[1]], axis=0)
    row_id = lax.broadcasted_iota(jnp.int32, (pair, pair), 0)
    col_id = lax.broadcasted_iota(jnp.int32, (pair, pair), 1)
    allowed[...] = jnp.logical_and(row_seg == seg_row[...], row_id >= col_id).astype(F32)
    net.settle(load_out)
    net.recv(other_rows, x_sems.at[0])
    for k in range(n):
        adds.start(order[k])

    def attended_body(col):
        span = pl.ds(col, 256)
        attended_grad[:, span] = dot(mixed_all[...], weights[3, :, span]).astype(BF16)

    loop(cols, 256, attended_body)
    for cond, z in ((net.z > 0, net.z - 1), (net.z < n - 1, net.z + 1)):

        @pl.when(cond)
        def _():
            pl.semaphore_signal(free.at[4], inc=1, device_id=net.device(z=z), device_id_type=MESH)

    net.settle(load_attended)

    def attention_items(m, left, right):
        for k in range(n):
            base = pl.ds(pl.multiple_of(order[k] * depth, depth), depth)
            red.item(3 + m, order[k], left[:, base], right, depth, block)
            if red.done_c < len(red.items) - 1:
                red.step_c()

    attention_items(3, mixed_all, attended)
    red.step_c()
    for load in load_parts:
        net.settle(load)
    masks = head_masks()
    lane = lax.broadcasted_iota(jnp.int32, (pair, LANES), 1)

    def head_body(col):
        span = pl.ds(col, LANES)
        cosine, sine = tables[0], tables[1]
        queries, key_rows, value_rows = queries_of[:, span], keys_of[:, span], values_of[:, span]
        out_grad = attended_grad[:, span]
        queries2, out_grad2 = both(queries, masks), both(out_grad, masks)
        may = jnp.concatenate([allowed[...], allowed[...]], axis=0)
        probs = softmax(queries2, key_rows, may)
        value_grad = dot(probs.astype(BF16), out_grad2, TN)
        prob_grad = dot(out_grad2, value_rows, NT)
        score_grad = probs * (prob_grad - jnp.sum(probs * prob_grad, axis=-1, keepdims=True))
        score_grad = score_grad.astype(BF16)
        query_grad = pick(dot(score_grad, key_rows), pair) * HD ** (-0.5)
        key_grad = dot(score_grad, queries2, TN) * HD ** (-0.5)
        grads_of[0][:, span] = turn(query_grad, cosine, -sine, lane).astype(BF16)
        grads_of[1][:, span] = turn(key_grad, cosine, -sine, lane).astype(BF16)
        grads_of[2][:, span] = value_grad.astype(BF16)

    loop(cols, LANES, head_body)
    net.settle(load_qkv)
    net.settle(load_normed)
    while red.done_y < 3 * n:
        red.step_y()
    attention_items(0, normed, grads_of[0])
    pl.semaphore_wait(free.at[4], beside)

    red.step_y()
    red.step_y()
    red.step_z()
    attention_items(1, normed, grads_of[1])
    red.step_y()
    red.step_z()
    red.step_y()
    red.step_z()
    red.step_z()
    attention_items(2, normed, grads_of[2])
    red.step_c()
    for entry in backs.sent:
        net.settle(entry)

    def normed_body(col):
        span = pl.ds(col, 256)
        term = dot(grads_of[0][...], weights[0, span, :], NT)
        term += dot(grads_of[1][...], weights[1, span, :], NT)
        term += dot(grads_of[2][...], weights[2, span, :], NT)
        back[0, 0, :, span] = term[:rows].astype(BF16)
        back[0, 1, :, span] = term[rows:].astype(BF16)

    loop(width, 256, normed_body)
    net.send(back.at[0, 1 - x], from_x, x_sems.at[1], net.device(x=1 - x))
    net.recv(from_x, x_sems.at[1])
    gain_sum[...] = jnp.zeros_like(gain_sum)

    def input_body(r):
        span = pl.ds(r, 16)
        grad_rows = back[0, x, span].astype(F32) + from_x[span].astype(F32)
        term, gain_term = norm_back(grad_rows, residual[span].astype(F32), gains[0:1])
        input_grad[span] += term
        gain_sum[...] += gain_term[:8] + gain_term[8:]

    loop(rows, 16, input_body)
    for i in range(dp):
        gain_to[i, 0:8] = gain_sum[:, i * block : (i + 1) * block]
        gain_to[i, 8:16] = ffn_sum[:, i * block : (i + 1) * block]
    for k in range(1, dp):
        to = (me + k) % dp
        net.send(gain_to.at[to], gain_from.at[me], gain_sems.at[me], (to, x))
    pl.semaphore_wait(free.at[3], beside)

    for k in range(n):
        adds.step_x()
        red.step_y()
        if red.done_z < red.done_y - 1:
            red.step_z()
    for k in range(n):
        red.step_y()
        adds.step_z()
        red.step_z()
    adds.finish()

    def block_body(r):
        span = pl.ds(r, 16)
        block_out[span] = (mixed[span] + adds.part(net.z, x)[span].astype(F32)).astype(BF16)

    loop(rows, 16, block_body)
    total = gain_to[me]
    for k in range(1, dp):
        source = (me + k) % dp
        net.recv(gain_from.at[source], gain_sems.at[source])
        total = total + gain_from[source]
    gain_x[0] = total
    net.send(gain_x.at[0], gain_x.at[1], x_sems.at[2], net.device(x=1 - x))
    while red.done_y < len(red.items):
        red.step_y()
        red.step_z()
    red.step_z()
    net.recv(gain_x.at[1], x_sems.at[2])
    gain_out[...] = gain_x[0] + gain_x[1]
    red.finish()
    net.drain()


def finish_kernel(ffn, attention, gains, qkv_grad, out_grad, gate_up_grad, down_grad, gain_sums):
    q, n = pl.program_id(0), pl.num_programs(0)
    z = lax.axis_index("dp") // 4
    gate_up_grad[...] = ffn[0:2, 0].astype(F32)
    down_grad[...] = ffn[2, 0].astype(F32).T
    total = attention[0, 2].astype(F32)
    total += jnp.where(z > 0, attention[0, 0].astype(F32), 0.0)
    total += jnp.where(z < n - 1, attention[0, 1].astype(F32), 0.0)

    @pl.when(q < 3)
    def _():
        qkv_grad[0] = total

    @pl.when(q == 3)
    def _():
        out_grad[...] = total.T

    gain_sums[0:1] = jnp.sum(gains[0:8], axis=0, keepdims=True)
    gain_sums[1:2] = jnp.sum(gains[8:16], axis=0, keepdims=True)


def call(kernel, collective_id, sends, locals_, vmem, outs, out_specs, scratch, sems, flags=0):
    def typed(entry):
        return (entry[:-1], F32) if entry[-1] is F32 else (entry, BF16)

    dma = pltpu.SemaphoreType.DMA
    return lambda in_specs, *args: pl.pallas_call(
        kernel,
        out_shape=[jax.ShapeDtypeStruct(*typed(entry)) for entry in outs],
        in_specs=in_specs,
        out_specs=out_specs,
        scratch_shapes=[pltpu.VMEM(*typed(entry)) for entry in scratch] + [dma((sends,)), dma((locals_,))] + [dma(entry) for entry in sems] + [pltpu.SemaphoreType.REGULAR((flags,))] * (flags > 0),
        compiler_params=pltpu.CompilerParams(collective_id=collective_id, has_side_effects=True, vmem_limit_bytes=vmem),
    )(*args)


def shards(dp, residual, seg_ids, attn_gain, w_qkv, w_out, ffn_gain, w_gate_up, w_down, cotangent):
    n = dp // 4
    rows, width = residual.shape
    group = seg_ids.shape[0]
    block, cols = w_qkv.shape[1:]
    part = w_gate_up.shape[2] // n
    wa = jnp.concatenate([w_qkv, w_out.T[None]], axis=0)
    wf = jnp.concatenate([w_gate_up, w_down.T[None]], axis=0)
    seg_col = seg_ids.reshape(2, rows, 1)
    seg_row = seg_ids.reshape(1, group)
    gains = jnp.concatenate(
        [jnp.broadcast_to(gain.astype(F32)[None], (8, block)) for gain in (attn_gain, ffn_gain)], axis=0
    )
    pairs = jnp.arange(LANES, dtype=jnp.int32) % (HD // 2)
    freq = (ROPE_BASE ** (-(pairs.astype(F32) * 2.0 / HD)))[None]
    mib = 1024 * 1024

    first = call(
        functools.partial(attention_kernel, dp), 1, 192, 8, 60 * mib,
        [
            (4, width, cols), (3, width, part), (n, 2, rows, width), (n, 2, rows, width), (group, width),
            (group, cols), (3, group, cols), (rows, width, F32), (2, group, LANES, F32), (16, width, F32),
        ],
        [ANY] * 5 + [VM] * 5,
        [
            (4, width, cols), (group, 3 * cols, F32), (dp, 16, block, F32), (group, group, F32),
            (rows, width), (group, width), (rows, width), (2, rows, width, F32), (rows, width), (rows, width),
        ],
        [(dp,), (4, n), (4, n), (4, n), (2, n), (2, n), (2,)],
    )
    (weights, ffn_weights, grad_all, normed_ffn, normed, attended, qkv, mixed, tables, all_gains) = first(
        [VM] * 6 + [ANY] * 2, residual, cotangent, seg_col, seg_row, gains, freq, wa, wf
    )
    every = n * 2 * rows
    slots = 3 * n
    second = call(
        functools.partial(ffn_kernel, dp), 2, 192, 64, 63 * mib,
        [(3, n, block, part), (4, 3, block, cols), (rows, width), (rows, width, F32), (16, block, F32)],
        [ANY] * 2 + [VM] * 3,
        [
            (4, width, part), (every, width), (every, part), (every, 2 * part),
            (n, 2, rows, width), (n, rows, width), (n + 1, rows, width),
            (slots, 2, 2, block, part), (slots, 2, block, part), (slots, block, part),
            (group, width), (group, group, F32), (rows, width), (8, width, F32), (8, width, F32),
            (dp, 16, block, F32), (dp, 16, block, F32), (2, 16, block, F32),
        ],
        [(n,), (n + 1,), (slots,), (slots,), (3, n), (4, n + 2), (3,), (dp,)],
        5,
    )
    result, totals, block_out, input_grad, gain_grads = second(
        [VM] * 6 + [ANY] * 7, mixed, residual, all_gains, seg_col, seg_row, tables, normed_ffn.reshape(every, width),
        grad_all.reshape(every, width), ffn_weights, normed, attended, qkv, weights,
    )
    qkv_grad, out_grad, gate_up_grad, down_grad, gain_sums = pl.pallas_call(
        finish_kernel,
        grid=(n,),
        out_shape=[
            jax.ShapeDtypeStruct(entry, F32)
            for entry in ((3, block, cols), (cols, block), (2, block, n * part), (n * part, block), (2, block))
        ],
        in_specs=[
            pl.BlockSpec((3, 1, block, part), lambda q: (0, q, 0, 0)),
            pl.BlockSpec((1, 3, block, cols), lambda q: (q, 0, 0, 0)),
            pl.BlockSpec((16, block), lambda q: (0, 0)),
        ],
        out_specs=[
            pl.BlockSpec((1, block, cols), lambda q: (jnp.minimum(q, 2), 0, 0)),
            pl.BlockSpec((cols, block), lambda q: (0, 0)),
            pl.BlockSpec((2, block, part), lambda q: (0, 0, q)),
            pl.BlockSpec((part, block), lambda q: (q, 0)),
            pl.BlockSpec((2, block), lambda q: (0, 0)),
        ],
        compiler_params=pltpu.CompilerParams(vmem_limit_bytes=32 * mib),
    )(result, totals, gain_grads)
    return block_out, input_grad, gain_sums[0], qkv_grad, out_grad, gain_sums[1], gate_up_grad, down_grad


def positions(segments):
    row_index = jnp.arange(segments.shape[1], dtype=jnp.int32)[None, :]
    previous = jnp.concatenate([segments[:, :1] - 1, segments[:, :-1]], axis=1)
    run_start = lax.cummax(jnp.where(segments != previous, row_index, 0), axis=1)
    return row_index - run_start


def rope_tables(places, head_dim):
    half_dim = head_dim // 2
    frequency = ROPE_BASE ** (-(jnp.arange(half_dim, dtype=jnp.float32) * 2.0 / head_dim))
    angles = places.astype(jnp.float32)[:, None, None] * frequency[None, None, :]
    return (jnp.cos(angles), jnp.sin(angles))


def rotate(field, cosine, sine_table):
    half_dim = field.shape[-1] // 2
    lower_half = field[..., :half_dim]
    upper_half = field[..., half_dim:]
    return jnp.concatenate(
        [
            lower_half * cosine - upper_half * sine_table,
            upper_half * cosine + lower_half * sine_table,
        ],
        axis=-1,
    )


def unrotate(field, cosine, sine_table):
    half_dim = field.shape[-1] // 2
    lower_half = field[..., :half_dim]
    upper_half = field[..., half_dim:]
    return jnp.concatenate(
        [
            lower_half * cosine + upper_half * sine_table,
            upper_half * cosine - lower_half * sine_table,
        ],
        axis=-1,
    )


def attention_scores(queries, key_rows, allowed):
    scores = jnp.einsum(
        "qhd,khd->hqk", queries, key_rows, preferred_element_type=jnp.float32
    ) * queries.shape[-1] ** (-0.5)
    return jnp.where(allowed[None], scores, -1e30)


def plain_shards(residual_in, seg_ids, attn_gain, w_qkv, w_out, ffn_gain, w_gate_up, w_down, cotangent):
    rows_local = residual_in.shape[0]
    group_rows = seg_ids.shape[0]
    offset = lax.axis_index("tensor") * rows_local
    live_rows = (lax.dynamic_slice_in_dim(seg_ids, offset, rows_local) >= 0).astype(jnp.float32)
    residual = residual_in.astype(jnp.float32)
    contract_rows = (((0,), (0,)), ((), ()))
    contract_cols = (((1,), (1,)), ((), ()))
    gain_attn, qkv_full, out_full = (
        lax.all_gather(attn_gain, "dp", axis=0, tiled=True),
        lax.all_gather(w_qkv, "dp", axis=1, tiled=True),
        lax.all_gather(w_out, "dp", axis=1, tiled=True),
    )
    norm_attn = lax.rsqrt(jnp.mean(residual * residual, axis=-1, keepdims=True) + EPSILON)
    unit_attn = residual * norm_attn
    normed = (unit_attn * gain_attn.astype(jnp.float32)).astype(jnp.bfloat16)
    normed_all = lax.all_gather(normed, "tensor", axis=0, tiled=True)
    projected = jnp.einsum("rd,cde->cre", normed_all, qkv_full, preferred_element_type=jnp.float32)
    head_count = qkv_full.shape[2] // HD
    head_shape = (group_rows, head_count, HD)
    cosine, sine_table = rope_tables(positions(seg_ids[None, :])[0], HD)
    queries = rotate(projected[0].reshape(head_shape), cosine, sine_table).astype(jnp.bfloat16)
    key_rows = rotate(projected[1].reshape(head_shape), cosine, sine_table).astype(jnp.bfloat16)
    value_rows = projected[2].reshape(head_shape).astype(jnp.bfloat16)
    row_index = jnp.arange(group_rows)
    allowed = (seg_ids[:, None] == seg_ids[None, :]) & (row_index[:, None] >= row_index[None, :])
    scores = attention_scores(queries, key_rows, allowed)
    row_top = jnp.max(scores, axis=-1, keepdims=True)
    log_total = row_top + jnp.log(jnp.sum(jnp.exp(scores - row_top), axis=-1, keepdims=True))
    weights = jnp.exp(scores - log_total).astype(jnp.bfloat16)
    attended = jnp.einsum("hqk,khd->qhd", weights, value_rows, preferred_element_type=jnp.float32)
    attended = attended.reshape(group_rows, head_count * HD).astype(jnp.bfloat16)
    mixed = residual + lax.psum_scatter(
        jnp.dot(attended, out_full, preferred_element_type=jnp.float32),
        "tensor",
        scatter_dimension=0,
        tiled=True,
    )
    gain_ffn, gate_up_full, down_full = (
        lax.all_gather(ffn_gain, "dp", axis=0, tiled=True),
        lax.all_gather(w_gate_up, "dp", axis=1, tiled=True),
        lax.all_gather(w_down, "dp", axis=1, tiled=True),
    )
    norm_ffn = lax.rsqrt(jnp.mean(mixed * mixed, axis=-1, keepdims=True) + EPSILON)
    unit_ffn = mixed * norm_ffn
    normed_ffn = (unit_ffn * gain_ffn.astype(jnp.float32)).astype(jnp.bfloat16)
    normed_ffn_all = lax.all_gather(normed_ffn, "tensor", axis=0, tiled=True)
    gate_up = jnp.einsum(
        "rd,cde->cre", normed_ffn_all, gate_up_full, preferred_element_type=jnp.float32
    )
    gate_pre = gate_up[0]
    up_pre = gate_up[1]
    sigmoid_gate = jax.nn.sigmoid(gate_pre)
    activated = gate_pre * sigmoid_gate
    hidden = (activated * up_pre).astype(jnp.bfloat16)
    output = mixed + lax.psum_scatter(
        jnp.dot(hidden, down_full, preferred_element_type=jnp.float32).astype(jnp.bfloat16),
        "tensor",
        scatter_dimension=0,
        tiled=True,
    ).astype(jnp.float32)
    grad_out = cotangent.astype(jnp.float32) * live_rows[:, None]
    grad_all = lax.all_gather(grad_out.astype(jnp.bfloat16), "tensor", axis=0, tiled=True)
    down_grad = lax.dot_general(hidden, grad_all, contract_rows, preferred_element_type=jnp.float32)
    hidden_grad = lax.dot_general(
        grad_all, down_full, contract_cols, preferred_element_type=jnp.float32
    )
    gate_grads = jnp.stack(
        [
            hidden_grad * up_pre * sigmoid_gate * (1.0 + gate_pre * (1.0 - sigmoid_gate)),
            hidden_grad * activated,
        ]
    ).astype(jnp.bfloat16)
    gate_up_grad = jnp.einsum(
        "rd,cre->cde", normed_ffn_all, gate_grads, preferred_element_type=jnp.float32
    )
    normed_ffn_grad = lax.psum_scatter(
        jnp.einsum("cre,cde->rd", gate_grads, gate_up_full, preferred_element_type=jnp.float32),
        "tensor",
        scatter_dimension=0,
        tiled=True,
    )
    ffn_gain_part = jnp.sum(normed_ffn_grad * unit_ffn, axis=0)
    scaled_ffn = normed_ffn_grad * gain_ffn.astype(jnp.float32)
    mixed_grad = grad_out + norm_ffn * (
        scaled_ffn - unit_ffn * jnp.mean(scaled_ffn * unit_ffn, axis=-1, keepdims=True)
    )
    mixed_all = lax.all_gather(mixed_grad.astype(jnp.bfloat16), "tensor", axis=0, tiled=True)
    out_grad = lax.dot_general(
        attended, mixed_all, contract_rows, preferred_element_type=jnp.float32
    )
    attended_grad = lax.dot_general(
        mixed_all, out_full, contract_cols, preferred_element_type=jnp.float32
    )
    attended_grad = attended_grad.astype(jnp.bfloat16).reshape(head_shape)
    probabilities = jnp.exp(attention_scores(queries, key_rows, allowed) - log_total)
    value_grad = jnp.einsum(
        "hqk,qhd->khd",
        probabilities.astype(jnp.bfloat16),
        attended_grad,
        preferred_element_type=jnp.float32,
    )
    prob_grad = jnp.einsum(
        "qhd,khd->hqk", attended_grad, value_rows, preferred_element_type=jnp.float32
    )
    score_grad = (
        probabilities * (prob_grad - jnp.sum(probabilities * prob_grad, axis=-1, keepdims=True))
    ).astype(jnp.bfloat16)
    scale_factor = HD ** (-0.5)
    query_grad = (
        jnp.einsum("hqk,khd->qhd", score_grad, key_rows, preferred_element_type=jnp.float32)
        * scale_factor
    )
    key_grad = (
        jnp.einsum("hqk,qhd->khd", score_grad, queries, preferred_element_type=jnp.float32)
        * scale_factor
    )
    qkv_grads = jnp.stack(
        [
            unrotate(query_grad, cosine, sine_table),
            unrotate(key_grad, cosine, sine_table),
            value_grad,
        ]
    )
    qkv_grads = qkv_grads.reshape(3, group_rows, head_count * HD).astype(jnp.bfloat16)
    qkv_grad = jnp.einsum("rd,cre->cde", normed_all, qkv_grads, preferred_element_type=jnp.float32)
    normed_grad = lax.psum_scatter(
        jnp.einsum("cre,cde->rd", qkv_grads, qkv_full, preferred_element_type=jnp.float32),
        "tensor",
        scatter_dimension=0,
        tiled=True,
    )
    attn_gain_part = jnp.sum(normed_grad * unit_attn, axis=0)
    scaled_attn = normed_grad * gain_attn.astype(jnp.float32)
    input_grad = mixed_grad + norm_attn * (
        scaled_attn - unit_attn * jnp.mean(scaled_attn * unit_attn, axis=-1, keepdims=True)
    )
    (
        query_total,
        key_total,
        value_total,
        out_total,
        attn_gain_total,
        gate_total,
        up_total,
        down_total,
        ffn_gain_total,
    ) = (
        lax.psum_scatter(qkv_grad[0], "dp", scatter_dimension=0, tiled=True),
        lax.psum_scatter(qkv_grad[1], "dp", scatter_dimension=0, tiled=True),
        lax.psum_scatter(qkv_grad[2], "dp", scatter_dimension=0, tiled=True),
        lax.psum_scatter(out_grad, "dp", scatter_dimension=1, tiled=True),
        lax.psum_scatter(attn_gain_part, "dp", scatter_dimension=0, tiled=True),
        lax.psum_scatter(gate_up_grad[0], "dp", scatter_dimension=0, tiled=True),
        lax.psum_scatter(gate_up_grad[1], "dp", scatter_dimension=0, tiled=True),
        lax.psum_scatter(down_grad, "dp", scatter_dimension=1, tiled=True),
        lax.psum_scatter(ffn_gain_part, "dp", scatter_dimension=0, tiled=True),
    )
    gate_up_total = jnp.stack([gate_total, up_total])
    qkv_total = jnp.stack([query_total, key_total, value_total])
    attn_gain_sum, ffn_gain_sum = lax.psum((attn_gain_total, ffn_gain_total), "tensor")
    return (
        output.astype(jnp.bfloat16),
        input_grad,
        attn_gain_sum,
        qkv_total,
        out_total,
        ffn_gain_sum,
        gate_up_total,
        down_total,
    )


def solution(mesh):
    in_specs = (
        P(("dp", "tensor"), None),
        P("dp"),
        P("dp"),
        P(None, "dp", "tensor"),
        P("tensor", "dp"),
        P("dp"),
        P(None, "dp", "tensor"),
        P("tensor", "dp"),
        P(("dp", "tensor"), None),
    )
    out_specs = (
        P(("dp", "tensor"), None),
        P(("dp", "tensor"), None),
        P("dp"),
        P(None, "dp", "tensor"),
        P("tensor", "dp"),
        P("dp"),
        P(None, "dp", "tensor"),
        P("tensor", "dp"),
    )
    dp = mesh.shape["dp"]
    local = functools.partial(shards, dp) if dp == 16 else plain_shards
    return jax.shard_map(local, mesh=mesh, in_specs=in_specs, out_specs=out_specs, check_vma=False)
```

```python
import functools

import jax
import jax.numpy as jnp
from jax import lax
from jax.experimental import pallas as pl
from jax.experimental.pallas import tpu as pltpu
from jax.sharding import PartitionSpec as P

HD = 64
EPSILON = 1e-05
ROPE_BASE = 130000.0
MESH = pl.DeviceIdType.MESH
ANY = pl.BlockSpec(memory_space=pl.ANY)
VM = pl.BlockSpec(memory_space=pltpu.VMEM)
F32 = jnp.float32
BF16 = jnp.bfloat16
LANES = 128
NT = (((1,), (1,)), ((), ()))
TN = (((0,), (0,)), ((), ()))
NN = (((1,), (0,)), ((), ()))


def dot(a, b, dims=NN):
    return lax.dot_general(a, b, dims, preferred_element_type=F32)


def when(cond, action):
    if cond is None:
        action()
    else:
        pl.when(cond)(action)


class Net:
    def __init__(self, dp, send_sems, local_sems):
        self.n = dp // 4
        self.dp_index = lax.axis_index("dp")
        self.x = lax.axis_index("tensor")
        self.z = self.dp_index // 4
        self.y = (self.dp_index // 2) % 2
        self.c = self.dp_index % 2
        self.send_sems = send_sems
        self.local_sems = local_sems
        self.sent = 0
        self.moved = 0
        self.pending = []
        self.kept = []

    def place(self, z, y, c):
        return (z * 2 + y) * 2 + c

    def device(self, z=None, y=None, c=None, x=None):
        z = self.z if z is None else z
        y = self.y if y is None else y
        c = self.c if c is None else c
        x = self.x if x is None else x
        return (self.place(z, y, c), x)

    def greet(self, devices):
        barrier = pltpu.get_barrier_semaphore()
        for device in devices:
            pl.semaphore_signal(barrier, inc=1, device_id=device, device_id_type=MESH)
        pl.semaphore_wait(barrier, len(devices))

    def send(self, src, dst, recv_sem, device, cond=None):
        sem = self.send_sems.at[self.sent]
        self.sent += 1
        copy = pltpu.make_async_remote_copy(
            src_ref=src, dst_ref=dst, send_sem=sem, recv_sem=recv_sem, device_id=device, device_id_type=MESH
        )
        when(cond, copy.start)
        self.pending.append((cond, copy))
        return self.pending[-1]

    def recv(self, dst, recv_sem):
        pltpu.make_async_remote_copy(
            src_ref=dst, dst_ref=dst, send_sem=self.send_sems.at[0], recv_sem=recv_sem,
            device_id=self.device(c=1 - self.c), device_id_type=MESH,
        ).wait_recv()

    def local(self, src, dst, cond=None):
        sem = self.local_sems.at[self.moved]
        self.moved += 1
        copy = pltpu.make_async_copy(src, dst, sem)
        when(cond, copy.start)
        self.kept.append((cond, copy))
        return self.kept[-1]

    def settle(self, entry):
        for entries, wait in ((self.kept, "wait"), (self.pending, "wait_send")):
            for k, known in enumerate(entries):
                if known is entry:
                    when(entry[0], getattr(entry[1], wait))
                    del entries[k]
                    return

    def drain(self):
        assert self.sent <= self.send_sems.shape[0] and self.moved <= self.local_sems.shape[0]
        for cond, copy in self.pending:
            when(cond, copy.wait_send)
        for cond, copy in self.kept:
            when(cond, copy.wait)


class Gather:
    def __init__(self, net, own, at, sems):
        self.net, self.own, self.at = net, own, at
        self.sems = sems

    def spread(self, block, src, ysend=True):
        net = self.net
        here = net.place(block, net.y, net.c)
        net.send(src, self.at(here), self.sems.at[1, block], net.device(y=1 - net.y))
        net.send(src, self.at(here), self.sems.at[2 + net.y, block], net.device(c=1 - net.c))

    def start(self):
        net = self.net
        here = self.at(net.dp_index)
        net.send(self.own, here, self.sems.at[0, net.z], net.device(z=net.z + 1), net.z < net.n - 1)
        net.send(self.own, here, self.sems.at[0, net.z], net.device(z=net.z - 1), net.z > 0)
        self.spread(net.z, self.own)
        self.kept = net.local(self.own, here)

    def step(self, s):
        net = self.net
        for sign in (1, -1):
            block = net.z - s * sign
            valid = jnp.logical_and(block >= 0, block < net.n)
            nxt = net.z + sign
            more = jnp.logical_and(nxt >= 0, nxt < net.n)
            here = self.at(net.place(block, net.y, net.c))

            @pl.when(valid)
            def _():
                net.recv(here, self.sems.at[0, block])

            net.send(here, here, self.sems.at[0, block], net.device(z=nxt), jnp.logical_and(valid, more))
            net.send(here, here, self.sems.at[1, block], net.device(y=1 - net.y), valid)
            net.send(here, here, self.sems.at[2 + net.y, block], net.device(c=1 - net.c), valid)

    def cross(self, block):
        net = self.net
        there = self.at(net.place(block, 1 - net.y, net.c))
        net.recv(there, self.sems.at[1, block])
        net.send(there, there, self.sems.at[3 - net.y, block], net.device(c=1 - net.c))

    def cross_step(self, s):
        net = self.net
        if s == 0:
            self.cross(net.z)
            return
        for sign in (1, -1):
            block = net.z - s * sign
            valid = jnp.logical_and(block >= 0, block < net.n)
            there = self.at(net.place(block, 1 - net.y, net.c))

            @pl.when(valid)
            def _():
                net.recv(there, self.sems.at[1, block])

            net.send(there, there, self.sems.at[3 - net.y, block], net.device(c=1 - net.c), valid)

    def finish(self, block):
        net = self.net
        for y in (0, 1):
            net.recv(self.at(net.place(block, y, 1 - net.c)), self.sems.at[2 + y, block])


class Exchange:
    def __init__(self, net, part, at, sems):
        self.net, self.part, self.at = net, part, at
        self.sems = sems

    def start(self):
        net = self.net
        here = self.at(net.dp_index)
        for d in list(range(1, net.n)):
            to = (net.z + d) % net.n
            net.send(self.part(to), here, self.sems.at[0, net.z], net.device(z=to))
        own = self.part(net.z)
        net.send(own, here, self.sems.at[1, net.z], net.device(y=1 - net.y))
        net.send(own, here, self.sems.at[2 + net.y, net.z], net.device(c=1 - net.c))
        self.kept = net.local(own, here)

    def step(self, block):
        net = self.net
        here = self.at(net.place(block, net.y, net.c))
        net.recv(here, self.sems.at[0, block])
        net.send(here, here, self.sems.at[1, block], net.device(y=1 - net.y))
        net.send(here, here, self.sems.at[2 + net.y, block], net.device(c=1 - net.c))

    cross = Gather.cross
    finish = Gather.finish


class Rows:
    def __init__(self, net, own, full, sems):
        self.net, self.own, self.full = net, own, full
        self.sems = sems

    def start(self):
        net = self.net
        here = self.full.at[net.z, net.x]
        net.send(self.own, here, self.sems.at[0, net.z], net.device(z=net.z + 1), net.z < net.n - 1)
        net.send(self.own, here, self.sems.at[0, net.z], net.device(z=net.z - 1), net.z > 0)
        net.send(self.own, here, self.sems.at[1, net.z], net.device(x=1 - net.x))
        self.kept = net.local(self.own, here)

    def step(self, s):
        net = self.net
        for sign in (1, -1):
            block = net.z - s * sign
            valid = jnp.logical_and(block >= 0, block < net.n)
            nxt = net.z + sign
            more = jnp.logical_and(nxt >= 0, nxt < net.n)
            here = self.full.at[block, net.x]

            @pl.when(valid)
            def _():
                net.recv(here, self.sems.at[0, block])

            net.send(here, here, self.sems.at[0, block], net.device(z=nxt), jnp.logical_and(valid, more))
            net.send(here, here, self.sems.at[1, block], net.device(x=1 - net.x), valid)

    def finish(self):
        net = self.net
        for block in range(net.n):
            net.recv(self.full.at[block, 1 - net.x], self.sems.at[1, block])


class Reduce:
    def __init__(self, net, part, from_c, from_y, result, line, sems, total):
        self.net, self.part, self.from_c, self.from_y = net, part, from_c, from_y
        self.result, self.totals = result
        self.line = line
        self.cs, self.ys, self.zs, self.ls, self.free = sems
        self.slots = part.shape[0]
        self.total = total
        self.items = []
        self.out = {}
        self.done_c = self.done_y = self.done_z = 0

    def add(self, total, term):
        def body(r):
            span = pl.ds(r, 16)
            total[span] = (total[span].astype(F32) + term[span].astype(F32)).astype(BF16)

        loop(total.shape[0], 16, body)

    def credit(self, which, device):
        pl.semaphore_signal(self.free.at[which], inc=1, device_id=device, device_id_type=MESH)

    def item(self, matrix, to, left, right, depth, block):
        net = self.net
        i = len(self.items)
        slot = i % self.slots
        self.items.append((matrix, to))
        assert self.done_z > i - self.slots
        for entry in self.out.pop(i - self.slots, ()):
            net.settle(entry)

        def body(col):
            term = dot(left, right[:, pl.ds(col, 256)], TN).astype(BF16)
            for y in (0, 1):
                for c in (0, 1):
                    at = (y * 2 + c) * block
                    self.part[slot, c, y, :, pl.ds(col, 256)] = term[at : at + block]

        loop(right.shape[1], 256, body)
        if i >= self.slots:
            pl.semaphore_wait(self.free.at[0], 1)
        self.out[i] = [
            net.send(self.part.at[slot, 1 - net.c], self.from_c.at[slot], self.cs.at[slot], net.device(c=1 - net.c))
        ]

    def step_c(self):
        net = self.net
        i = self.done_c
        self.done_c += 1
        slot = i % self.slots
        net.recv(self.from_c.at[slot], self.cs.at[slot])
        for y in (0, 1):
            self.add(self.part.at[slot, net.c, y], self.from_c.at[slot, y])
        if i + self.slots < self.total:
            self.credit(0, net.device(c=1 - net.c))
        if i >= self.slots:
            pl.semaphore_wait(self.free.at[1], 1)
        self.out[i].append(
            net.send(self.part.at[slot, net.c, 1 - net.y], self.from_y.at[slot], self.ys.at[slot], net.device(y=1 - net.y))
        )

    def step_y(self):
        net = self.net
        i = self.done_y
        self.done_y += 1
        slot = i % self.slots
        matrix, to = self.items[i]
        net.recv(self.from_y.at[slot], self.ys.at[slot])
        self.add(self.part.at[slot, net.c, net.y], self.from_y.at[slot])
        if i + self.slots < self.total:
            self.credit(1, net.device(y=1 - net.y))
        matrices = self.result.shape[0]
        if matrix >= matrices:
            return
        src = self.part.at[slot, net.c, net.y]
        dst = self.result.at[matrix, net.z]
        away = to != net.z
        self.out[i].append(net.send(src, dst, self.zs.at[matrix, net.z], net.device(z=to), away))
        self.out[i].append(net.local(src, dst, jnp.logical_not(away)))
        self.done_z += 1

    def step_z(self):
        net = self.net
        i = self.done_z
        self.done_z += 1
        assert i < self.done_y
        matrix, to = self.items[i]
        m = matrix - self.result.shape[0]
        total = self.part.at[i % self.slots, net.c, net.y]
        behind = jnp.where(to > net.z, net.z > 0, net.z < net.n - 1)
        place = self.line(m, to)

        @pl.when(jnp.logical_and(to != net.z, behind))
        def _():
            net.recv(place, self.ls.at[m, to])
            self.add(total, place)

        side = jnp.where(to > net.z, 0, 1)
        nxt = jnp.where(to > net.z, net.z + 1, net.z - 1)
        there = net.device(z=nxt)
        last = jnp.logical_and(to != net.z, to == nxt)
        self.out[i].append(net.send(total, place, self.ls.at[m, to], there, jnp.logical_and(to != net.z, to != nxt)))
        self.out[i].append(net.send(total, self.totals.at[m, side], self.ls.at[m, net.n + side], there, last))
        self.out[i].append(net.local(total, self.totals.at[m, 2], to == net.z))

    def finish(self):
        net = self.net
        for matrix in range(self.result.shape[0]):
            for d in range(1, net.n):
                block = (net.z + d) % net.n
                net.recv(self.result.at[matrix, block], self.zs.at[matrix, block])
        for m in range(self.totals.shape[0]):
            for side, cond in ((0, net.z > 0), (1, net.z < net.n - 1)):

                @pl.when(cond)
                def _():
                    net.recv(self.totals.at[m, side], self.ls.at[m, net.n + side])


def loop(total, step, body):
    @pl.loop(0, total // step)
    def _(i):
        body(pl.multiple_of(i * step, step))


def turn(field, cosine, sine, lane):
    half = HD // 2
    partner = jnp.where(lane % HD < half, pltpu.roll(field, LANES - half, 1), pltpu.roll(field, half, 1))
    return field * cosine + partner * sine


def head_masks():
    lane = lax.broadcasted_iota(jnp.int32, (1, LANES), 1)
    return (lane < HD).astype(BF16), (lane >= HD).astype(BF16)


def both(field, masks):
    return jnp.concatenate([field * masks[0], field * masks[1]], axis=0)


def pick(stacked, rows):
    lane = lax.broadcasted_iota(jnp.int32, (1, LANES), 1)
    return jnp.where(lane < HD, stacked[:rows], stacked[rows:])


def softmax(queries2, key_rows, allowed):
    scores = dot(queries2, key_rows, NT) * HD ** (-0.5)
    scores = jnp.where(allowed > 0, scores, -1e30)
    raised = jnp.exp(scores - jnp.max(scores, axis=-1, keepdims=True))
    return raised / jnp.sum(raised, axis=-1, keepdims=True)


def attention_kernel(
    dp,
    residual, cotangent, seg, attn_gain, ffn_gain, freq, w_out, w_down, w_qkv, w_gate_up,
    wa_out, wf_out, grad_out, normed_ffn_out, normed_out, attended_out, qkv_out, mixed_out, tables_out, gains_out, allowed,
    weights, pre, gains, all_gains, live, grad_own, normed_all, ffn_own, partial, to_x, from_x, out_own, down_own,
    send_sems, local_sems, gain_sems, q_sems, o_sems, f_sems, g_sems, n_sems, x_sems,
):
    net = Net(dp, send_sems, local_sems)
    n = net.n
    rows, width = residual.shape
    block, cols = w_qkv.shape[1:]
    group = 2 * rows
    part = w_gate_up.shape[2] // n
    depth = width // n
    me, x = net.dp_index, net.x
    lane = lax.broadcasted_iota(jnp.int32, (group, LANES), 1)
    net.greet([((me + k) % dp, x) for k in range(1, dp)] + [(me, 1 - x)])

    def at_weights(first, count):
        return lambda index: weights.at[pl.ds(first, count), pl.ds(pl.multiple_of(index * block, block), block)]

    def ffn_part(m):
        def own(to):
            span = pl.ds(pl.multiple_of(to * part, part), part)
            return down_own.at[:, span] if m == 2 else w_gate_up.at[m, :, span]

        return own

    def ffn_place(m):
        return lambda index: wf_out.at[m, pl.ds(pl.multiple_of(index * block, block), block)]

    qkv = Gather(net, w_qkv, at_weights(0, 3), q_sems)
    out = Gather(net, out_own, at_weights(3, 1), o_sems)
    ffn = [Exchange(net, ffn_part(m), ffn_place(m), f_sems.at[m]) for m in range(3)]
    grads = Rows(net, grad_own, grad_out, g_sems)
    ffn_rows = Rows(net, ffn_own, normed_ffn_out, n_sems)
    own_rows = normed_all.at[pl.ds(pl.multiple_of(x * rows, rows), rows)]
    other_rows = normed_all.at[pl.ds(pl.multiple_of((1 - x) * rows, rows), rows)]

    def send_gains():
        gains[0:8] = jnp.broadcast_to(attn_gain[...].astype(F32), (8, block))
        gains[8:16] = jnp.broadcast_to(ffn_gain[...].astype(F32), (8, block))
        for k in range(1, dp):
            net.send(gains, all_gains.at[me], gain_sems.at[me], ((me + k) % dp, x))
        all_gains[me] = gains[...]

    def turn_weights():
        out_own[0] = w_out[...].T

        def body(r):
            down_own[:, pl.ds(r, 512)] = w_down[pl.ds(r, 512)].T

        loop(w_down.shape[0], 512, body)

    def mask_grads():
        seg_rows = jnp.broadcast_to(seg[...].astype(F32), (LANES, group))
        seg_cols = seg_rows.T
        alive = (seg_cols >= 0).astype(F32)
        live[0] = alive[:rows]
        live[1] = alive[rows:]
        row_id = lax.broadcasted_iota(jnp.int32, (group, group), 0)
        col_id = lax.broadcasted_iota(jnp.int32, (group, group), 1)
        same = jnp.concatenate([seg_cols] * (group // LANES), axis=1) == jnp.concatenate([seg_rows] * (group // LANES), axis=0)
        mask = jnp.logical_and(same, row_id >= col_id).astype(F32)
        allowed[...] = mask
        angles = (jnp.sum(mask, axis=1, keepdims=True) - 1.0) * freq[...]
        tables_out[0] = jnp.cos(angles)
        tables_out[1] = jnp.where(lane % HD < HD // 2, -jnp.sin(angles), jnp.sin(angles))

        def body(r):
            span = pl.ds(r, 16)
            grad_own[span] = (cotangent[span].astype(F32) * live[x, span, 0:1]).astype(BF16)

        loop(rows, 16, body)

    def norm():
        for k in range(1, dp):
            source = (me + k) % dp
            net.recv(all_gains.at[source], gain_sems.at[source])
        for i in range(dp):
            gains_out[:, i * block : (i + 1) * block] = all_gains[i]

        def body(r):
            value = residual[pl.ds(r, 16)].astype(F32)
            unit = value * lax.rsqrt(jnp.mean(value * value, axis=-1, keepdims=True) + EPSILON)
            to = pl.multiple_of(x * rows + r, 16)
            normed_all[pl.ds(to, 16)] = (unit * gains_out[0:1]).astype(BF16)

        loop(rows, 16, body)
        net.send(own_rows, own_rows, x_sems.at[0], net.device(x=1 - x))

    def project(k):
        if k == 0:
            net.recv(other_rows, x_sems.at[0])
            net.settle(qkv.kept)
            net.local(normed_all, normed_out)
        b = (net.z + k) % n
        qkv.finish(b)
        base = pl.multiple_of(b * depth, depth)

        def body(col):
            for m in range(3):
                term = dot(normed_all[:, pl.ds(base, depth)], weights[m, pl.ds(base, depth), pl.ds(col, 256)])
                to = pl.ds(pl.multiple_of(m * cols + col, 256), 256)
                pre[:, to] = term if k == 0 else pre[:, to] + term

        loop(cols, 256, body)

    def heads():
        masks = head_masks()

        def body(col):
            cosine, sine = tables_out[0], tables_out[1]
            queries = turn(pre[:, pl.ds(col, LANES)], cosine, sine, lane).astype(BF16)
            key_rows = turn(pre[:, pl.ds(pl.multiple_of(cols + col, LANES), LANES)], cosine, sine, lane).astype(BF16)
            value_rows = pre[:, pl.ds(pl.multiple_of(2 * cols + col, LANES), LANES)].astype(BF16)
            qkv_out[0, :, pl.ds(col, LANES)] = queries
            qkv_out[1, :, pl.ds(col, LANES)] = key_rows
            qkv_out[2, :, pl.ds(col, LANES)] = value_rows
            may = jnp.concatenate([allowed[...], allowed[...]], axis=0)
            probs = softmax(both(queries, masks), key_rows, may).astype(BF16)
            attended_out[:, pl.ds(col, LANES)] = pick(dot(probs, value_rows), group).astype(BF16)

        loop(cols, LANES, body)

    def join():
        for k in range(n):
            out.finish((net.z + k) % n)
        net.settle(out.kept)
        net.local(weights, wa_out)

        def body(col):
            term = dot(attended_out[...], weights[3, pl.ds(col, 256), :], NT)
            partial[0, :, pl.ds(col, 256)] = term[:rows]
            partial[1, :, pl.ds(col, 256)] = term[rows:]

        loop(width, 256, body)

        def to_body(r):
            to_x[pl.ds(r, 16)] = partial[1 - x, pl.ds(r, 16)].astype(BF16)

        loop(rows, 16, to_body)
        net.send(to_x, from_x, x_sems.at[1], net.device(x=1 - x))

    def mix():
        net.recv(from_x, x_sems.at[1])

        def body(r):
            span = pl.ds(r, 16)
            value = residual[span].astype(F32) + partial[x, span] + from_x[span].astype(F32)
            mixed_out[span] = value
            unit = value * lax.rsqrt(jnp.mean(value * value, axis=-1, keepdims=True) + EPSILON)
            ffn_own[span] = (unit * gains_out[8:9]).astype(BF16)

        loop(rows, 16, body)

    def ffn_step(m, k):
        ffn[m].step((net.z + k) % n)

    def ffn_cross(m):
        for k in range(n):
            ffn[m].cross((net.z + k) % n)

    qkv.start()
    turn_weights()
    out.start()
    qkv.step(1)
    mask_grads()
    send_gains()
    out.step(1)
    qkv.step(2)
    qkv.cross_step(0)
    norm()
    qkv.cross_step(1)
    ffn[2].start()
    out.step(2)
    grads.start()
    qkv.step(3)
    out.cross_step(0)
    qkv.cross_step(2)
    ffn[0].start()
    qkv.cross_step(3)
    project(0)
    project(1)
    out.cross_step(1)
    project(2)
    project(3)
    out.cross_step(2)
    grads.step(1)
    out.step(3)
    out.cross_step(3)
    ffn_step(2, 3)
    heads()
    ffn[1].start()
    join()
    grads.step(2)
    ffn_step(0, 2)
    ffn_step(0, 3)
    mix()
    ffn_rows.start()
    ffn_step(1, 1)
    ffn_step(2, 2)
    ffn_step(1, 2)
    ffn_step(0, 1)
    grads.step(3)
    ffn_rows.step(1)
    ffn_cross(0)
    ffn_step(1, 3)
    ffn_cross(1)
    ffn_rows.step(2)
    ffn_rows.step(3)
    ffn_step(2, 1)
    ffn_cross(2)
    for m in range(3):
        for k in range(n):
            ffn[m].finish((net.z + k) % n)
    grads.finish()
    ffn_rows.finish()
    net.drain()


def far_first(net):
    n = net.n
    table = [sorted(range(n), key=lambda b: (-abs(b - z), -b)) for z in range(n)]
    return [sum(jnp.where(net.z == z, table[z][k], 0) for z in range(n)) for k in range(n)]


class RowSum:
    def __init__(self, net, order, part, from_x, from_z, sems):
        self.net, self.order, self.part, self.from_x, self.from_z = net, order, part, from_x, from_z
        self.xs, self.zs = sems
        self.sent = []
        self.done_x = self.done_z = 0

    def start(self, b):
        net = self.net
        self.sent.append(
            net.send(self.part(b, 1 - net.x), self.from_x.at[b], self.xs.at[b], net.device(x=1 - net.x))
        )

    def add(self, total, term):
        def body(r):
            span = pl.ds(r, 16)
            total[span] = (total[span].astype(F32) + term[span].astype(F32)).astype(BF16)

        loop(total.shape[0], 16, body)

    def step_x(self):
        net = self.net
        b = self.order[self.done_x]
        self.done_x += 1
        net.recv(self.from_x.at[b], self.xs.at[b])
        self.add(self.part(b, net.x), self.from_x.at[b])

    def step_z(self):
        net = self.net
        b = self.order[self.done_z]
        self.done_z += 1
        total = self.part(b, net.x)
        behind = jnp.where(b > net.z, net.z > 0, net.z < net.n - 1)

        @pl.when(jnp.logical_and(b != net.z, behind))
        def _():
            net.recv(self.from_z.at[b], self.zs.at[b])
            self.add(total, self.from_z.at[b])

        slot = jnp.where(b == net.z - 1, net.n, b)
        to = jnp.where(b > net.z, net.z + 1, net.z - 1)
        self.sent.append(net.send(total, self.from_z.at[slot], self.zs.at[slot], net.device(z=to), b != net.z))

    def finish(self):
        net = self.net
        total = self.part(net.z, net.x)
        for slot, cond in ((net.z, net.z > 0), (net.n, net.z < net.n - 1)):

            @pl.when(cond)
            def _():
                net.recv(self.from_z.at[slot], self.zs.at[slot])
                self.add(total, self.from_z.at[slot])


def norm_back(grad, value, gain):
    scale = lax.rsqrt(jnp.mean(value * value, axis=-1, keepdims=True) + EPSILON)
    unit = value * scale
    scaled = grad * gain
    back = scale * (scaled - unit * jnp.mean(scaled * unit, axis=-1, keepdims=True))
    return back, grad * unit


def ffn_kernel(
    dp,
    mixed, residual, gains, allowed, tables, normed_ffn_hbm, grad_hbm, wf, normed_hbm, attended_hbm, qkv_hbm, wa,
    result, totals, block_out, input_grad, gain_out,
    weights, grad, hidden, gate_up_grad, back, back_x, back_z, part, from_c, from_y,
    mixed_all, from_x, gain_sum, ffn_sum, gain_to, gain_from, gain_x,
    send_sems, local_sems, bx_sems, bz_sems, rc_sems, ry_sems, rz_sems, rl_sems, x_sems, gain_sems, free,
):
    net = Net(dp, send_sems, local_sems)
    n, me, x = net.n, net.dp_index, net.x
    rows, width = mixed.shape
    cols = wf.shape[2]
    every = grad.shape[0]
    block = width // dp
    depth = width // n
    pair = 2 * rows
    assert width == 2 * cols and width == 2 * every and wa.shape[2] == cols

    def features(half):
        return weights.at[3, pl.ds(half * every, every)]

    loads = [net.local(normed_ffn_hbm.at[:, pl.ds(half * cols, cols)], features(half)) for half in (0, 1)]
    loads += [net.local(wf.at[m], weights.at[m]) for m in range(3)] + [net.local(grad_hbm, grad)]
    net.greet(
        [((me + k) % dp, x) for k in range(1, dp)] + [(me, 1 - x)]
    )
    order = far_first(net)
    beside = jnp.where(net.z > 0, 1, 0) + jnp.where(net.z < n - 1, 1, 0)
    gate_grad, up_grad = gate_up_grad.at[:, pl.ds(0, cols)], gate_up_grad.at[:, pl.ds(cols, cols)]
    add = gate_up_grad
    backs = RowSum(net, order, lambda b, half: back.at[b, half], back_x, back_z, (bx_sems, bz_sems))
    adds = RowSum(
        net, order, lambda b, half: add.at[pl.ds(pl.multiple_of((b * 2 + half) * rows, rows), rows)],
        back_x, back_z, (bx_sems, bz_sems),
    )
    red = Reduce(
        net, part, from_c, from_y, (result, totals),
        lambda m, to: weights.at[3, pl.ds(pl.multiple_of((m * n + to) * block, block), block)],
        (rc_sems, ry_sems, rz_sems, rl_sems, free), 7 * n,
    )
    for load in loads:
        net.settle(load)

    def rows_of(b):
        return pl.ds(pl.multiple_of(b * pair, pair), pair)

    def forward(k):
        here = rows_of(order[k])

        def body(col):
            span = pl.ds(col, 256)

            def project(m):
                return dot(features(0)[here], weights[m, pl.ds(0, cols), span]) + dot(
                    features(1)[here], weights[m, pl.ds(cols, cols), span]
                )

            gate, up = project(0), project(1)
            hidden_grad = dot(grad[here], weights[2, :, span])
            sigmoid = 1.0 / (1.0 + jnp.exp(-gate))
            active = gate * sigmoid
            hidden[here, span] = (active * up).astype(BF16)
            gate_grad[here, span] = (hidden_grad * up * sigmoid * (1.0 + gate * (1.0 - sigmoid))).astype(BF16)
            up_grad[here, span] = (hidden_grad * active).astype(BF16)

        loop(cols, 256, body)

    def backward(k):
        b = order[k]
        here = rows_of(b)

        def body(col):
            span = pl.ds(col, 256)
            term = dot(gate_grad[here], weights[0, span, :], NT) + dot(up_grad[here], weights[1, span, :], NT)
            term = term.astype(BF16)
            back[b, 0, :, span] = term[:rows]
            back[b, 1, :, span] = term[rows:]

        loop(width, 256, body)
        backs.start(b)

    def add_chunk(k):
        here = rows_of(order[k])

        def body(col):
            span = pl.ds(col, 256)
            add[here, span] = dot(hidden[here], weights[2, span, :], NT).astype(BF16)

        loop(width, 256, body)

    ffn_items = [(2, k) for k in range(n)] + [(m, k) for k in range(n) for m in (0, 1)]
    attention_items = [(3, k) for k in range(n)] + [(m, k) for k in range(n) for m in range(3)]

    def ffn_item():
        m, k = ffn_items[len(red.items)]
        b = order[k]
        base = b * depth
        if m == 2:
            left = grad[:, pl.ds(pl.multiple_of(base, depth), depth)]
        else:
            row = pl.ds(pl.multiple_of(base // cols * every, every), every)
            left = weights[3, row, pl.ds(pl.multiple_of(base % cols, depth), depth)]
        red.item(m, b, left, (gate_grad, up_grad, hidden)[m], depth, block)

    def attention_item():
        m, k = attention_items[len(red.items) - len(ffn_items)]
        base = pl.ds(pl.multiple_of(order[k] * depth, depth), depth)
        left, right = (mixed_all, attended) if m == 3 else (normed, grads_of[m])
        red.item(3 + m, order[k], left[:, base], right, depth, block)

    queries_of, keys_of, values_of = [hidden.at[pl.ds(m * pair, pair)] for m in range(3)]
    attended = hidden.at[pl.ds(3 * pair, pair)]
    normed = grad.at[pl.ds(0, pair)]
    grads_of = [
        grad.at[pl.ds(2 * pair, pair), pl.ds(0, cols)],
        grad.at[pl.ds(2 * pair, pair), pl.ds(cols, cols)],
        grad.at[pl.ds(3 * pair, pair), pl.ds(0, cols)],
    ]
    attended_grad = grad.at[pl.ds(3 * pair, pair), pl.ds(cols, cols)]
    own_rows = mixed_all.at[pl.ds(pl.multiple_of(x * rows, rows), rows)]
    other_rows = mixed_all.at[pl.ds(pl.multiple_of((1 - x) * rows, rows), rows)]
    late = {}

    def tell_beside(which):
        for cond, z in ((net.z > 0, net.z - 1), (net.z < n - 1, net.z + 1)):

            @pl.when(cond)
            def _():
                pl.semaphore_signal(free.at[which], inc=1, device_id=net.device(z=z), device_id_type=MESH)

    def mix_grads():
        backs.finish()
        ffn_sum[...] = jnp.zeros_like(ffn_sum)

        def body(r):
            span = pl.ds(r, 16)
            own = pl.ds(pl.multiple_of((net.z * 2 + x) * rows + r, 16), 16)
            term, gain_term = norm_back(back[net.z, x, span].astype(F32), mixed[span], gains[8:9])
            value = grad[own].astype(F32) + term
            input_grad[span] = value
            mixed_all[pl.ds(pl.multiple_of(x * rows + r, 16), 16)] = value.astype(BF16)
            ffn_sum[...] += gain_term[:8] + gain_term[8:]

        loop(rows, 16, body)
        net.send(own_rows, own_rows, x_sems.at[0], net.device(x=1 - x))
        pl.semaphore_signal(free.at[2], inc=1, device_id=net.device(x=1 - x), device_id_type=MESH)
        tell_beside(3)

    def load_out():
        late["out"] = net.local(wa.at[3], weights.at[3])

    def load_rest():
        late["normed"] = net.local(normed_hbm, normed)
        late["qkv"] = net.local(wa.at[pl.ds(0, 3)], weights.at[pl.ds(0, 3)])
        late["parts"] = [net.local(qkv_hbm.at[m], hidden.at[pl.ds(m * pair, pair)]) for m in range(3)]
        late["attended"] = net.local(attended_hbm, attended)

    def start_adds():
        pl.semaphore_wait(free.at[2], 1)
        for k in range(n):
            adds.start(order[k])

    def attended_back():
        net.settle(late["out"])
        net.recv(other_rows, x_sems.at[0])

        def body(col):
            span = pl.ds(col, 256)
            attended_grad[:, span] = dot(mixed_all[...], weights[3, :, span]).astype(BF16)

        loop(cols, 256, body)
        tell_beside(4)
        net.settle(late["attended"])

    def heads():
        for load in late["parts"]:
            net.settle(load)
        masks = head_masks()
        lane = lax.broadcasted_iota(jnp.int32, (pair, LANES), 1)

        def body(col):
            span = pl.ds(col, LANES)
            cosine, sine = tables[0], tables[1]
            queries, key_rows, value_rows = queries_of[:, span], keys_of[:, span], values_of[:, span]
            out_grad = attended_grad[:, span]
            queries2, out_grad2 = both(queries, masks), both(out_grad, masks)
            may = jnp.concatenate([allowed[...], allowed[...]], axis=0)
            probs = softmax(queries2, key_rows, may)
            value_grad = dot(probs.astype(BF16), out_grad2, TN)
            prob_grad = dot(out_grad2, value_rows, NT)
            score_grad = probs * (prob_grad - jnp.sum(probs * prob_grad, axis=-1, keepdims=True))
            score_grad = score_grad.astype(BF16)
            query_grad = pick(dot(score_grad, key_rows), pair) * HD ** (-0.5)
            key_grad = dot(score_grad, queries2, TN) * HD ** (-0.5)
            grads_of[0][:, span] = turn(query_grad, cosine, -sine, lane).astype(BF16)
            grads_of[1][:, span] = turn(key_grad, cosine, -sine, lane).astype(BF16)
            grads_of[2][:, span] = value_grad.astype(BF16)

        loop(cols, LANES, body)
        net.settle(late["normed"])

    def normed_back():
        net.settle(late["qkv"])
        for entry in backs.sent:
            net.settle(entry)

        def body(col):
            span = pl.ds(col, 256)
            term = dot(grads_of[0][...], weights[0, span, :], NT)
            term += dot(grads_of[1][...], weights[1, span, :], NT)
            term += dot(grads_of[2][...], weights[2, span, :], NT)
            back[0, 0, :, span] = term[:rows].astype(BF16)
            back[0, 1, :, span] = term[rows:].astype(BF16)

        loop(width, 256, body)
        net.send(back.at[0, 1 - x], from_x, x_sems.at[1], net.device(x=1 - x))

    def input_back():
        net.recv(from_x, x_sems.at[1])
        gain_sum[...] = jnp.zeros_like(gain_sum)

        def body(r):
            span = pl.ds(r, 16)
            grad_rows = back[0, x, span].astype(F32) + from_x[span].astype(F32)
            term, gain_term = norm_back(grad_rows, residual[span].astype(F32), gains[0:1])
            input_grad[span] += term
            gain_sum[...] += gain_term[:8] + gain_term[8:]

        loop(rows, 16, body)
        for i in range(dp):
            gain_to[i, 0:8] = gain_sum[:, i * block : (i + 1) * block]
            gain_to[i, 8:16] = ffn_sum[:, i * block : (i + 1) * block]
        for k in range(1, dp):
            to = (me + k) % dp
            net.send(gain_to.at[to], gain_from.at[me], gain_sems.at[me], (to, x))

    def sum_gains():
        total = gain_to[me]
        for k in range(1, dp):
            source = (me + k) % dp
            net.recv(gain_from.at[source], gain_sems.at[source])
            total = total + gain_from[source]
        gain_x[0] = total
        net.send(gain_x.at[0], gain_x.at[1], x_sems.at[2], net.device(x=1 - x))

    def block_rows():
        adds.finish()

        def body(r):
            span = pl.ds(r, 16)
            block_out[span] = (mixed[span] + adds.part(net.z, x)[span].astype(F32)).astype(BF16)

        loop(rows, 16, body)

    forward(0)
    backward(0)
    forward(1)
    backward(1)
    forward(2)
    forward(3)
    backs.step_x()
    backs.step_z()
    ffn_item()
    backward(2)
    red.step_c()
    ffn_item()
    backs.step_x()
    ffn_item()
    backs.step_z()
    red.step_c()
    ffn_item()
    red.step_y()
    ffn_item()
    backs.step_x()
    red.step_c()
    red.step_c()
    backs.step_z()
    backward(3)
    ffn_item()
    ffn_item()
    red.step_c()
    red.step_c()
    ffn_item()
    ffn_item()
    red.step_c()
    ffn_item()
    backs.step_x()
    red.step_y()
    red.step_c()
    red.step_y()
    red.step_y()
    red.step_c()
    ffn_item()
    backs.step_z()
    ffn_item()
    add_chunk(0)
    red.step_y()
    red.step_c()
    load_out()
    red.step_y()
    red.step_c()
    red.step_y()
    mix_grads()
    add_chunk(1)
    add_chunk(2)
    red.step_y()
    add_chunk(3)
    red.step_c()
    start_adds()
    load_rest()
    attended_back()
    red.step_y()
    red.step_y()
    pl.semaphore_wait(free.at[3], beside)
    attention_item()
    attention_item()
    red.step_c()
    attention_item()
    red.step_c()
    red.step_y()
    attention_item()
    heads()
    adds.step_x()
    adds.step_z()
    red.step_y()
    pl.semaphore_wait(free.at[4], beside)
    red.step_c()
    adds.step_x()
    attention_item()
    red.step_y()
    red.step_c()
    red.step_y()
    attention_item()
    red.step_c()
    attention_item()
    red.step_z()
    adds.step_z()
    red.step_y()
    red.step_z()
    red.step_y()
    red.step_c()
    attention_item()
    red.step_c()
    attention_item()
    adds.step_x()
    normed_back()
    attention_item()
    red.step_z()
    red.step_c()
    adds.step_z()
    attention_item()
    red.step_c()
    red.step_y()
    attention_item()
    red.step_z()
    red.step_y()
    red.step_c()
    attention_item()
    attention_item()
    red.step_z()
    red.step_y()
    adds.step_x()
    red.step_y()
    red.step_z()
    red.step_c()
    adds.step_z()
    red.step_c()
    red.step_c()
    attention_item()
    input_back()
    red.step_y()
    red.step_y()
    red.step_z()
    red.step_z()
    red.step_c()
    red.step_y()
    attention_item()
    red.step_c()
    red.step_c()
    red.step_y()
    for _ in range(3):
        red.step_z()
    red.step_y()
    sum_gains()
    red.step_z()
    red.step_z()
    for _ in range(3):
        red.step_y()
    block_rows()
    for _ in range(3):
        red.step_z()
    assert red.done_y == red.done_z == red.total and adds.done_z == n
    net.recv(gain_x.at[1], x_sems.at[2])
    gain_out[...] = gain_x[0] + gain_x[1]
    red.finish()
    net.drain()


def finish_kernel(ffn, attention, gains, qkv_grad, out_grad, gate_up_grad, down_grad, gain_sums):
    q, n = pl.program_id(0), pl.num_programs(0)
    z = lax.axis_index("dp") // 4
    gate_up_grad[...] = ffn[0:2, 0].astype(F32)
    down_grad[...] = ffn[2, 0].astype(F32).T
    total = attention[0, 2].astype(F32)
    total += jnp.where(z > 0, attention[0, 0].astype(F32), 0.0)
    total += jnp.where(z < n - 1, attention[0, 1].astype(F32), 0.0)

    @pl.when(q < 3)
    def _():
        qkv_grad[0] = total

    @pl.when(q == 3)
    def _():
        out_grad[...] = total.T

    gain_sums[0:1] = jnp.sum(gains[0:8], axis=0, keepdims=True)
    gain_sums[1:2] = jnp.sum(gains[8:16], axis=0, keepdims=True)


def call(kernel, collective_id, sends, locals_, vmem, outs, out_specs, scratch, sems, flags=0):
    def typed(entry):
        return (entry[:-1], F32) if entry[-1] is F32 else (entry, BF16)

    dma = pltpu.SemaphoreType.DMA
    return lambda in_specs, *args: pl.pallas_call(
        kernel,
        out_shape=[jax.ShapeDtypeStruct(*typed(entry)) for entry in outs],
        in_specs=in_specs,
        out_specs=out_specs,
        scratch_shapes=[pltpu.VMEM(*typed(entry)) for entry in scratch] + [dma((sends,)), dma((locals_,))] + [dma(entry) for entry in sems] + [pltpu.SemaphoreType.REGULAR((flags,))] * (flags > 0),
        compiler_params=pltpu.CompilerParams(collective_id=collective_id, has_side_effects=True, vmem_limit_bytes=vmem),
    )(*args)


def shards(dp, residual, seg_ids, attn_gain, w_qkv, w_out, ffn_gain, w_gate_up, w_down, cotangent):
    n = dp // 4
    rows, width = residual.shape
    group = seg_ids.shape[0]
    block, cols = w_qkv.shape[1:]
    part = w_gate_up.shape[2] // n
    pairs = jnp.arange(LANES, dtype=jnp.int32) % (HD // 2)
    freq = (ROPE_BASE ** (-(pairs.astype(F32) * 2.0 / HD)))[None]
    mib = 1024 * 1024

    first = call(
        functools.partial(attention_kernel, dp), 1, 192, 12, 60 * mib,
        [
            (4, width, cols), (3, width, part), (n, 2, rows, width), (n, 2, rows, width), (group, width),
            (group, cols), (3, group, cols), (rows, width, F32), (2, group, LANES, F32), (16, width, F32), (group, group, F32),
        ],
        [ANY] * 5 + [VM] * 6,
        [
            (4, width, cols), (group, 3 * cols, F32), (16, block, F32), (dp, 16, block, F32), (2, rows, LANES, F32),
            (rows, width), (group, width), (rows, width), (2, rows, width, F32), (rows, width), (rows, width),
            (1, block, cols), (block, n * part),
        ],
        [(dp,), (4, n), (4, n), (3, 4, n), (2, n), (2, n), (2,)],
    )
    (weights, ffn_weights, grad_all, normed_ffn, normed, attended, qkv, mixed, tables, all_gains, allowed) = first(
        [VM] * 8 + [ANY] * 2, residual, cotangent, seg_ids[None], attn_gain[None], ffn_gain[None], freq, w_out, w_down,
        w_qkv, w_gate_up,
    )
    every = n * 2 * rows
    slots = 3 * n
    second = call(
        functools.partial(ffn_kernel, dp), 2, 192, 64, 63 * mib,
        [(3, n, block, part), (4, 3, block, cols), (rows, width), (rows, width, F32), (16, block, F32)],
        [ANY] * 2 + [VM] * 3,
        [
            (4, width, part), (every, width), (every, part), (every, 2 * part),
            (n, 2, rows, width), (n, rows, width), (n + 1, rows, width),
            (slots, 2, 2, block, part), (slots, 2, block, part), (slots, block, part),
            (group, width), (rows, width), (8, width, F32), (8, width, F32),
            (dp, 16, block, F32), (dp, 16, block, F32), (2, 16, block, F32),
        ],
        [(n,), (n + 1,), (slots,), (slots,), (3, n), (4, n + 2), (3,), (dp,)],
        5,
    )
    result, totals, block_out, input_grad, gain_grads = second(
        [VM] * 5 + [ANY] * 7, mixed, residual, all_gains, allowed, tables, normed_ffn.reshape(every, width),
        grad_all.reshape(every, width), ffn_weights, normed, attended, qkv, weights,
    )
    qkv_grad, out_grad, gate_up_grad, down_grad, gain_sums = pl.pallas_call(
        finish_kernel,
        grid=(n,),
        out_shape=[
            jax.ShapeDtypeStruct(entry, F32)
            for entry in ((3, block, cols), (cols, block), (2, block, n * part), (n * part, block), (2, block))
        ],
        in_specs=[
            pl.BlockSpec((3, 1, block, part), lambda q: (0, q, 0, 0)),
            pl.BlockSpec((1, 3, block, cols), lambda q: (q, 0, 0, 0)),
            pl.BlockSpec((16, block), lambda q: (0, 0)),
        ],
        out_specs=[
            pl.BlockSpec((1, block, cols), lambda q: (jnp.minimum(q, 2), 0, 0)),
            pl.BlockSpec((cols, block), lambda q: (0, 0)),
            pl.BlockSpec((2, block, part), lambda q: (0, 0, q)),
            pl.BlockSpec((part, block), lambda q: (q, 0)),
            pl.BlockSpec((2, block), lambda q: (0, 0)),
        ],
        compiler_params=pltpu.CompilerParams(vmem_limit_bytes=32 * mib),
    )(result, totals, gain_grads)
    return block_out, input_grad, gain_sums[0], qkv_grad, out_grad, gain_sums[1], gate_up_grad, down_grad


def positions(segments):
    row_index = jnp.arange(segments.shape[1], dtype=jnp.int32)[None, :]
    previous = jnp.concatenate([segments[:, :1] - 1, segments[:, :-1]], axis=1)
    run_start = lax.cummax(jnp.where(segments != previous, row_index, 0), axis=1)
    return row_index - run_start


def rope_tables(places, head_dim):
    half_dim = head_dim // 2
    frequency = ROPE_BASE ** (-(jnp.arange(half_dim, dtype=jnp.float32) * 2.0 / head_dim))
    angles = places.astype(jnp.float32)[:, None, None] * frequency[None, None, :]
    return (jnp.cos(angles), jnp.sin(angles))


def rotate(field, cosine, sine_table):
    half_dim = field.shape[-1] // 2
    lower_half = field[..., :half_dim]
    upper_half = field[..., half_dim:]
    return jnp.concatenate(
        [
            lower_half * cosine - upper_half * sine_table,
            upper_half * cosine + lower_half * sine_table,
        ],
        axis=-1,
    )


def unrotate(field, cosine, sine_table):
    half_dim = field.shape[-1] // 2
    lower_half = field[..., :half_dim]
    upper_half = field[..., half_dim:]
    return jnp.concatenate(
        [
            lower_half * cosine + upper_half * sine_table,
            upper_half * cosine - lower_half * sine_table,
        ],
        axis=-1,
    )


def attention_scores(queries, key_rows, allowed):
    scores = jnp.einsum(
        "qhd,khd->hqk", queries, key_rows, preferred_element_type=jnp.float32
    ) * queries.shape[-1] ** (-0.5)
    return jnp.where(allowed[None], scores, -1e30)


def plain_shards(residual_in, seg_ids, attn_gain, w_qkv, w_out, ffn_gain, w_gate_up, w_down, cotangent):
    rows_local = residual_in.shape[0]
    group_rows = seg_ids.shape[0]
    offset = lax.axis_index("tensor") * rows_local
    live_rows = (lax.dynamic_slice_in_dim(seg_ids, offset, rows_local) >= 0).astype(jnp.float32)
    residual = residual_in.astype(jnp.float32)
    contract_rows = (((0,), (0,)), ((), ()))
    contract_cols = (((1,), (1,)), ((), ()))
    gain_attn, qkv_full, out_full = (
        lax.all_gather(attn_gain, "dp", axis=0, tiled=True),
        lax.all_gather(w_qkv, "dp", axis=1, tiled=True),
        lax.all_gather(w_out, "dp", axis=1, tiled=True),
    )
    norm_attn = lax.rsqrt(jnp.mean(residual * residual, axis=-1, keepdims=True) + EPSILON)
    unit_attn = residual * norm_attn
    normed = (unit_attn * gain_attn.astype(jnp.float32)).astype(jnp.bfloat16)
    normed_all = lax.all_gather(normed, "tensor", axis=0, tiled=True)
    projected = jnp.einsum("rd,cde->cre", normed_all, qkv_full, preferred_element_type=jnp.float32)
    head_count = qkv_full.shape[2] // HD
    head_shape = (group_rows, head_count, HD)
    cosine, sine_table = rope_tables(positions(seg_ids[None, :])[0], HD)
    queries = rotate(projected[0].reshape(head_shape), cosine, sine_table).astype(jnp.bfloat16)
    key_rows = rotate(projected[1].reshape(head_shape), cosine, sine_table).astype(jnp.bfloat16)
    value_rows = projected[2].reshape(head_shape).astype(jnp.bfloat16)
    row_index = jnp.arange(group_rows)
    allowed = (seg_ids[:, None] == seg_ids[None, :]) & (row_index[:, None] >= row_index[None, :])
    scores = attention_scores(queries, key_rows, allowed)
    row_top = jnp.max(scores, axis=-1, keepdims=True)
    log_total = row_top + jnp.log(jnp.sum(jnp.exp(scores - row_top), axis=-1, keepdims=True))
    weights = jnp.exp(scores - log_total).astype(jnp.bfloat16)
    attended = jnp.einsum("hqk,khd->qhd", weights, value_rows, preferred_element_type=jnp.float32)
    attended = attended.reshape(group_rows, head_count * HD).astype(jnp.bfloat16)
    mixed = residual + lax.psum_scatter(
        jnp.dot(attended, out_full, preferred_element_type=jnp.float32),
        "tensor",
        scatter_dimension=0,
        tiled=True,
    )
    gain_ffn, gate_up_full, down_full = (
        lax.all_gather(ffn_gain, "dp", axis=0, tiled=True),
        lax.all_gather(w_gate_up, "dp", axis=1, tiled=True),
        lax.all_gather(w_down, "dp", axis=1, tiled=True),
    )
    norm_ffn = lax.rsqrt(jnp.mean(mixed * mixed, axis=-1, keepdims=True) + EPSILON)
    unit_ffn = mixed * norm_ffn
    normed_ffn = (unit_ffn * gain_ffn.astype(jnp.float32)).astype(jnp.bfloat16)
    normed_ffn_all = lax.all_gather(normed_ffn, "tensor", axis=0, tiled=True)
    gate_up = jnp.einsum(
        "rd,cde->cre", normed_ffn_all, gate_up_full, preferred_element_type=jnp.float32
    )
    gate_pre = gate_up[0]
    up_pre = gate_up[1]
    sigmoid_gate = jax.nn.sigmoid(gate_pre)
    activated = gate_pre * sigmoid_gate
    hidden = (activated * up_pre).astype(jnp.bfloat16)
    output = mixed + lax.psum_scatter(
        jnp.dot(hidden, down_full, preferred_element_type=jnp.float32).astype(jnp.bfloat16),
        "tensor",
        scatter_dimension=0,
        tiled=True,
    ).astype(jnp.float32)
    grad_out = cotangent.astype(jnp.float32) * live_rows[:, None]
    grad_all = lax.all_gather(grad_out.astype(jnp.bfloat16), "tensor", axis=0, tiled=True)
    down_grad = lax.dot_general(hidden, grad_all, contract_rows, preferred_element_type=jnp.float32)
    hidden_grad = lax.dot_general(
        grad_all, down_full, contract_cols, preferred_element_type=jnp.float32
    )
    gate_grads = jnp.stack(
        [
            hidden_grad * up_pre * sigmoid_gate * (1.0 + gate_pre * (1.0 - sigmoid_gate)),
            hidden_grad * activated,
        ]
    ).astype(jnp.bfloat16)
    gate_up_grad = jnp.einsum(
        "rd,cre->cde", normed_ffn_all, gate_grads, preferred_element_type=jnp.float32
    )
    normed_ffn_grad = lax.psum_scatter(
        jnp.einsum("cre,cde->rd", gate_grads, gate_up_full, preferred_element_type=jnp.float32),
        "tensor",
        scatter_dimension=0,
        tiled=True,
    )
    ffn_gain_part = jnp.sum(normed_ffn_grad * unit_ffn, axis=0)
    scaled_ffn = normed_ffn_grad * gain_ffn.astype(jnp.float32)
    mixed_grad = grad_out + norm_ffn * (
        scaled_ffn - unit_ffn * jnp.mean(scaled_ffn * unit_ffn, axis=-1, keepdims=True)
    )
    mixed_all = lax.all_gather(mixed_grad.astype(jnp.bfloat16), "tensor", axis=0, tiled=True)
    out_grad = lax.dot_general(
        attended, mixed_all, contract_rows, preferred_element_type=jnp.float32
    )
    attended_grad = lax.dot_general(
        mixed_all, out_full, contract_cols, preferred_element_type=jnp.float32
    )
    attended_grad = attended_grad.astype(jnp.bfloat16).reshape(head_shape)
    probabilities = jnp.exp(attention_scores(queries, key_rows, allowed) - log_total)
    value_grad = jnp.einsum(
        "hqk,qhd->khd",
        probabilities.astype(jnp.bfloat16),
        attended_grad,
        preferred_element_type=jnp.float32,
    )
    prob_grad = jnp.einsum(
        "qhd,khd->hqk", attended_grad, value_rows, preferred_element_type=jnp.float32
    )
    score_grad = (
        probabilities * (prob_grad - jnp.sum(probabilities * prob_grad, axis=-1, keepdims=True))
    ).astype(jnp.bfloat16)
    scale_factor = HD ** (-0.5)
    query_grad = (
        jnp.einsum("hqk,khd->qhd", score_grad, key_rows, preferred_element_type=jnp.float32)
        * scale_factor
    )
    key_grad = (
        jnp.einsum("hqk,qhd->khd", score_grad, queries, preferred_element_type=jnp.float32)
        * scale_factor
    )
    qkv_grads = jnp.stack(
        [
            unrotate(query_grad, cosine, sine_table),
            unrotate(key_grad, cosine, sine_table),
            value_grad,
        ]
    )
    qkv_grads = qkv_grads.reshape(3, group_rows, head_count * HD).astype(jnp.bfloat16)
    qkv_grad = jnp.einsum("rd,cre->cde", normed_all, qkv_grads, preferred_element_type=jnp.float32)
    normed_grad = lax.psum_scatter(
        jnp.einsum("cre,cde->rd", qkv_grads, qkv_full, preferred_element_type=jnp.float32),
        "tensor",
        scatter_dimension=0,
        tiled=True,
    )
    attn_gain_part = jnp.sum(normed_grad * unit_attn, axis=0)
    scaled_attn = normed_grad * gain_attn.astype(jnp.float32)
    input_grad = mixed_grad + norm_attn * (
        scaled_attn - unit_attn * jnp.mean(scaled_attn * unit_attn, axis=-1, keepdims=True)
    )
    (
        query_total,
        key_total,
        value_total,
        out_total,
        attn_gain_total,
        gate_total,
        up_total,
        down_total,
        ffn_gain_total,
    ) = (
        lax.psum_scatter(qkv_grad[0], "dp", scatter_dimension=0, tiled=True),
        lax.psum_scatter(qkv_grad[1], "dp", scatter_dimension=0, tiled=True),
        lax.psum_scatter(qkv_grad[2], "dp", scatter_dimension=0, tiled=True),
        lax.psum_scatter(out_grad, "dp", scatter_dimension=1, tiled=True),
        lax.psum_scatter(attn_gain_part, "dp", scatter_dimension=0, tiled=True),
        lax.psum_scatter(gate_up_grad[0], "dp", scatter_dimension=0, tiled=True),
        lax.psum_scatter(gate_up_grad[1], "dp", scatter_dimension=0, tiled=True),
        lax.psum_scatter(down_grad, "dp", scatter_dimension=1, tiled=True),
        lax.psum_scatter(ffn_gain_part, "dp", scatter_dimension=0, tiled=True),
    )
    gate_up_total = jnp.stack([gate_total, up_total])
    qkv_total = jnp.stack([query_total, key_total, value_total])
    attn_gain_sum, ffn_gain_sum = lax.psum((attn_gain_total, ffn_gain_total), "tensor")
    return (
        output.astype(jnp.bfloat16),
        input_grad,
        attn_gain_sum,
        qkv_total,
        out_total,
        ffn_gain_sum,
        gate_up_total,
        down_total,
    )


def solution(mesh):
    in_specs = (
        P(("dp", "tensor"), None),
        P("dp"),
        P("dp"),
        P(None, "dp", "tensor"),
        P("tensor", "dp"),
        P("dp"),
        P(None, "dp", "tensor"),
        P("tensor", "dp"),
        P(("dp", "tensor"), None),
    )
    out_specs = (
        P(("dp", "tensor"), None),
        P(("dp", "tensor"), None),
        P("dp"),
        P(None, "dp", "tensor"),
        P("tensor", "dp"),
        P("dp"),
        P(None, "dp", "tensor"),
        P("tensor", "dp"),
    )
    dp = mesh.shape["dp"]
    local = functools.partial(shards, dp) if dp == 16 else plain_shards
    return jax.shard_map(local, mesh=mesh, in_specs=in_specs, out_specs=out_specs, check_vma=False)
```

```python
import functools

import jax
import jax.numpy as jnp
from jax import lax
from jax.experimental import pallas as pl
from jax.experimental.pallas import tpu as pltpu
from jax.sharding import PartitionSpec as P

HD = 64
EPSILON = 1e-05
ROPE_BASE = 130000.0
MESH = pl.DeviceIdType.MESH
ANY = pl.BlockSpec(memory_space=pl.ANY)
VM = pl.BlockSpec(memory_space=pltpu.VMEM)
F32 = jnp.float32
BF16 = jnp.bfloat16
LANES = 128
SLOTS = 9
LIMIT = 66977792
NT = (((1,), (1,)), ((), ()))
TN = (((0,), (0,)), ((), ()))
NN = (((1,), (0,)), ((), ()))


def dot(a, b, dims=NN):
    return lax.dot_general(a, b, dims, preferred_element_type=F32)


def when(cond, action):
    if cond is None:
        action()
    else:
        pl.when(cond)(action)


class Net:
    def __init__(self, dp, send_sems, local_sems):
        self.n = dp // 4
        self.dp_index = lax.axis_index("dp")
        self.x = lax.axis_index("tensor")
        self.z = self.dp_index // 4
        self.y = (self.dp_index // 2) % 2
        self.c = self.dp_index % 2
        self.send_sems = send_sems
        self.local_sems = local_sems
        self.sent = 0
        self.moved = 0
        self.pending = []
        self.kept = []
        self.tags = {}

    def place(self, z, y, c):
        return (z * 2 + y) * 2 + c

    def device(self, z=None, y=None, c=None, x=None):
        z = self.z if z is None else z
        y = self.y if y is None else y
        c = self.c if c is None else c
        x = self.x if x is None else x
        return (self.place(z, y, c), x)

    def greet(self, devices):
        barrier = pltpu.get_barrier_semaphore()
        for device in devices:
            pl.semaphore_signal(barrier, inc=1, device_id=device, device_id_type=MESH)
        pl.semaphore_wait(barrier, len(devices))

    def send(self, src, dst, recv_sem, device, cond=None):
        sem = self.send_sems.at[self.sent]
        self.sent += 1
        copy = pltpu.make_async_remote_copy(
            src_ref=src, dst_ref=dst, send_sem=sem, recv_sem=recv_sem, device_id=device, device_id_type=MESH
        )
        when(cond, copy.start)
        self.pending.append((cond, copy))
        return self.pending[-1]

    def recv(self, dst, recv_sem):
        pltpu.make_async_remote_copy(
            src_ref=dst, dst_ref=dst, send_sem=self.send_sems.at[0], recv_sem=recv_sem,
            device_id=self.device(c=1 - self.c), device_id_type=MESH,
        ).wait_recv()

    def local(self, src, dst, cond=None):
        sem = self.local_sems.at[self.moved]
        self.moved += 1
        copy = pltpu.make_async_copy(src, dst, sem)
        when(cond, copy.start)
        self.kept.append((cond, copy))
        return self.kept[-1]

    def settle(self, entry):
        for entries, wait in ((self.kept, "wait"), (self.pending, "wait_send")):
            for k, known in enumerate(entries):
                if known is entry:
                    when(entry[0], getattr(entry[1], wait))
                    del entries[k]
                    return

    def tag(self, name, entries):
        self.tags.setdefault(name, []).extend(entries)

    def settle_tag(self, *names):
        for name in names:
            for entry in self.tags.pop(name, ()):
                self.settle(entry)

    def drain(self):
        assert self.sent <= self.send_sems.shape[0] and self.moved <= self.local_sems.shape[0]
        for cond, copy in self.pending:
            when(cond, copy.wait_send)
        for cond, copy in self.kept:
            when(cond, copy.wait)


class Gather:
    def __init__(self, net, own, at, sems, tag):
        self.net, self.own, self.at, self.tag = net, own, at, tag
        self.sems = sems

    def spread(self, block, src, ysend=True):
        net = self.net
        here = net.place(block, net.y, net.c)
        net.tag(self.tag, [net.send(src, self.at(here), self.sems.at[1, block], net.device(y=1 - net.y))])
        net.tag(self.tag, [net.send(src, self.at(here), self.sems.at[2 + net.y, block], net.device(c=1 - net.c))])

    def start(self):
        net = self.net
        here = self.at(net.dp_index)
        net.tag(self.tag, [net.send(self.own, here, self.sems.at[0, net.z], net.device(z=net.z + 1), net.z < net.n - 1)])
        net.tag(self.tag, [net.send(self.own, here, self.sems.at[0, net.z], net.device(z=net.z - 1), net.z > 0)])
        self.spread(net.z, self.own)
        self.kept = net.local(self.own, here)

    def step(self, s):
        net = self.net
        for sign in (1, -1):
            block = net.z - s * sign
            valid = jnp.logical_and(block >= 0, block < net.n)
            nxt = net.z + sign
            more = jnp.logical_and(nxt >= 0, nxt < net.n)
            here = self.at(net.place(block, net.y, net.c))

            @pl.when(valid)
            def _():
                net.recv(here, self.sems.at[0, block])

            net.tag(self.tag, [net.send(here, here, self.sems.at[0, block], net.device(z=nxt), jnp.logical_and(valid, more))])
            net.tag(self.tag, [net.send(here, here, self.sems.at[1, block], net.device(y=1 - net.y), valid)])
            net.tag(self.tag, [net.send(here, here, self.sems.at[2 + net.y, block], net.device(c=1 - net.c), valid)])

    def cross(self, block):
        net = self.net
        there = self.at(net.place(block, 1 - net.y, net.c))
        net.recv(there, self.sems.at[1, block])
        net.tag(self.tag, [net.send(there, there, self.sems.at[3 - net.y, block], net.device(c=1 - net.c))])

    def cross_step(self, s):
        net = self.net
        if s == 0:
            self.cross(net.z)
            return
        for sign in (1, -1):
            block = net.z - s * sign
            valid = jnp.logical_and(block >= 0, block < net.n)
            there = self.at(net.place(block, 1 - net.y, net.c))

            @pl.when(valid)
            def _():
                net.recv(there, self.sems.at[1, block])

            net.tag(self.tag, [net.send(there, there, self.sems.at[3 - net.y, block], net.device(c=1 - net.c), valid)])

    def finish(self, block):
        net = self.net
        for y in (0, 1):
            net.recv(self.at(net.place(block, y, 1 - net.c)), self.sems.at[2 + y, block])


class Exchange:
    def __init__(self, net, part, at, sems, tag):
        self.net, self.part, self.at, self.tag = net, part, at, tag
        self.sems = sems

    def start(self):
        net = self.net
        here = self.at(net.dp_index)
        for d in list(range(1, net.n)):
            to = (net.z + d) % net.n
            net.tag(self.tag, [net.send(self.part(to), here, self.sems.at[0, net.z], net.device(z=to))])
        own = self.part(net.z)
        net.tag(self.tag, [net.send(own, here, self.sems.at[1, net.z], net.device(y=1 - net.y))])
        net.tag(self.tag, [net.send(own, here, self.sems.at[2 + net.y, net.z], net.device(c=1 - net.c))])
        self.kept = net.local(own, here)

    def step(self, block):
        net = self.net
        here = self.at(net.place(block, net.y, net.c))
        net.recv(here, self.sems.at[0, block])
        net.send(here, here, self.sems.at[1, block], net.device(y=1 - net.y))
        net.send(here, here, self.sems.at[2 + net.y, block], net.device(c=1 - net.c))

    def cross(self, block):
        net = self.net
        there = self.at(net.place(block, 1 - net.y, net.c))
        net.recv(there, self.sems.at[1, block])
        net.send(there, there, self.sems.at[3 - net.y, block], net.device(c=1 - net.c))

    finish = Gather.finish


class Rows:
    def __init__(self, net, own, at, sems, tag):
        self.net, self.own, self.at, self.tag = net, own, at, tag
        self.sems = sems

    def start(self):
        net = self.net
        here = self.at(net.z, net.x)
        own = here if self.own is None else self.own
        net.tag(self.tag, [net.send(own, here, self.sems.at[0, net.z], net.device(z=net.z + 1), net.z < net.n - 1)])
        net.tag(self.tag, [net.send(own, here, self.sems.at[0, net.z], net.device(z=net.z - 1), net.z > 0)])
        net.tag(self.tag, [net.send(own, here, self.sems.at[1, net.z], net.device(x=1 - net.x))])
        if self.own is not None:
            net.tag(self.tag + "_kept", [net.local(own, here)])

    def step(self, s):
        net = self.net
        forwarded = []
        for sign in (1, -1):
            block = net.z - s * sign
            valid = jnp.logical_and(block >= 0, block < net.n)
            nxt = net.z + sign
            more = jnp.logical_and(nxt >= 0, nxt < net.n)
            here = self.at(block, net.x)

            @pl.when(valid)
            def _():
                net.recv(here, self.sems.at[0, block])

            forwarded.append(net.send(here, here, self.sems.at[0, block], net.device(z=nxt), jnp.logical_and(valid, more)))
            forwarded.append(net.send(here, here, self.sems.at[1, block], net.device(x=1 - net.x), valid))
        if self.own is None:
            net.tag(self.tag, forwarded)

    def finish(self, block):
        net = self.net
        net.recv(self.at(block, 1 - net.x), self.sems.at[1, block])


class Reduce:
    def __init__(self, net, part, from_c, from_y, result, line, sems, total):
        self.net, self.part, self.from_c, self.from_y = net, part, from_c, from_y
        self.result, self.totals = result
        self.line = line
        self.cs, self.ys, self.zs, self.ls, self.free = sems
        self.slots = part.shape[0]
        self.total = total
        self.items = []
        self.out = {}
        self.done_c = self.done_y = self.done_z = 0

    def add(self, total, term):
        def body(r):
            span = pl.ds(r, 16)
            total[span] = (total[span].astype(F32) + term[span].astype(F32)).astype(BF16)

        loop(total.shape[0], 16, body)

    def credit(self, which, device):
        pl.semaphore_signal(self.free.at[which], inc=1, device_id=device, device_id_type=MESH)

    def item(self, matrix, to, left, right, depth, block):
        net = self.net
        i = len(self.items)
        slot = i % self.slots
        self.items.append((matrix, to))
        assert self.done_z > i - self.slots
        for entry in self.out.pop(i - self.slots, ()):
            net.settle(entry)

        def body(col):
            term = dot(left, right[:, pl.ds(col, 256)], TN).astype(BF16)
            for y in (0, 1):
                for c in (0, 1):
                    at = (y * 2 + c) * block
                    self.part[slot, c, y, :, pl.ds(col, 256)] = term[at : at + block]

        loop(right.shape[1], 256, body)
        if i >= self.slots:
            pl.semaphore_wait(self.free.at[0], 1)
        self.out[i] = [
            net.send(self.part.at[slot, 1 - net.c], self.from_c.at[slot], self.cs.at[slot], net.device(c=1 - net.c))
        ]

    def step_c(self):
        net = self.net
        i = self.done_c
        self.done_c += 1
        slot = i % self.slots
        net.recv(self.from_c.at[slot], self.cs.at[slot])
        for y in (0, 1):
            self.add(self.part.at[slot, net.c, y], self.from_c.at[slot, y])
        if i + self.slots < self.total:
            self.credit(0, net.device(c=1 - net.c))
        if i >= self.slots:
            pl.semaphore_wait(self.free.at[1], 1)
        self.out[i].append(
            net.send(self.part.at[slot, net.c, 1 - net.y], self.from_y.at[slot], self.ys.at[slot], net.device(y=1 - net.y))
        )

    def step_y(self):
        net = self.net
        i = self.done_y
        self.done_y += 1
        slot = i % self.slots
        matrix, to = self.items[i]
        net.recv(self.from_y.at[slot], self.ys.at[slot])
        self.add(self.part.at[slot, net.c, net.y], self.from_y.at[slot])
        if i + self.slots < self.total:
            self.credit(1, net.device(y=1 - net.y))
        matrices = self.result.shape[0]
        if matrix >= matrices:
            return
        src = self.part.at[slot, net.c, net.y]
        dst = self.result.at[matrix, net.z]
        away = to != net.z
        self.out[i].append(net.send(src, dst, self.zs.at[matrix, net.z], net.device(z=to), away))
        self.out[i].append(net.local(src, dst, jnp.logical_not(away)))
        self.done_z += 1

    def step_z(self):
        net = self.net
        i = self.done_z
        self.done_z += 1
        assert i < self.done_y
        matrix, to = self.items[i]
        m = matrix - self.result.shape[0]
        total = self.part.at[i % self.slots, net.c, net.y]
        behind = jnp.where(to > net.z, net.z > 0, net.z < net.n - 1)
        place = self.line(m, to)

        @pl.when(jnp.logical_and(to != net.z, behind))
        def _():
            net.recv(place, self.ls.at[m, to])
            self.add(total, place)

        side = jnp.where(to > net.z, 0, 1)
        nxt = jnp.where(to > net.z, net.z + 1, net.z - 1)
        there = net.device(z=nxt)
        last = jnp.logical_and(to != net.z, to == nxt)
        self.out[i].append(net.send(total, place, self.ls.at[m, to], there, jnp.logical_and(to != net.z, to != nxt)))
        self.out[i].append(net.send(total, self.totals.at[m, side], self.ls.at[m, net.n + side], there, last))
        self.out[i].append(net.local(total, self.totals.at[m, 2], to == net.z))

    def finish(self):
        net = self.net
        for matrix in range(self.result.shape[0]):
            for d in range(1, net.n):
                block = (net.z + d) % net.n
                net.recv(self.result.at[matrix, block], self.zs.at[matrix, block])
        for m in range(self.totals.shape[0]):
            for side, cond in ((0, net.z > 0), (1, net.z < net.n - 1)):

                @pl.when(cond)
                def _():
                    net.recv(self.totals.at[m, side], self.ls.at[m, net.n + side])


def loop(total, step, body):
    @pl.loop(0, total // step)
    def _(i):
        body(pl.multiple_of(i * step, step))


def turn(field, cosine, sine, lane):
    half = HD // 2
    partner = jnp.where(lane % HD < half, pltpu.roll(field, LANES - half, 1), pltpu.roll(field, half, 1))
    return field * cosine + partner * sine


def head_masks():
    lane = lax.broadcasted_iota(jnp.int32, (1, LANES), 1)
    return (lane < HD).astype(BF16), (lane >= HD).astype(BF16)


def both(field, masks):
    return jnp.concatenate([field * masks[0], field * masks[1]], axis=0)


def pick(stacked, rows):
    lane = lax.broadcasted_iota(jnp.int32, (1, LANES), 1)
    return jnp.where(lane < HD, stacked[:rows], stacked[rows:])


def softmax(queries2, key_rows, allowed):
    scores = dot(queries2, key_rows, NT) * HD ** (-0.5)
    scores = jnp.where(allowed > 0, scores, -1e30)
    raised = jnp.exp(scores - jnp.max(scores, axis=-1, keepdims=True))
    return raised / jnp.sum(raised, axis=-1, keepdims=True)


def far_first(net):
    n = net.n
    table = [sorted(range(n), key=lambda b: (-abs(b - z), -b)) for z in range(n)]
    return [sum(jnp.where(net.z == z, table[z][k], 0) for z in range(n)) for k in range(n)]


class RowSum:
    def __init__(self, net, order, part, from_x, from_z, sems):
        self.net, self.order, self.part, self.from_x, self.from_z = net, order, part, from_x, from_z
        self.xs, self.zs = sems
        self.sent = []
        self.done_x = self.done_z = 0

    def start(self, b):
        net = self.net
        self.sent.append(
            net.send(self.part(b, 1 - net.x), self.from_x.at[b], self.xs.at[b], net.device(x=1 - net.x))
        )

    def add(self, total, term):
        def body(r):
            span = pl.ds(r, 16)
            total[span] = (total[span].astype(F32) + term[span].astype(F32)).astype(BF16)

        loop(total.shape[0], 16, body)

    def step_x(self, k):
        net = self.net
        b = self.order[k]
        self.done_x += 1
        net.recv(self.from_x.at[b], self.xs.at[b])
        self.add(self.part(b, net.x), self.from_x.at[b])

    def step_z(self, k):
        net = self.net
        b = self.order[k]
        self.done_z += 1
        total = self.part(b, net.x)
        behind = jnp.where(b > net.z, net.z > 0, net.z < net.n - 1)

        @pl.when(jnp.logical_and(b != net.z, behind))
        def _():
            net.recv(self.from_z.at[b], self.zs.at[b])
            self.add(total, self.from_z.at[b])

        slot = jnp.where(b == net.z - 1, net.n, b)
        to = jnp.where(b > net.z, net.z + 1, net.z - 1)
        self.sent.append(net.send(total, self.from_z.at[slot], self.zs.at[slot], net.device(z=to), b != net.z))

    def finish(self):
        net = self.net
        total = self.part(net.z, net.x)
        for slot, cond in ((net.z, net.z > 0), (net.n, net.z < net.n - 1)):

            @pl.when(cond)
            def _():
                net.recv(self.from_z.at[slot], self.zs.at[slot])
                self.add(total, self.from_z.at[slot])


def norm_back(grad, value, gain):
    scale = lax.rsqrt(jnp.mean(value * value, axis=-1, keepdims=True) + EPSILON)
    unit = value * scale
    scaled = grad * gain
    back = scale * (scaled - unit * jnp.mean(scaled * unit, axis=-1, keepdims=True))
    return back, grad * unit


def layer_kernel(
    dp,
    residual, seg, attn_gain, ffn_gain, freq, w_out, w_down, w_qkv, w_gate_up, cotangent,
    result, totals, wa_out, wf_out, normed_ffn_out, normed_out, attended_out, qkv_out, block_out, input_grad, gain_out,
    weights, grad, hidden, gate_up_grad, back, back_x, back_z, part, from_c, from_y,
    mixed_all, from_x, pre, mixed, tables, allowed, gains, all_gains, gains_all, gain_sum, ffn_sum, gain_to,
    gain_from, gain_x,
    send_sems, local_sems, gain_sems, q_sems, o_sems, f_sems, g_sems, n_sems, x_sems,
    bx_sems, bz_sems, rc_sems, ry_sems, rz_sems, rl_sems, back_gain_sems, free,
):
    net = Net(dp, send_sems, local_sems)
    n, me, x = net.n, net.dp_index, net.x
    rows, width = residual.shape
    block, cols = w_qkv.shape[1:]
    group = pair = 2 * rows
    every = grad.shape[0]
    depth = width // n
    assert w_gate_up.shape[2] == n * cols and width == 2 * cols and width == 2 * every and width == dp * block
    lane = lax.broadcasted_iota(jnp.int32, (group, LANES), 1)
    live = gain_to
    assert gain_to.shape == (group // 16, 16, LANES)
    order = far_first(net)
    beside = jnp.where(net.z > 0, 1, 0) + jnp.where(net.z < n - 1, 1, 0)
    net.greet([((me + k) % dp, x) for k in range(1, dp)] + [(me, 1 - x)])

    def block_rows_of(z, half):
        return pl.ds(pl.multiple_of((z * 2 + half) * rows, rows), rows)

    normed_all = back.at[0]
    ffn_own, to_x = back.at[1, 0], back.at[1, 1]
    down_own = hidden.at[pl.ds(0, n * block)]
    out_own = hidden.at[pl.ds(n * block, block)]
    early_qkv = [
        gate_up_grad.at[pl.ds(0, group), pl.ds(0, cols)],
        gate_up_grad.at[pl.ds(0, group), pl.ds(cols, cols)],
        gate_up_grad.at[pl.ds(group, group), pl.ds(0, cols)],
    ]
    early_attended = gate_up_grad.at[pl.ds(group, group), pl.ds(cols, cols)]

    def at_weights(first, count):
        return lambda index: weights.at[pl.ds(first, count), pl.ds(pl.multiple_of(index * block, block), block)]

    def at_out(index):
        return weights.at[3, pl.ds(pl.multiple_of(index * block, block), block)]

    def ffn_part(m):
        def own(to):
            if m == 2:
                return down_own.at[pl.ds(pl.multiple_of(to * block, block), block)]
            return w_gate_up.at[m, :, pl.ds(pl.multiple_of(to * cols, cols), cols)]

        return own

    def ffn_place(m):
        return lambda index: wf_out.at[m, pl.ds(pl.multiple_of(index * block, block), block)]

    qkv = Gather(net, w_qkv, at_weights(0, 3), q_sems, "qkv")
    out = Gather(net, out_own, at_out, o_sems, "out")
    ffn = [Exchange(net, ffn_part(m), ffn_place(m), f_sems.at[m], "ffn") for m in range(3)]
    grads = Rows(net, None, lambda z, half: grad.at[block_rows_of(z, half)], g_sems, "grads")
    ffn_rows = Rows(net, ffn_own, lambda z, half: normed_ffn_out.at[z, half], n_sems, "rows")
    load_grad = net.local(cotangent, grad.at[block_rows_of(net.z, x)])

    def send_gains():
        gains[0:8] = jnp.broadcast_to(attn_gain[...].astype(F32), (8, block))
        gains[8:16] = jnp.broadcast_to(ffn_gain[...].astype(F32), (8, block))
        for k in range(1, dp):
            net.send(gains, all_gains.at[me], gain_sems.at[me], ((me + k) % dp, x))
        all_gains[me] = gains[...]

    def turn_weights():
        out_own[...] = w_out[...].T
        for q in range(n):
            down_own[q * block : (q + 1) * block] = w_down[q * cols : (q + 1) * cols].T

    def mask_grads():
        seg_rows = jnp.broadcast_to(seg[...].astype(F32), (LANES, group))
        seg_cols = seg_rows.T
        alive = (seg_cols >= 0).astype(F32)
        for i in range(group // 16):
            live[i] = alive[i * 16 : (i + 1) * 16]
        row_id = lax.broadcasted_iota(jnp.int32, (group, group), 0)
        col_id = lax.broadcasted_iota(jnp.int32, (group, group), 1)
        same = jnp.concatenate([seg_cols] * (group // LANES), axis=1) == jnp.concatenate([seg_rows] * (group // LANES), axis=0)
        mask = jnp.logical_and(same, row_id >= col_id).astype(F32)
        allowed[...] = mask
        angles = (jnp.sum(mask, axis=1, keepdims=True) - 1.0) * freq[...]
        tables[0] = jnp.cos(angles)
        tables[1] = jnp.where(lane % HD < HD // 2, -jnp.sin(angles), jnp.sin(angles))

        net.settle(load_grad)

        def body(r):
            span = pl.ds(pl.multiple_of((net.z * 2 + x) * rows + r, 16), 16)
            grad[span] = (grad[span].astype(F32) * live[(x * rows + r) // 16, :, 0:1]).astype(BF16)

        loop(rows, 16, body)

    def norm():
        for k in range(1, dp):
            source = (me + k) % dp
            net.recv(all_gains.at[source], gain_sems.at[source])
        for i in range(dp):
            gains_all[:, i * block : (i + 1) * block] = all_gains[i]

        def body(r):
            value = residual[pl.ds(r, 16)].astype(F32)
            unit = value * lax.rsqrt(jnp.mean(value * value, axis=-1, keepdims=True) + EPSILON)
            normed_all[x, pl.ds(r, 16)] = (unit * gains_all[0:1]).astype(BF16)

        loop(rows, 16, body)
        net.tag("normed", [net.send(normed_all.at[x], normed_all.at[x], x_sems.at[0], net.device(x=1 - x))])

    def project(k):
        if k == 0:
            net.recv(normed_all.at[1 - x], x_sems.at[0])
            net.settle(qkv.kept)
            net.tag("normed", [net.local(normed_all.at[half], normed_out.at[pl.ds(half * rows, rows)]) for half in (0, 1)])
        b = (net.z + k) % n
        qkv.finish(b)
        base = pl.multiple_of(b * depth, depth)

        def body(col):
            left = jnp.concatenate([normed_all[0, :, pl.ds(base, depth)], normed_all[1, :, pl.ds(base, depth)]], axis=0)
            for m in range(3):
                term = dot(left, weights[m, pl.ds(base, depth), pl.ds(col, 256)])
                to = pl.ds(pl.multiple_of(m * cols + col, 256), 256)
                pre[:, to] = term if k == 0 else pre[:, to] + term

        loop(cols, 256, body)
        if k == n - 1:
            net.tag("save", [net.local(weights.at[pl.ds(0, 3)], wa_out.at[pl.ds(0, 3)])])

    def attend():
        masks = head_masks()

        def body(col):
            cosine, sine = tables[0], tables[1]
            queries = turn(pre[:, pl.ds(col, LANES)], cosine, sine, lane).astype(BF16)
            key_rows = turn(pre[:, pl.ds(pl.multiple_of(cols + col, LANES), LANES)], cosine, sine, lane).astype(BF16)
            value_rows = pre[:, pl.ds(pl.multiple_of(2 * cols + col, LANES), LANES)].astype(BF16)
            early_qkv[0][:, pl.ds(col, LANES)] = queries
            early_qkv[1][:, pl.ds(col, LANES)] = key_rows
            early_qkv[2][:, pl.ds(col, LANES)] = value_rows
            may = jnp.concatenate([allowed[...], allowed[...]], axis=0)
            probs = softmax(both(queries, masks), key_rows, may).astype(BF16)
            early_attended[:, pl.ds(col, LANES)] = pick(dot(probs, value_rows), group).astype(BF16)

        loop(cols, LANES, body)
        net.tag("early", [net.local(early_qkv[m], qkv_out.at[m]) for m in range(3)])
        net.tag("early", [net.local(early_attended, attended_out)])

    def join():
        for k in range(n):
            out.finish((net.z + k) % n)
        net.settle(out.kept)
        net.tag("save_out", [net.local(weights.at[3], wa_out.at[3])])

        def body(col):
            span = pl.ds(col, 256)
            term = dot(early_attended[...], weights[3, span, :], NT)
            low, high = term[:rows], term[rows:]
            input_grad[:, span] = jnp.where(x == 0, low, high)
            to_x[:, span] = jnp.where(x == 0, high, low).astype(BF16)

        loop(width, 256, body)
        net.tag("to_x", [net.send(to_x, from_x, x_sems.at[1], net.device(x=1 - x))])

    def mix():
        net.recv(from_x, x_sems.at[1])

        def body(r):
            span = pl.ds(r, 16)
            value = residual[span].astype(F32) + input_grad[span] + from_x[span].astype(F32)
            mixed[span] = value
            unit = value * lax.rsqrt(jnp.mean(value * value, axis=-1, keepdims=True) + EPSILON)
            ffn_own[span] = (unit * gains_all[8:9]).astype(BF16)

        loop(rows, 16, body)

    def load_ffn(m):
        for k in range(n):
            ffn[m].finish((net.z + k) % n)
        net.settle(ffn[m].kept)
        net.settle_tag("qkv", "save")
        net.tag("weights", [net.local(wf_out.at[m], weights.at[m])])

    def load_rows(k):
        net.settle_tag("out", "save_out", "rows_kept")
        b = order[k]
        ffn_rows.finish(b)
        for x_half in (0, 1):
            for half in (0, 1):
                there = pl.ds(pl.multiple_of(half * every + (b * 2 + x_half) * rows, rows), rows)
                src = normed_ffn_out.at[b, x_half, :, pl.ds(half * cols, cols)]
                net.tag("load%d" % k, [net.local(src, weights.at[3, there])])

    def ffn_step(m, k):
        ffn[m].step((net.z + k) % n)

    def ffn_cross(m):
        for k in range(n):
            ffn[m].cross((net.z + k) % n)


    def features(half):
        return weights.at[3, pl.ds(half * every, every)]

    gate_grad, up_grad = gate_up_grad.at[:, pl.ds(0, cols)], gate_up_grad.at[:, pl.ds(cols, cols)]
    add = gate_up_grad
    backs = RowSum(net, order, lambda b, half: back.at[b, half], back_x, back_z, (bx_sems, bz_sems))
    adds = RowSum(
        net, order, lambda b, half: add.at[pl.ds(pl.multiple_of((b * 2 + half) * rows, rows), rows)],
        back_x, back_z, (bx_sems, bz_sems),
    )
    red = Reduce(
        net, part, from_c, from_y, (result, totals),
        lambda m, to: weights.at[3, pl.ds(pl.multiple_of((m * n + to) * block, block), block)],
        (rc_sems, ry_sems, rz_sems, rl_sems, free), 7 * n,
    )
    def rows_of(b):
        return pl.ds(pl.multiple_of(b * pair, pair), pair)

    def forward(k):
        net.settle_tag("load%d" % k, "weights", "ffn", "early")
        grads.finish(order[k])
        here = rows_of(order[k])

        def body(col):
            span = pl.ds(col, 256)

            def project(m):
                return dot(features(0)[here], weights[m, pl.ds(0, cols), span]) + dot(
                    features(1)[here], weights[m, pl.ds(cols, cols), span]
                )

            gate, up = project(0), project(1)
            hidden_grad = dot(grad[here], weights[2, :, span])
            sigmoid = 1.0 / (1.0 + jnp.exp(-gate))
            active = gate * sigmoid
            hidden[here, span] = (active * up).astype(BF16)
            gate_grad[here, span] = (hidden_grad * up * sigmoid * (1.0 + gate * (1.0 - sigmoid))).astype(BF16)
            up_grad[here, span] = (hidden_grad * active).astype(BF16)

        loop(cols, 256, body)

    def backward(k):
        net.settle_tag("normed", "to_x", "rows")
        b = order[k]
        here = rows_of(b)

        def body(col):
            span = pl.ds(col, 256)
            term = dot(gate_grad[here], weights[0, span, :], NT) + dot(up_grad[here], weights[1, span, :], NT)
            term = term.astype(BF16)
            back[b, 0, :, span] = term[:rows]
            back[b, 1, :, span] = term[rows:]

        loop(width, 256, body)
        backs.start(b)

    def add_chunk(k):
        here = rows_of(order[k])

        def body(col):
            span = pl.ds(col, 256)
            add[here, span] = dot(hidden[here], weights[2, span, :], NT).astype(BF16)

        loop(width, 256, body)
        if k == 0:
            pl.semaphore_wait(free.at[2], 1)
        adds.start(order[k])

    ffn_items = [(2, k) for k in range(n)] + [(m, k) for k in range(n) for m in (0, 1)]
    attention_items = [(3, k) for k in range(n)] + [(m, k) for k in range(n) for m in range(3)]

    def ffn_item():
        m, k = ffn_items[len(red.items)]
        b = order[k]
        base = b * depth
        if m == 2:
            left = grad[:, pl.ds(pl.multiple_of(base, depth), depth)]
        else:
            row = pl.ds(pl.multiple_of(base // cols * every, every), every)
            left = weights[3, row, pl.ds(pl.multiple_of(base % cols, depth), depth)]
        red.item(m, b, left, (gate_grad, up_grad, hidden)[m], depth, block)

    def attention_item():
        m, k = attention_items[len(red.items) - len(ffn_items)]
        base = pl.ds(pl.multiple_of(order[k] * depth, depth), depth)
        left, right = (mixed_all, attended) if m == 3 else (normed, grads_of[m])
        red.item(3 + m, order[k], left[:, base], right, depth, block)

    queries_of, keys_of, values_of = [hidden.at[pl.ds(m * pair, pair)] for m in range(3)]
    attended = hidden.at[pl.ds(3 * pair, pair)]
    normed = grad.at[pl.ds(0, pair)]
    grads_of = [
        grad.at[pl.ds(2 * pair, pair), pl.ds(0, cols)],
        grad.at[pl.ds(2 * pair, pair), pl.ds(cols, cols)],
        grad.at[pl.ds(3 * pair, pair), pl.ds(0, cols)],
    ]
    attended_grad = grad.at[pl.ds(3 * pair, pair), pl.ds(cols, cols)]
    own_rows = mixed_all.at[pl.ds(pl.multiple_of(x * rows, rows), rows)]
    other_rows = mixed_all.at[pl.ds(pl.multiple_of((1 - x) * rows, rows), rows)]
    late = {}

    def tell_beside(which):
        for cond, z in ((net.z > 0, net.z - 1), (net.z < n - 1, net.z + 1)):

            @pl.when(cond)
            def _():
                pl.semaphore_signal(free.at[which], inc=1, device_id=net.device(z=z), device_id_type=MESH)

    def mix_grads():
        backs.finish()
        ffn_sum[...] = jnp.zeros_like(ffn_sum)

        def body(r):
            span = pl.ds(r, 16)
            own = pl.ds(pl.multiple_of((net.z * 2 + x) * rows + r, 16), 16)
            term, gain_term = norm_back(back[net.z, x, span].astype(F32), mixed[span], gains_all[8:9])
            value = grad[own].astype(F32) + term
            input_grad[span] = value
            mixed_all[pl.ds(pl.multiple_of(x * rows + r, 16), 16)] = value.astype(BF16)
            ffn_sum[...] += gain_term[:8] + gain_term[8:]

        loop(rows, 16, body)
        net.send(own_rows, own_rows, x_sems.at[2], net.device(x=1 - x))
        pl.semaphore_signal(free.at[2], inc=1, device_id=net.device(x=1 - x), device_id_type=MESH)
        tell_beside(3)

    def load_out():
        late["out"] = net.local(wa_out.at[3], weights.at[3])

    def load_rest():
        net.settle_tag("grads")
        late["normed"] = net.local(normed_out, normed)
        late["qkv"] = net.local(wa_out.at[pl.ds(0, 3)], weights.at[pl.ds(0, 3)])
        late["parts"] = [net.local(qkv_out.at[m], hidden.at[pl.ds(m * pair, pair)]) for m in range(3)]
        late["attended"] = net.local(attended_out, attended)

    def step_adds():
        if adds.done_z == 0:
            pl.semaphore_wait(free.at[3], beside)
        adds.step_z(adds.done_z)

    def attended_back():
        net.settle(late["out"])
        net.recv(other_rows, x_sems.at[2])

        def body(col):
            span = pl.ds(col, 256)
            attended_grad[:, span] = dot(mixed_all[...], weights[3, :, span]).astype(BF16)

        loop(cols, 256, body)
        tell_beside(4)
        net.settle(late["attended"])

    def heads():
        for load in late["parts"]:
            net.settle(load)
        masks = head_masks()

        def body(col):
            span = pl.ds(col, LANES)
            cosine, sine = tables[0], tables[1]
            queries, key_rows, value_rows = queries_of[:, span], keys_of[:, span], values_of[:, span]
            out_grad = attended_grad[:, span]
            queries2, out_grad2 = both(queries, masks), both(out_grad, masks)
            may = jnp.concatenate([allowed[...], allowed[...]], axis=0)
            probs = softmax(queries2, key_rows, may)
            value_grad = dot(probs.astype(BF16), out_grad2, TN)
            prob_grad = dot(out_grad2, value_rows, NT)
            score_grad = probs * (prob_grad - jnp.sum(probs * prob_grad, axis=-1, keepdims=True))
            score_grad = score_grad.astype(BF16)
            query_grad = pick(dot(score_grad, key_rows), pair) * HD ** (-0.5)
            key_grad = dot(score_grad, queries2, TN) * HD ** (-0.5)
            grads_of[0][:, span] = turn(query_grad, cosine, -sine, lane).astype(BF16)
            grads_of[1][:, span] = turn(key_grad, cosine, -sine, lane).astype(BF16)
            grads_of[2][:, span] = value_grad.astype(BF16)

        loop(cols, LANES, body)
        net.settle(late["normed"])

    def normed_back():
        net.settle(late["qkv"])
        for entry in backs.sent:
            net.settle(entry)

        def body(col):
            span = pl.ds(col, 256)
            term = dot(grads_of[0][...], weights[0, span, :], NT)
            term += dot(grads_of[1][...], weights[1, span, :], NT)
            term += dot(grads_of[2][...], weights[2, span, :], NT)
            back[0, 0, :, span] = term[:rows].astype(BF16)
            back[0, 1, :, span] = term[rows:].astype(BF16)

        loop(width, 256, body)
        net.send(back.at[0, 1 - x], from_x, x_sems.at[3], net.device(x=1 - x))

    def input_back():
        net.recv(from_x, x_sems.at[3])
        gain_sum[...] = jnp.zeros_like(gain_sum)

        def body(r):
            span = pl.ds(r, 16)
            grad_rows = back[0, x, span].astype(F32) + from_x[span].astype(F32)
            term, gain_term = norm_back(grad_rows, residual[span].astype(F32), gains_all[0:1])
            input_grad[span] += term
            gain_sum[...] += gain_term[:8] + gain_term[8:]

        loop(rows, 16, body)
        for i in range(dp):
            gain_to[i, 0:8] = gain_sum[:, i * block : (i + 1) * block]
            gain_to[i, 8:16] = ffn_sum[:, i * block : (i + 1) * block]
        for k in range(1, dp):
            to = (me + k) % dp
            net.send(gain_to.at[to], gain_from.at[me], back_gain_sems.at[me], (to, x))

    def sum_gains():
        total = gain_to[me]
        for k in range(1, dp):
            source = (me + k) % dp
            net.recv(gain_from.at[source], back_gain_sems.at[source])
            total = total + gain_from[source]
        gain_x[0] = total
        net.send(gain_x.at[0], gain_x.at[1], x_sems.at[4], net.device(x=1 - x))

    def block_rows():
        adds.finish()

        def body(r):
            span = pl.ds(r, 16)
            block_out[span] = (mixed[span] + adds.part(net.z, x)[span].astype(F32)).astype(BF16)

        loop(rows, 16, body)

    qkv.start()
    turn_weights()
    out.start()
    send_gains()
    qkv.step(1)
    out.step(1)
    qkv.step(2)
    qkv.cross_step(0)
    out.cross_step(0)
    ffn[0].start()
    mask_grads()
    out.step(2)
    norm()
    grads.start()
    ffn[2].start()
    qkv.cross_step(1)
    qkv.step(3)
    qkv.cross_step(2)
    ffn_step(0, 3)
    out.cross_step(1)
    out.step(3)
    ffn_step(0, 2)
    qkv.cross_step(3)
    project(0)
    ffn_step(0, 1)
    grads.step(1)
    project(1)
    project(2)
    out.cross_step(2)
    project(3)
    ffn[1].start()
    attend()
    out.cross_step(3)
    join()
    mix()
    ffn_rows.start()
    grads.step(2)
    ffn_step(2, 1)
    ffn_step(2, 3)
    ffn_step(1, 1)
    ffn_step(1, 3)
    ffn_step(1, 2)
    ffn_step(2, 2)
    ffn_rows.step(1)
    load_rows(3)
    ffn_cross(1)
    ffn_cross(0)
    grads.step(3)
    ffn_cross(2)
    load_ffn(0)
    load_ffn(2)
    load_rows(2)
    ffn_rows.step(2)
    load_ffn(1)
    forward(3)
    forward(2)
    ffn_rows.step(3)
    load_rows(1)
    forward(1)
    backward(2)
    load_rows(0)
    forward(0)
    ffn_item()
    backward(0)
    red.step_c()
    backward(1)
    ffn_item()
    red.step_y()
    backs.step_x(2)
    ffn_item()
    red.step_c()
    backs.step_x(0)
    backs.step_z(0)
    red.step_c()
    ffn_item()
    ffn_item()
    backward(3)
    red.step_c()
    backs.step_x(1)
    backs.step_z(1)
    backs.step_z(2)
    red.step_c()
    ffn_item()
    ffn_item()
    red.step_y()
    red.step_y()
    red.step_c()
    red.step_c()
    ffn_item()
    ffn_item()
    red.step_c()
    backs.step_x(3)
    red.step_y()
    ffn_item()
    red.step_y()
    mix_grads()
    red.step_c()
    red.step_c()
    for _ in range(3):
        red.step_y()
    ffn_item()
    ffn_item()
    red.step_y()
    add_chunk(0)
    add_chunk(1)
    red.step_c()
    add_chunk(2)
    load_out()
    add_chunk(3)
    load_rest()
    red.step_y()
    attended_back()
    heads()
    red.step_c()
    attention_item()
    adds.step_x(adds.done_x)
    red.step_y()
    red.step_c()
    step_adds()
    attention_item()
    red.step_c()
    attention_item()
    adds.step_x(adds.done_x)
    for _ in range(3):
        attention_item()
    red.step_c()
    red.step_y()
    attention_item()
    red.step_c()
    attention_item()
    pl.semaphore_wait(free.at[4], beside)
    step_adds()
    red.step_c()
    red.step_y()
    red.step_z()
    red.step_c()
    red.step_c()
    attention_item()
    normed_back()
    red.step_y()
    red.step_z()
    red.step_c()
    red.step_y()
    adds.step_x(adds.done_x)
    attention_item()
    step_adds()
    red.step_y()
    red.step_z()
    red.step_c()
    red.step_y()
    attention_item()
    red.step_y()
    red.step_y()
    red.step_z()
    input_back()
    red.step_y()
    red.step_z()
    red.step_c()
    attention_item()
    red.step_c()
    red.step_z()
    red.step_y()
    adds.step_x(adds.done_x)
    red.step_z()
    red.step_y()
    red.step_c()
    attention_item()
    red.step_c()
    red.step_z()
    red.step_y()
    sum_gains()
    red.step_z()
    attention_item()
    red.step_c()
    attention_item()
    red.step_z()
    red.step_z()
    red.step_y()
    attention_item()
    red.step_z()
    red.step_y()
    red.step_c()
    red.step_z()
    step_adds()
    red.step_c()
    red.step_y()
    red.step_y()
    red.step_z()
    red.step_z()
    red.step_y()
    block_rows()
    red.step_z()
    assert red.done_y == red.done_z == red.total and adds.done_z == n and backs.done_x == n
    net.recv(gain_x.at[1], x_sems.at[4])
    gain_out[...] = gain_x[0] + gain_x[1]
    red.finish()
    net.drain()


def finish_kernel(ffn, attention, gains, qkv_grad, out_grad, gate_up_grad, down_grad, gain_sums):
    q, n = pl.program_id(0), pl.num_programs(0)
    z = lax.axis_index("dp") // 4
    gate_up_grad[...] = ffn[0:2, 0].astype(F32)
    down_grad[...] = ffn[2, 0].astype(F32).T
    total = attention[0, 2].astype(F32)
    total += jnp.where(z > 0, attention[0, 0].astype(F32), 0.0)
    total += jnp.where(z < n - 1, attention[0, 1].astype(F32), 0.0)

    @pl.when(q < 3)
    def _():
        qkv_grad[0] = total

    @pl.when(q == 3)
    def _():
        out_grad[...] = total.T

    gain_sums[0:1] = jnp.sum(gains[0:8], axis=0, keepdims=True)
    gain_sums[1:2] = jnp.sum(gains[8:16], axis=0, keepdims=True)


def call(kernel, collective_id, sends, locals_, vmem, outs, out_specs, scratch, sems, flags=0):
    def typed(entry):
        return (entry[:-1], F32) if entry[-1] is F32 else (entry, BF16)

    dma = pltpu.SemaphoreType.DMA
    return lambda in_specs, *args: pl.pallas_call(
        kernel,
        out_shape=[jax.ShapeDtypeStruct(*typed(entry)) for entry in outs],
        in_specs=in_specs,
        out_specs=out_specs,
        scratch_shapes=[pltpu.VMEM(*typed(entry)) for entry in scratch] + [dma((sends,)), dma((locals_,))] + [dma(entry) for entry in sems] + [pltpu.SemaphoreType.REGULAR((flags,))] * (flags > 0),
        compiler_params=pltpu.CompilerParams(collective_id=collective_id, has_side_effects=True, vmem_limit_bytes=vmem),
    )(*args)


def shards(dp, residual, seg_ids, attn_gain, w_qkv, w_out, ffn_gain, w_gate_up, w_down, cotangent):
    n = dp // 4
    rows, width = residual.shape
    group = seg_ids.shape[0]
    block, cols = w_qkv.shape[1:]
    part = w_gate_up.shape[2] // n
    pairs = jnp.arange(LANES, dtype=jnp.int32) % (HD // 2)
    freq = (ROPE_BASE ** (-(pairs.astype(F32) * 2.0 / HD)))[None]

    every = n * 2 * rows
    slots = SLOTS
    layer = call(
        functools.partial(layer_kernel, dp), 1, 320, 112, LIMIT,
        [
            (3, n, block, part), (4, 3, block, cols), (4, width, cols), (3, width, part), (n, 2, rows, width),
            (group, width), (group, cols), (3, group, cols), (rows, width), (rows, width, F32), (16, block, F32),
        ],
        [ANY] * 8 + [VM] * 3,
        [
            (4, width, cols), (every, width), (every, part), (every, 2 * part),
            (n, 2, rows, width), (n, rows, width), (n + 1, rows, width),
            (slots, 2, 2, block, part), (slots, 2, block, part), (slots, block, part),
            (group, width), (rows, width), (group, 3 * cols, F32), (rows, width, F32), (2, group, LANES, F32),
            (group, group, F32), (16, block, F32), (dp, 16, block, F32), (16, width, F32),
            (8, width, F32), (8, width, F32), (dp, 16, block, F32), (dp, 16, block, F32), (2, 16, block, F32),
        ],
        [
            (dp,), (4, n), (4, n), (3, 4, n), (2, n), (2, n), (5,),
            (n,), (n + 1,), (slots,), (slots,), (3, n), (4, n + 2), (dp,),
        ],
        5,
    )
    outputs = layer(
        [VM] * 7 + [ANY] * 3, residual, seg_ids[None], attn_gain[None], ffn_gain[None], freq, w_out, w_down, w_qkv,
        w_gate_up, cotangent,
    )
    result, totals, block_out, input_grad, gain_grads = outputs[0], outputs[1], outputs[8], outputs[9], outputs[10]
    qkv_grad, out_grad, gate_up_grad, down_grad, gain_sums = pl.pallas_call(
        finish_kernel,
        grid=(n,),
        out_shape=[
            jax.ShapeDtypeStruct(entry, F32)
            for entry in ((3, block, cols), (cols, block), (2, block, n * part), (n * part, block), (2, block))
        ],
        in_specs=[
            pl.BlockSpec((3, 1, block, part), lambda q: (0, q, 0, 0)),
            pl.BlockSpec((1, 3, block, cols), lambda q: (q, 0, 0, 0)),
            pl.BlockSpec((16, block), lambda q: (0, 0)),
        ],
        out_specs=[
            pl.BlockSpec((1, block, cols), lambda q: (jnp.minimum(q, 2), 0, 0)),
            pl.BlockSpec((cols, block), lambda q: (0, 0)),
            pl.BlockSpec((2, block, part), lambda q: (0, 0, q)),
            pl.BlockSpec((part, block), lambda q: (q, 0)),
            pl.BlockSpec((2, block), lambda q: (0, 0)),
        ],
        compiler_params=pltpu.CompilerParams(vmem_limit_bytes=LIMIT),
    )(result, totals, gain_grads)
    return block_out, input_grad, gain_sums[0], qkv_grad, out_grad, gain_sums[1], gate_up_grad, down_grad


def positions(segments):
    row_index = jnp.arange(segments.shape[1], dtype=jnp.int32)[None, :]
    previous = jnp.concatenate([segments[:, :1] - 1, segments[:, :-1]], axis=1)
    run_start = lax.cummax(jnp.where(segments != previous, row_index, 0), axis=1)
    return row_index - run_start


def rope_tables(places, head_dim):
    half_dim = head_dim // 2
    frequency = ROPE_BASE ** (-(jnp.arange(half_dim, dtype=jnp.float32) * 2.0 / head_dim))
    angles = places.astype(jnp.float32)[:, None, None] * frequency[None, None, :]
    return (jnp.cos(angles), jnp.sin(angles))


def rotate(field, cosine, sine_table):
    half_dim = field.shape[-1] // 2
    lower_half = field[..., :half_dim]
    upper_half = field[..., half_dim:]
    return jnp.concatenate(
        [
            lower_half * cosine - upper_half * sine_table,
            upper_half * cosine + lower_half * sine_table,
        ],
        axis=-1,
    )


def unrotate(field, cosine, sine_table):
    half_dim = field.shape[-1] // 2
    lower_half = field[..., :half_dim]
    upper_half = field[..., half_dim:]
    return jnp.concatenate(
        [
            lower_half * cosine + upper_half * sine_table,
            upper_half * cosine - lower_half * sine_table,
        ],
        axis=-1,
    )


def attention_scores(queries, key_rows, allowed):
    scores = jnp.einsum(
        "qhd,khd->hqk", queries, key_rows, preferred_element_type=jnp.float32
    ) * queries.shape[-1] ** (-0.5)
    return jnp.where(allowed[None], scores, -1e30)


def plain_shards(residual_in, seg_ids, attn_gain, w_qkv, w_out, ffn_gain, w_gate_up, w_down, cotangent):
    rows_local = residual_in.shape[0]
    group_rows = seg_ids.shape[0]
    offset = lax.axis_index("tensor") * rows_local
    live_rows = (lax.dynamic_slice_in_dim(seg_ids, offset, rows_local) >= 0).astype(jnp.float32)
    residual = residual_in.astype(jnp.float32)
    contract_rows = (((0,), (0,)), ((), ()))
    contract_cols = (((1,), (1,)), ((), ()))
    gain_attn, qkv_full, out_full = (
        lax.all_gather(attn_gain, "dp", axis=0, tiled=True),
        lax.all_gather(w_qkv, "dp", axis=1, tiled=True),
        lax.all_gather(w_out, "dp", axis=1, tiled=True),
    )
    norm_attn = lax.rsqrt(jnp.mean(residual * residual, axis=-1, keepdims=True) + EPSILON)
    unit_attn = residual * norm_attn
    normed = (unit_attn * gain_attn.astype(jnp.float32)).astype(jnp.bfloat16)
    normed_all = lax.all_gather(normed, "tensor", axis=0, tiled=True)
    projected = jnp.einsum("rd,cde->cre", normed_all, qkv_full, preferred_element_type=jnp.float32)
    head_count = qkv_full.shape[2] // HD
    head_shape = (group_rows, head_count, HD)
    cosine, sine_table = rope_tables(positions(seg_ids[None, :])[0], HD)
    queries = rotate(projected[0].reshape(head_shape), cosine, sine_table).astype(jnp.bfloat16)
    key_rows = rotate(projected[1].reshape(head_shape), cosine, sine_table).astype(jnp.bfloat16)
    value_rows = projected[2].reshape(head_shape).astype(jnp.bfloat16)
    row_index = jnp.arange(group_rows)
    allowed = (seg_ids[:, None] == seg_ids[None, :]) & (row_index[:, None] >= row_index[None, :])
    scores = attention_scores(queries, key_rows, allowed)
    row_top = jnp.max(scores, axis=-1, keepdims=True)
    log_total = row_top + jnp.log(jnp.sum(jnp.exp(scores - row_top), axis=-1, keepdims=True))
    weights = jnp.exp(scores - log_total).astype(jnp.bfloat16)
    attended = jnp.einsum("hqk,khd->qhd", weights, value_rows, preferred_element_type=jnp.float32)
    attended = attended.reshape(group_rows, head_count * HD).astype(jnp.bfloat16)
    mixed = residual + lax.psum_scatter(
        jnp.dot(attended, out_full, preferred_element_type=jnp.float32),
        "tensor",
        scatter_dimension=0,
        tiled=True,
    )
    gain_ffn, gate_up_full, down_full = (
        lax.all_gather(ffn_gain, "dp", axis=0, tiled=True),
        lax.all_gather(w_gate_up, "dp", axis=1, tiled=True),
        lax.all_gather(w_down, "dp", axis=1, tiled=True),
    )
    norm_ffn = lax.rsqrt(jnp.mean(mixed * mixed, axis=-1, keepdims=True) + EPSILON)
    unit_ffn = mixed * norm_ffn
    normed_ffn = (unit_ffn * gain_ffn.astype(jnp.float32)).astype(jnp.bfloat16)
    normed_ffn_all = lax.all_gather(normed_ffn, "tensor", axis=0, tiled=True)
    gate_up = jnp.einsum(
        "rd,cde->cre", normed_ffn_all, gate_up_full, preferred_element_type=jnp.float32
    )
    gate_pre = gate_up[0]
    up_pre = gate_up[1]
    sigmoid_gate = jax.nn.sigmoid(gate_pre)
    activated = gate_pre * sigmoid_gate
    hidden = (activated * up_pre).astype(jnp.bfloat16)
    output = mixed + lax.psum_scatter(
        jnp.dot(hidden, down_full, preferred_element_type=jnp.float32).astype(jnp.bfloat16),
        "tensor",
        scatter_dimension=0,
        tiled=True,
    ).astype(jnp.float32)
    grad_out = cotangent.astype(jnp.float32) * live_rows[:, None]
    grad_all = lax.all_gather(grad_out.astype(jnp.bfloat16), "tensor", axis=0, tiled=True)
    down_grad = lax.dot_general(hidden, grad_all, contract_rows, preferred_element_type=jnp.float32)
    hidden_grad = lax.dot_general(
        grad_all, down_full, contract_cols, preferred_element_type=jnp.float32
    )
    gate_grads = jnp.stack(
        [
            hidden_grad * up_pre * sigmoid_gate * (1.0 + gate_pre * (1.0 - sigmoid_gate)),
            hidden_grad * activated,
        ]
    ).astype(jnp.bfloat16)
    gate_up_grad = jnp.einsum(
        "rd,cre->cde", normed_ffn_all, gate_grads, preferred_element_type=jnp.float32
    )
    normed_ffn_grad = lax.psum_scatter(
        jnp.einsum("cre,cde->rd", gate_grads, gate_up_full, preferred_element_type=jnp.float32),
        "tensor",
        scatter_dimension=0,
        tiled=True,
    )
    ffn_gain_part = jnp.sum(normed_ffn_grad * unit_ffn, axis=0)
    scaled_ffn = normed_ffn_grad * gain_ffn.astype(jnp.float32)
    mixed_grad = grad_out + norm_ffn * (
        scaled_ffn - unit_ffn * jnp.mean(scaled_ffn * unit_ffn, axis=-1, keepdims=True)
    )
    mixed_all = lax.all_gather(mixed_grad.astype(jnp.bfloat16), "tensor", axis=0, tiled=True)
    out_grad = lax.dot_general(
        attended, mixed_all, contract_rows, preferred_element_type=jnp.float32
    )
    attended_grad = lax.dot_general(
        mixed_all, out_full, contract_cols, preferred_element_type=jnp.float32
    )
    attended_grad = attended_grad.astype(jnp.bfloat16).reshape(head_shape)
    probabilities = jnp.exp(attention_scores(queries, key_rows, allowed) - log_total)
    value_grad = jnp.einsum(
        "hqk,qhd->khd",
        probabilities.astype(jnp.bfloat16),
        attended_grad,
        preferred_element_type=jnp.float32,
    )
    prob_grad = jnp.einsum(
        "qhd,khd->hqk", attended_grad, value_rows, preferred_element_type=jnp.float32
    )
    score_grad = (
        probabilities * (prob_grad - jnp.sum(probabilities * prob_grad, axis=-1, keepdims=True))
    ).astype(jnp.bfloat16)
    scale_factor = HD ** (-0.5)
    query_grad = (
        jnp.einsum("hqk,khd->qhd", score_grad, key_rows, preferred_element_type=jnp.float32)
        * scale_factor
    )
    key_grad = (
        jnp.einsum("hqk,qhd->khd", score_grad, queries, preferred_element_type=jnp.float32)
        * scale_factor
    )
    qkv_grads = jnp.stack(
        [
            unrotate(query_grad, cosine, sine_table),
            unrotate(key_grad, cosine, sine_table),
            value_grad,
        ]
    )
    qkv_grads = qkv_grads.reshape(3, group_rows, head_count * HD).astype(jnp.bfloat16)
    qkv_grad = jnp.einsum("rd,cre->cde", normed_all, qkv_grads, preferred_element_type=jnp.float32)
    normed_grad = lax.psum_scatter(
        jnp.einsum("cre,cde->rd", qkv_grads, qkv_full, preferred_element_type=jnp.float32),
        "tensor",
        scatter_dimension=0,
        tiled=True,
    )
    attn_gain_part = jnp.sum(normed_grad * unit_attn, axis=0)
    scaled_attn = normed_grad * gain_attn.astype(jnp.float32)
    input_grad = mixed_grad + norm_attn * (
        scaled_attn - unit_attn * jnp.mean(scaled_attn * unit_attn, axis=-1, keepdims=True)
    )
    (
        query_total,
        key_total,
        value_total,
        out_total,
        attn_gain_total,
        gate_total,
        up_total,
        down_total,
        ffn_gain_total,
    ) = (
        lax.psum_scatter(qkv_grad[0], "dp", scatter_dimension=0, tiled=True),
        lax.psum_scatter(qkv_grad[1], "dp", scatter_dimension=0, tiled=True),
        lax.psum_scatter(qkv_grad[2], "dp", scatter_dimension=0, tiled=True),
        lax.psum_scatter(out_grad, "dp", scatter_dimension=1, tiled=True),
        lax.psum_scatter(attn_gain_part, "dp", scatter_dimension=0, tiled=True),
        lax.psum_scatter(gate_up_grad[0], "dp", scatter_dimension=0, tiled=True),
        lax.psum_scatter(gate_up_grad[1], "dp", scatter_dimension=0, tiled=True),
        lax.psum_scatter(down_grad, "dp", scatter_dimension=1, tiled=True),
        lax.psum_scatter(ffn_gain_part, "dp", scatter_dimension=0, tiled=True),
    )
    gate_up_total = jnp.stack([gate_total, up_total])
    qkv_total = jnp.stack([query_total, key_total, value_total])
    attn_gain_sum, ffn_gain_sum = lax.psum((attn_gain_total, ffn_gain_total), "tensor")
    return (
        output.astype(jnp.bfloat16),
        input_grad,
        attn_gain_sum,
        qkv_total,
        out_total,
        ffn_gain_sum,
        gate_up_total,
        down_total,
    )


def solution(mesh):
    in_specs = (
        P(("dp", "tensor"), None),
        P("dp"),
        P("dp"),
        P(None, "dp", "tensor"),
        P("tensor", "dp"),
        P("dp"),
        P(None, "dp", "tensor"),
        P("tensor", "dp"),
        P(("dp", "tensor"), None),
    )
    out_specs = (
        P(("dp", "tensor"), None),
        P(("dp", "tensor"), None),
        P("dp"),
        P(None, "dp", "tensor"),
        P("tensor", "dp"),
        P("dp"),
        P(None, "dp", "tensor"),
        P("tensor", "dp"),
    )
    dp = mesh.shape["dp"]
    local = functools.partial(shards, dp) if dp == 16 else plain_shards
    return jax.shard_map(local, mesh=mesh, in_specs=in_specs, out_specs=out_specs, check_vma=False)
```

```python
import functools

import jax
import jax.numpy as jnp
from jax import lax
from jax.experimental import pallas as pl
from jax.experimental.pallas import tpu as pltpu
from jax.sharding import PartitionSpec as P

HD = 64
EPSILON = 1e-05
ROPE_BASE = 130000.0
MESH = pl.DeviceIdType.MESH
ANY = pl.BlockSpec(memory_space=pl.ANY)
VM = pl.BlockSpec(memory_space=pltpu.VMEM)
F32 = jnp.float32
BF16 = jnp.bfloat16
LANES = 128
SLOTS = 9
LIMIT = 66977792
NT = (((1,), (1,)), ((), ()))
TN = (((0,), (0,)), ((), ()))
NN = (((1,), (0,)), ((), ()))


def dot(a, b, dims=NN):
    return lax.dot_general(a, b, dims, preferred_element_type=F32)


def when(cond, action):
    if cond is None:
        action()
    else:
        pl.when(cond)(action)


class Net:
    def __init__(self, dp, send_sems, local_sems):
        self.n = dp // 4
        self.dp_index = lax.axis_index("dp")
        self.x = lax.axis_index("tensor")
        self.z = self.dp_index // 4
        self.y = (self.dp_index // 2) % 2
        self.c = self.dp_index % 2
        self.send_sems = send_sems
        self.local_sems = local_sems
        self.sent = 0
        self.moved = 0
        self.pending = []
        self.kept = []
        self.tags = {}

    def place(self, z, y, c):
        return (z * 2 + y) * 2 + c

    def device(self, z=None, y=None, c=None, x=None):
        z = self.z if z is None else z
        y = self.y if y is None else y
        c = self.c if c is None else c
        x = self.x if x is None else x
        return (self.place(z, y, c), x)

    def greet(self, devices):
        barrier = pltpu.get_barrier_semaphore()
        for device in devices:
            pl.semaphore_signal(barrier, inc=1, device_id=device, device_id_type=MESH)
        pl.semaphore_wait(barrier, len(devices))

    def send(self, src, dst, recv_sem, device, cond=None):
        sem = self.send_sems.at[self.sent]
        self.sent += 1
        copy = pltpu.make_async_remote_copy(
            src_ref=src, dst_ref=dst, send_sem=sem, recv_sem=recv_sem, device_id=device, device_id_type=MESH
        )
        when(cond, copy.start)
        self.pending.append((cond, copy))
        return self.pending[-1]

    def recv(self, dst, recv_sem):
        pltpu.make_async_remote_copy(
            src_ref=dst, dst_ref=dst, send_sem=self.send_sems.at[0], recv_sem=recv_sem,
            device_id=self.device(c=1 - self.c), device_id_type=MESH,
        ).wait_recv()

    def local(self, src, dst, cond=None):
        sem = self.local_sems.at[self.moved]
        self.moved += 1
        copy = pltpu.make_async_copy(src, dst, sem)
        when(cond, copy.start)
        self.kept.append((cond, copy))
        return self.kept[-1]

    def settle(self, entry):
        for entries, wait in ((self.kept, "wait"), (self.pending, "wait_send")):
            for k, known in enumerate(entries):
                if known is entry:
                    when(entry[0], getattr(entry[1], wait))
                    del entries[k]
                    return

    def tag(self, name, entries):
        self.tags.setdefault(name, []).extend(entries)

    def settle_tag(self, *names):
        for name in names:
            for entry in self.tags.pop(name, ()):
                self.settle(entry)

    def drain(self):
        assert self.sent <= self.send_sems.shape[0] and self.moved <= self.local_sems.shape[0]
        for cond, copy in self.pending:
            when(cond, copy.wait_send)
        for cond, copy in self.kept:
            when(cond, copy.wait)


class Gather:
    def __init__(self, net, own, at, sems, tag):
        self.net, self.own, self.at, self.tag = net, own, at, tag
        self.sems = sems

    def spread(self, block, src, ysend=True):
        net = self.net
        here = net.place(block, net.y, net.c)
        net.tag(self.tag, [net.send(src, self.at(here), self.sems.at[1, block], net.device(y=1 - net.y))])
        net.tag(self.tag, [net.send(src, self.at(here), self.sems.at[2 + net.y, block], net.device(c=1 - net.c))])

    def start(self):
        net = self.net
        here = self.at(net.dp_index)
        net.tag(self.tag, [net.send(self.own, here, self.sems.at[0, net.z], net.device(z=net.z + 1), net.z < net.n - 1)])
        net.tag(self.tag, [net.send(self.own, here, self.sems.at[0, net.z], net.device(z=net.z - 1), net.z > 0)])
        self.spread(net.z, self.own)
        self.kept = net.local(self.own, here)

    def step(self, s):
        net = self.net
        for sign in (1, -1):
            block = net.z - s * sign
            valid = jnp.logical_and(block >= 0, block < net.n)
            nxt = net.z + sign
            more = jnp.logical_and(nxt >= 0, nxt < net.n)
            here = self.at(net.place(block, net.y, net.c))

            @pl.when(valid)
            def _():
                net.recv(here, self.sems.at[0, block])

            net.tag(self.tag, [net.send(here, here, self.sems.at[0, block], net.device(z=nxt), jnp.logical_and(valid, more))])
            net.tag(self.tag, [net.send(here, here, self.sems.at[1, block], net.device(y=1 - net.y), valid)])
            net.tag(self.tag, [net.send(here, here, self.sems.at[2 + net.y, block], net.device(c=1 - net.c), valid)])

    def cross(self, block):
        net = self.net
        there = self.at(net.place(block, 1 - net.y, net.c))
        net.recv(there, self.sems.at[1, block])
        net.tag(self.tag, [net.send(there, there, self.sems.at[3 - net.y, block], net.device(c=1 - net.c))])

    def cross_step(self, s):
        net = self.net
        if s == 0:
            self.cross(net.z)
            return
        for sign in (1, -1):
            block = net.z - s * sign
            valid = jnp.logical_and(block >= 0, block < net.n)
            there = self.at(net.place(block, 1 - net.y, net.c))

            @pl.when(valid)
            def _():
                net.recv(there, self.sems.at[1, block])

            net.tag(self.tag, [net.send(there, there, self.sems.at[3 - net.y, block], net.device(c=1 - net.c), valid)])

    def finish(self, block):
        net = self.net
        for y in (0, 1):
            net.recv(self.at(net.place(block, y, 1 - net.c)), self.sems.at[2 + y, block])


class Exchange:
    def __init__(self, net, part, at, sems, tag):
        self.net, self.part, self.at, self.tag = net, part, at, tag
        self.sems = sems

    def start(self):
        net = self.net
        here = self.at(net.dp_index)
        for d in list(range(1, net.n)):
            to = (net.z + d) % net.n
            net.tag(self.tag, [net.send(self.part(to), here, self.sems.at[0, net.z], net.device(z=to))])
        own = self.part(net.z)
        net.tag(self.tag, [net.send(own, here, self.sems.at[1, net.z], net.device(y=1 - net.y))])
        net.tag(self.tag, [net.send(own, here, self.sems.at[2 + net.y, net.z], net.device(c=1 - net.c))])
        self.kept = net.local(own, here)

    def step(self, block):
        net = self.net
        here = self.at(net.place(block, net.y, net.c))
        net.recv(here, self.sems.at[0, block])
        net.send(here, here, self.sems.at[1, block], net.device(y=1 - net.y))
        net.send(here, here, self.sems.at[2 + net.y, block], net.device(c=1 - net.c))

    def cross(self, block):
        net = self.net
        there = self.at(net.place(block, 1 - net.y, net.c))
        net.recv(there, self.sems.at[1, block])
        net.send(there, there, self.sems.at[3 - net.y, block], net.device(c=1 - net.c))

    finish = Gather.finish


class Rows:
    def __init__(self, net, own, at, sems, tag):
        self.net, self.own, self.at, self.tag = net, own, at, tag
        self.sems = sems

    def start(self):
        net = self.net
        here = self.at(net.z, net.x)
        own = here if self.own is None else self.own
        net.tag(self.tag, [net.send(own, here, self.sems.at[0, net.z], net.device(z=net.z + 1), net.z < net.n - 1)])
        net.tag(self.tag, [net.send(own, here, self.sems.at[0, net.z], net.device(z=net.z - 1), net.z > 0)])
        net.tag(self.tag, [net.send(own, here, self.sems.at[1, net.z], net.device(x=1 - net.x))])
        if self.own is not None:
            net.tag(self.tag + "_kept", [net.local(own, here)])

    def step(self, s):
        net = self.net
        forwarded = []
        for sign in (1, -1):
            block = net.z - s * sign
            valid = jnp.logical_and(block >= 0, block < net.n)
            nxt = net.z + sign
            more = jnp.logical_and(nxt >= 0, nxt < net.n)
            here = self.at(block, net.x)

            @pl.when(valid)
            def _():
                net.recv(here, self.sems.at[0, block])

            forwarded.append(net.send(here, here, self.sems.at[0, block], net.device(z=nxt), jnp.logical_and(valid, more)))
            forwarded.append(net.send(here, here, self.sems.at[1, block], net.device(x=1 - net.x), valid))
        if self.own is None:
            net.tag(self.tag, forwarded)

    def finish(self, block):
        net = self.net
        net.recv(self.at(block, 1 - net.x), self.sems.at[1, block])


class Reduce:
    def __init__(self, net, part, from_c, from_y, result, line, sems, total):
        self.net, self.part, self.from_c, self.from_y = net, part, from_c, from_y
        self.result, self.totals = result
        self.line = line
        self.cs, self.ys, self.zs, self.ls, self.free = sems
        self.slots = part.shape[0]
        self.total = total
        self.items = []
        self.out = {}
        self.done_c = self.done_y = self.done_z = 0

    def add(self, total, term):
        def body(r):
            span = pl.ds(r, 16)
            total[span] = (total[span].astype(F32) + term[span].astype(F32)).astype(BF16)

        loop(total.shape[0], 16, body, 8)

    def credit(self, which, device):
        pl.semaphore_signal(self.free.at[which], inc=1, device_id=device, device_id_type=MESH)

    def item(self, matrix, to, left, right, depth, block):
        net = self.net
        i = len(self.items)
        slot = i % self.slots
        self.items.append((matrix, to))
        assert self.done_z > i - self.slots
        for entry in self.out.pop(i - self.slots, ()):
            net.settle(entry)

        def body(col):
            term = dot(left, right[:, pl.ds(col, 256)], TN).astype(BF16)
            for y in (0, 1):
                for c in (0, 1):
                    at = (y * 2 + c) * block
                    self.part[slot, c, y, :, pl.ds(col, 256)] = term[at : at + block]

        loop(right.shape[1], 256, body, 4)
        if i >= self.slots:
            pl.semaphore_wait(self.free.at[0], 1)
        self.out[i] = [
            net.send(self.part.at[slot, 1 - net.c], self.from_c.at[slot], self.cs.at[slot], net.device(c=1 - net.c))
        ]

    def step_c(self):
        net = self.net
        i = self.done_c
        self.done_c += 1
        slot = i % self.slots
        net.recv(self.from_c.at[slot], self.cs.at[slot])
        for y in (0, 1):
            self.add(self.part.at[slot, net.c, y], self.from_c.at[slot, y])
        if i + self.slots < self.total:
            self.credit(0, net.device(c=1 - net.c))
        if i >= self.slots:
            pl.semaphore_wait(self.free.at[1], 1)
        self.out[i].append(
            net.send(self.part.at[slot, net.c, 1 - net.y], self.from_y.at[slot], self.ys.at[slot], net.device(y=1 - net.y))
        )

    def step_y(self):
        net = self.net
        i = self.done_y
        self.done_y += 1
        slot = i % self.slots
        matrix, to = self.items[i]
        net.recv(self.from_y.at[slot], self.ys.at[slot])
        self.add(self.part.at[slot, net.c, net.y], self.from_y.at[slot])
        if i + self.slots < self.total:
            self.credit(1, net.device(y=1 - net.y))
        matrices = self.result.shape[0]
        if matrix >= matrices:
            return
        src = self.part.at[slot, net.c, net.y]
        dst = self.result.at[matrix, net.z]
        away = to != net.z
        self.out[i].append(net.send(src, dst, self.zs.at[matrix, net.z], net.device(z=to), away))
        self.out[i].append(net.local(src, dst, jnp.logical_not(away)))
        self.done_z += 1

    def step_z(self):
        net = self.net
        i = self.done_z
        self.done_z += 1
        assert i < self.done_y
        matrix, to = self.items[i]
        m = matrix - self.result.shape[0]
        total = self.part.at[i % self.slots, net.c, net.y]
        behind = jnp.where(to > net.z, net.z > 0, net.z < net.n - 1)
        place = self.line(m, to)

        @pl.when(jnp.logical_and(to != net.z, behind))
        def _():
            net.recv(place, self.ls.at[m, to])
            self.add(total, place)

        side = jnp.where(to > net.z, 0, 1)
        nxt = jnp.where(to > net.z, net.z + 1, net.z - 1)
        there = net.device(z=nxt)
        last = jnp.logical_and(to != net.z, to == nxt)
        self.out[i].append(net.send(total, place, self.ls.at[m, to], there, jnp.logical_and(to != net.z, to != nxt)))
        self.out[i].append(net.send(total, self.totals.at[m, side], self.ls.at[m, net.n + side], there, last))
        self.out[i].append(net.local(total, self.totals.at[m, 2], to == net.z))

    def finish(self):
        net = self.net
        for matrix in range(self.result.shape[0]):
            for d in range(1, net.n):
                block = (net.z + d) % net.n
                net.recv(self.result.at[matrix, block], self.zs.at[matrix, block])
        for m in range(self.totals.shape[0]):
            for side, cond in ((0, net.z > 0), (1, net.z < net.n - 1)):

                @pl.when(cond)
                def _():
                    net.recv(self.totals.at[m, side], self.ls.at[m, net.n + side])


def loop(total, step, body, unroll):
    @pl.loop(0, total // step, unroll=unroll)
    def _(i):
        body(pl.multiple_of(i * step, step))


def turn(field, cosine, sine, lane):
    half = HD // 2
    partner = jnp.where(lane % HD < half, pltpu.roll(field, LANES - half, 1), pltpu.roll(field, half, 1))
    return field * cosine + partner * sine


def head_masks():
    lane = lax.broadcasted_iota(jnp.int32, (1, LANES), 1)
    return (lane < HD).astype(BF16), (lane >= HD).astype(BF16)


def both(field, masks):
    return jnp.concatenate([field * masks[0], field * masks[1]], axis=0)


def pick(stacked, rows):
    lane = lax.broadcasted_iota(jnp.int32, (1, LANES), 1)
    return jnp.where(lane < HD, stacked[:rows], stacked[rows:])


def softmax(queries2, key_rows, allowed):
    scores = dot(queries2, key_rows, NT) * HD ** (-0.5)
    scores = jnp.where(allowed > 0, scores, -1e30)
    raised = jnp.exp(scores - jnp.max(scores, axis=-1, keepdims=True))
    return raised / jnp.sum(raised, axis=-1, keepdims=True)


def far_first(net):
    n = net.n
    table = [sorted(range(n), key=lambda b: (-abs(b - z), -b)) for z in range(n)]
    return [sum(jnp.where(net.z == z, table[z][k], 0) for z in range(n)) for k in range(n)]


class RowSum:
    def __init__(self, net, order, part, from_x, from_z, sems):
        self.net, self.order, self.part, self.from_x, self.from_z = net, order, part, from_x, from_z
        self.xs, self.zs = sems
        self.sent = []
        self.done_x = self.done_z = 0

    def start(self, b):
        net = self.net
        self.sent.append(
            net.send(self.part(b, 1 - net.x), self.from_x.at[b], self.xs.at[b], net.device(x=1 - net.x))
        )

    def add(self, total, term):
        def body(r):
            span = pl.ds(r, 16)
            total[span] = (total[span].astype(F32) + term[span].astype(F32)).astype(BF16)

        loop(total.shape[0], 16, body, 8)

    def step_x(self, k):
        net = self.net
        b = self.order[k]
        self.done_x += 1
        net.recv(self.from_x.at[b], self.xs.at[b])
        self.add(self.part(b, net.x), self.from_x.at[b])

    def step_z(self, k):
        net = self.net
        b = self.order[k]
        self.done_z += 1
        total = self.part(b, net.x)
        behind = jnp.where(b > net.z, net.z > 0, net.z < net.n - 1)

        @pl.when(jnp.logical_and(b != net.z, behind))
        def _():
            net.recv(self.from_z.at[b], self.zs.at[b])
            self.add(total, self.from_z.at[b])

        slot = jnp.where(b == net.z - 1, net.n, b)
        to = jnp.where(b > net.z, net.z + 1, net.z - 1)
        self.sent.append(net.send(total, self.from_z.at[slot], self.zs.at[slot], net.device(z=to), b != net.z))

    def finish(self):
        net = self.net
        total = self.part(net.z, net.x)
        for slot, cond in ((net.z, net.z > 0), (net.n, net.z < net.n - 1)):

            @pl.when(cond)
            def _():
                net.recv(self.from_z.at[slot], self.zs.at[slot])
                self.add(total, self.from_z.at[slot])


def norm_back(grad, value, gain):
    scale = lax.rsqrt(jnp.mean(value * value, axis=-1, keepdims=True) + EPSILON)
    unit = value * scale
    scaled = grad * gain
    back = scale * (scaled - unit * jnp.mean(scaled * unit, axis=-1, keepdims=True))
    return back, grad * unit


def layer_kernel(
    dp,
    residual, seg, attn_gain, ffn_gain, freq, w_out, w_down, w_qkv, w_gate_up, cotangent,
    result, totals, wa_out, wf_out, normed_ffn_out, normed_out, attended_out, qkv_out, block_out, input_grad, gain_out,
    weights, grad, hidden, gate_up_grad, back, back_x, back_z, part, from_c, from_y,
    mixed_all, from_x, pre, mixed, tables, allowed, gains, all_gains, gains_all, gain_sum, ffn_sum, gain_to,
    gain_from, gain_x,
    send_sems, local_sems, gain_sems, q_sems, o_sems, f_sems, g_sems, n_sems, x_sems,
    bx_sems, bz_sems, rc_sems, ry_sems, rz_sems, rl_sems, back_gain_sems, free,
):
    net = Net(dp, send_sems, local_sems)
    n, me, x = net.n, net.dp_index, net.x
    rows, width = residual.shape
    block, cols = w_qkv.shape[1:]
    group = pair = 2 * rows
    every = grad.shape[0]
    depth = width // n
    assert w_gate_up.shape[2] == n * cols and width == 2 * cols and width == 2 * every and width == dp * block
    lane = lax.broadcasted_iota(jnp.int32, (group, LANES), 1)
    live = gain_to
    assert gain_to.shape == (group // 16, 16, LANES)
    order = far_first(net)
    beside = jnp.where(net.z > 0, 1, 0) + jnp.where(net.z < n - 1, 1, 0)
    net.greet([((me + k) % dp, x) for k in range(1, dp)] + [(me, 1 - x)])

    def block_rows_of(z, half):
        return pl.ds(pl.multiple_of((z * 2 + half) * rows, rows), rows)

    normed_all = back.at[0]
    ffn_own, to_x = back.at[1, 0], back.at[1, 1]
    down_own = hidden.at[pl.ds(0, n * block)]
    out_own = hidden.at[pl.ds(n * block, block)]
    early_qkv = [
        gate_up_grad.at[pl.ds(0, group), pl.ds(0, cols)],
        gate_up_grad.at[pl.ds(0, group), pl.ds(cols, cols)],
        gate_up_grad.at[pl.ds(group, group), pl.ds(0, cols)],
    ]
    early_attended = gate_up_grad.at[pl.ds(group, group), pl.ds(cols, cols)]

    def at_weights(first, count):
        return lambda index: weights.at[pl.ds(first, count), pl.ds(pl.multiple_of(index * block, block), block)]

    def at_out(index):
        return weights.at[3, pl.ds(pl.multiple_of(index * block, block), block)]

    def ffn_part(m):
        def own(to):
            if m == 2:
                return down_own.at[pl.ds(pl.multiple_of(to * block, block), block)]
            return w_gate_up.at[m, :, pl.ds(pl.multiple_of(to * cols, cols), cols)]

        return own

    def ffn_place(m):
        return lambda index: wf_out.at[m, pl.ds(pl.multiple_of(index * block, block), block)]

    qkv = Gather(net, w_qkv, at_weights(0, 3), q_sems, "qkv")
    out = Gather(net, out_own, at_out, o_sems, "out")
    ffn = [Exchange(net, ffn_part(m), ffn_place(m), f_sems.at[m], "ffn") for m in range(3)]
    grads = Rows(net, None, lambda z, half: grad.at[block_rows_of(z, half)], g_sems, "grads")
    ffn_rows = Rows(net, ffn_own, lambda z, half: normed_ffn_out.at[z, half], n_sems, "rows")
    load_grad = net.local(cotangent, grad.at[block_rows_of(net.z, x)])

    def send_gains():
        gains[0:8] = jnp.broadcast_to(attn_gain[...].astype(F32), (8, block))
        gains[8:16] = jnp.broadcast_to(ffn_gain[...].astype(F32), (8, block))
        for k in range(1, dp):
            net.send(gains, all_gains.at[me], gain_sems.at[me], ((me + k) % dp, x))
        all_gains[me] = gains[...]

    def turn_weights():
        out_own[...] = w_out[...].T
        for q in range(n):
            down_own[q * block : (q + 1) * block] = w_down[q * cols : (q + 1) * cols].T

    def mask_grads():
        seg_rows = jnp.broadcast_to(seg[...].astype(F32), (LANES, group))
        seg_cols = seg_rows.T
        alive = (seg_cols >= 0).astype(F32)
        for i in range(group // 16):
            live[i] = alive[i * 16 : (i + 1) * 16]
        row_id = lax.broadcasted_iota(jnp.int32, (group, group), 0)
        col_id = lax.broadcasted_iota(jnp.int32, (group, group), 1)
        same = jnp.concatenate([seg_cols] * (group // LANES), axis=1) == jnp.concatenate([seg_rows] * (group // LANES), axis=0)
        mask = jnp.logical_and(same, row_id >= col_id).astype(F32)
        allowed[...] = mask
        angles = (jnp.sum(mask, axis=1, keepdims=True) - 1.0) * freq[...]
        tables[0] = jnp.cos(angles)
        tables[1] = jnp.where(lane % HD < HD // 2, -jnp.sin(angles), jnp.sin(angles))

        net.settle(load_grad)

        def body(r):
            span = pl.ds(pl.multiple_of((net.z * 2 + x) * rows + r, 16), 16)
            grad[span] = (grad[span].astype(F32) * live[(x * rows + r) // 16, :, 0:1]).astype(BF16)

        loop(rows, 16, body, 4)

    def norm():
        for k in range(1, dp):
            source = (me + k) % dp
            net.recv(all_gains.at[source], gain_sems.at[source])
        for i in range(dp):
            gains_all[:, i * block : (i + 1) * block] = all_gains[i]

        def body(r):
            value = residual[pl.ds(r, 16)].astype(F32)
            unit = value * lax.rsqrt(jnp.mean(value * value, axis=-1, keepdims=True) + EPSILON)
            normed_all[x, pl.ds(r, 16)] = (unit * gains_all[0:1]).astype(BF16)

        loop(rows, 16, body, 4)
        net.tag("normed", [net.send(normed_all.at[x], normed_all.at[x], x_sems.at[0], net.device(x=1 - x))])

    def project(k):
        if k == 0:
            net.recv(normed_all.at[1 - x], x_sems.at[0])
            net.settle(qkv.kept)
            net.tag("normed", [net.local(normed_all.at[half], normed_out.at[pl.ds(half * rows, rows)]) for half in (0, 1)])
        b = (net.z + k) % n
        qkv.finish(b)
        base = pl.multiple_of(b * depth, depth)

        def body(col):
            left = jnp.concatenate([normed_all[0, :, pl.ds(base, depth)], normed_all[1, :, pl.ds(base, depth)]], axis=0)
            for m in range(3):
                term = dot(left, weights[m, pl.ds(base, depth), pl.ds(col, 256)])
                to = pl.ds(pl.multiple_of(m * cols + col, 256), 256)
                pre[:, to] = term if k == 0 else pre[:, to] + term

        loop(cols, 256, body, 4)
        if k == n - 1:
            net.tag("save", [net.local(weights.at[pl.ds(0, 3)], wa_out.at[pl.ds(0, 3)])])

    def attend():
        masks = head_masks()

        def body(col):
            cosine, sine = tables[0], tables[1]
            queries = turn(pre[:, pl.ds(col, LANES)], cosine, sine, lane).astype(BF16)
            key_rows = turn(pre[:, pl.ds(pl.multiple_of(cols + col, LANES), LANES)], cosine, sine, lane).astype(BF16)
            value_rows = pre[:, pl.ds(pl.multiple_of(2 * cols + col, LANES), LANES)].astype(BF16)
            early_qkv[0][:, pl.ds(col, LANES)] = queries
            early_qkv[1][:, pl.ds(col, LANES)] = key_rows
            early_qkv[2][:, pl.ds(col, LANES)] = value_rows
            may = jnp.concatenate([allowed[...], allowed[...]], axis=0)
            probs = softmax(both(queries, masks), key_rows, may).astype(BF16)
            early_attended[:, pl.ds(col, LANES)] = pick(dot(probs, value_rows), group).astype(BF16)

        loop(cols, LANES, body, 4)
        net.tag("early", [net.local(early_qkv[m], qkv_out.at[m]) for m in range(3)])
        net.tag("early", [net.local(early_attended, attended_out)])

    def join():
        for k in range(n):
            out.finish((net.z + k) % n)
        net.settle(out.kept)
        net.tag("save_out", [net.local(weights.at[3], wa_out.at[3])])

        def body(col):
            span = pl.ds(col, 256)
            term = dot(early_attended[...], weights[3, span, :], NT)
            low, high = term[:rows], term[rows:]
            input_grad[:, span] = jnp.where(x == 0, low, high)
            to_x[:, span] = jnp.where(x == 0, high, low).astype(BF16)

        loop(width, 256, body, 4)
        net.tag("to_x", [net.send(to_x, from_x, x_sems.at[1], net.device(x=1 - x))])

    def mix():
        net.recv(from_x, x_sems.at[1])

        def body(r):
            span = pl.ds(r, 16)
            value = residual[span].astype(F32) + input_grad[span] + from_x[span].astype(F32)
            mixed[span] = value
            unit = value * lax.rsqrt(jnp.mean(value * value, axis=-1, keepdims=True) + EPSILON)
            ffn_own[span] = (unit * gains_all[8:9]).astype(BF16)

        loop(rows, 16, body, 4)

    def load_ffn(m):
        for k in range(n):
            ffn[m].finish((net.z + k) % n)
        net.settle(ffn[m].kept)
        net.settle_tag("qkv", "save")
        net.tag("weights", [net.local(wf_out.at[m], weights.at[m])])

    def load_rows(k):
        net.settle_tag("out", "save_out", "rows_kept")
        b = order[k]
        ffn_rows.finish(b)
        for x_half in (0, 1):
            for half in (0, 1):
                there = pl.ds(pl.multiple_of(half * every + (b * 2 + x_half) * rows, rows), rows)
                src = normed_ffn_out.at[b, x_half, :, pl.ds(half * cols, cols)]
                net.tag("load%d" % k, [net.local(src, weights.at[3, there])])

    def ffn_step(m, k):
        ffn[m].step((net.z + k) % n)

    def ffn_cross(m):
        for k in range(n):
            ffn[m].cross((net.z + k) % n)


    def features(half):
        return weights.at[3, pl.ds(half * every, every)]

    gate_grad, up_grad = gate_up_grad.at[:, pl.ds(0, cols)], gate_up_grad.at[:, pl.ds(cols, cols)]
    add = gate_up_grad
    backs = RowSum(net, order, lambda b, half: back.at[b, half], back_x, back_z, (bx_sems, bz_sems))
    adds = RowSum(
        net, order, lambda b, half: add.at[pl.ds(pl.multiple_of((b * 2 + half) * rows, rows), rows)],
        back_x, back_z, (bx_sems, bz_sems),
    )
    red = Reduce(
        net, part, from_c, from_y, (result, totals),
        lambda m, to: weights.at[3, pl.ds(pl.multiple_of((m * n + to) * block, block), block)],
        (rc_sems, ry_sems, rz_sems, rl_sems, free), 7 * n,
    )
    def rows_of(b):
        return pl.ds(pl.multiple_of(b * pair, pair), pair)

    def forward(k):
        net.settle_tag("load%d" % k, "weights", "ffn", "early")
        grads.finish(order[k])
        here = rows_of(order[k])

        def body(col):
            span = pl.ds(col, 256)

            def project(m):
                return dot(features(0)[here], weights[m, pl.ds(0, cols), span]) + dot(
                    features(1)[here], weights[m, pl.ds(cols, cols), span]
                )

            gate, up = project(0), project(1)
            hidden_grad = dot(grad[here], weights[2, :, span])
            sigmoid = 1.0 / (1.0 + jnp.exp(-gate))
            active = gate * sigmoid
            hidden[here, span] = (active * up).astype(BF16)
            gate_grad[here, span] = (hidden_grad * up * sigmoid * (1.0 + gate * (1.0 - sigmoid))).astype(BF16)
            up_grad[here, span] = (hidden_grad * active).astype(BF16)

        loop(cols, 256, body, 4)

    def backward(k):
        net.settle_tag("normed", "to_x", "rows")
        b = order[k]
        here = rows_of(b)

        def body(col):
            span = pl.ds(col, 256)
            term = dot(gate_grad[here], weights[0, span, :], NT) + dot(up_grad[here], weights[1, span, :], NT)
            term = term.astype(BF16)
            back[b, 0, :, span] = term[:rows]
            back[b, 1, :, span] = term[rows:]

        loop(width, 256, body, 4)
        backs.start(b)

    def add_chunk(k):
        here = rows_of(order[k])

        def body(col):
            span = pl.ds(col, 256)
            add[here, span] = dot(hidden[here], weights[2, span, :], NT).astype(BF16)

        loop(width, 256, body, 4)
        if k == 0:
            pl.semaphore_wait(free.at[2], 1)
        adds.start(order[k])

    ffn_items = [(2, k) for k in range(n)] + [(m, k) for k in range(n) for m in (0, 1)]
    attention_items = [(3, k) for k in range(n)] + [(m, k) for k in range(n) for m in range(3)]

    def ffn_item():
        m, k = ffn_items[len(red.items)]
        b = order[k]
        base = b * depth
        if m == 2:
            left = grad[:, pl.ds(pl.multiple_of(base, depth), depth)]
        else:
            row = pl.ds(pl.multiple_of(base // cols * every, every), every)
            left = weights[3, row, pl.ds(pl.multiple_of(base % cols, depth), depth)]
        red.item(m, b, left, (gate_grad, up_grad, hidden)[m], depth, block)

    def attention_item():
        m, k = attention_items[len(red.items) - len(ffn_items)]
        base = pl.ds(pl.multiple_of(order[k] * depth, depth), depth)
        left, right = (mixed_all, attended) if m == 3 else (normed, grads_of[m])
        red.item(3 + m, order[k], left[:, base], right, depth, block)

    queries_of, keys_of, values_of = [hidden.at[pl.ds(m * pair, pair)] for m in range(3)]
    attended = hidden.at[pl.ds(3 * pair, pair)]
    normed = grad.at[pl.ds(0, pair)]
    grads_of = [
        grad.at[pl.ds(2 * pair, pair), pl.ds(0, cols)],
        grad.at[pl.ds(2 * pair, pair), pl.ds(cols, cols)],
        grad.at[pl.ds(3 * pair, pair), pl.ds(0, cols)],
    ]
    attended_grad = grad.at[pl.ds(3 * pair, pair), pl.ds(cols, cols)]
    own_rows = mixed_all.at[pl.ds(pl.multiple_of(x * rows, rows), rows)]
    other_rows = mixed_all.at[pl.ds(pl.multiple_of((1 - x) * rows, rows), rows)]
    late = {}

    def tell_beside(which):
        for cond, z in ((net.z > 0, net.z - 1), (net.z < n - 1, net.z + 1)):

            @pl.when(cond)
            def _():
                pl.semaphore_signal(free.at[which], inc=1, device_id=net.device(z=z), device_id_type=MESH)

    def mix_grads():
        backs.finish()
        ffn_sum[...] = jnp.zeros_like(ffn_sum)

        def body(r):
            span = pl.ds(r, 16)
            own = pl.ds(pl.multiple_of((net.z * 2 + x) * rows + r, 16), 16)
            term, gain_term = norm_back(back[net.z, x, span].astype(F32), mixed[span], gains_all[8:9])
            value = grad[own].astype(F32) + term
            input_grad[span] = value
            mixed_all[pl.ds(pl.multiple_of(x * rows + r, 16), 16)] = value.astype(BF16)
            ffn_sum[...] += gain_term[:8] + gain_term[8:]

        loop(rows, 16, body, 4)
        net.send(own_rows, own_rows, x_sems.at[2], net.device(x=1 - x))
        pl.semaphore_signal(free.at[2], inc=1, device_id=net.device(x=1 - x), device_id_type=MESH)
        tell_beside(3)

    def load_out():
        late["out"] = net.local(wa_out.at[3], weights.at[3])

    def load_rest():
        net.settle_tag("grads")
        late["normed"] = net.local(normed_out, normed)
        late["qkv"] = net.local(wa_out.at[pl.ds(0, 3)], weights.at[pl.ds(0, 3)])
        late["parts"] = [net.local(qkv_out.at[m], hidden.at[pl.ds(m * pair, pair)]) for m in range(3)]
        late["attended"] = net.local(attended_out, attended)

    def step_adds():
        if adds.done_z == 0:
            pl.semaphore_wait(free.at[3], beside)
        adds.step_z(adds.done_z)

    def attended_back():
        net.settle(late["out"])
        net.recv(other_rows, x_sems.at[2])

        def body(col):
            span = pl.ds(col, 256)
            attended_grad[:, span] = dot(mixed_all[...], weights[3, :, span]).astype(BF16)

        loop(cols, 256, body, 4)
        tell_beside(4)
        net.settle(late["attended"])

    def heads():
        for load in late["parts"]:
            net.settle(load)
        masks = head_masks()

        def body(col):
            span = pl.ds(col, LANES)
            cosine, sine = tables[0], tables[1]
            queries, key_rows, value_rows = queries_of[:, span], keys_of[:, span], values_of[:, span]
            out_grad = attended_grad[:, span]
            queries2, out_grad2 = both(queries, masks), both(out_grad, masks)
            may = jnp.concatenate([allowed[...], allowed[...]], axis=0)
            probs = softmax(queries2, key_rows, may)
            value_grad = dot(probs.astype(BF16), out_grad2, TN)
            prob_grad = dot(out_grad2, value_rows, NT)
            score_grad = probs * (prob_grad - jnp.sum(probs * prob_grad, axis=-1, keepdims=True))
            score_grad = score_grad.astype(BF16)
            query_grad = pick(dot(score_grad, key_rows), pair) * HD ** (-0.5)
            key_grad = dot(score_grad, queries2, TN) * HD ** (-0.5)
            grads_of[0][:, span] = turn(query_grad, cosine, -sine, lane).astype(BF16)
            grads_of[1][:, span] = turn(key_grad, cosine, -sine, lane).astype(BF16)
            grads_of[2][:, span] = value_grad.astype(BF16)

        loop(cols, LANES, body, 4)
        net.settle(late["normed"])

    def normed_back():
        net.settle(late["qkv"])
        for entry in backs.sent:
            net.settle(entry)

        def body(col):
            span = pl.ds(col, 256)
            term = dot(grads_of[0][...], weights[0, span, :], NT)
            term += dot(grads_of[1][...], weights[1, span, :], NT)
            term += dot(grads_of[2][...], weights[2, span, :], NT)
            back[0, 0, :, span] = term[:rows].astype(BF16)
            back[0, 1, :, span] = term[rows:].astype(BF16)

        loop(width, 256, body, 4)
        net.send(back.at[0, 1 - x], from_x, x_sems.at[3], net.device(x=1 - x))

    def input_back():
        net.recv(from_x, x_sems.at[3])
        gain_sum[...] = jnp.zeros_like(gain_sum)

        def body(r):
            span = pl.ds(r, 16)
            grad_rows = back[0, x, span].astype(F32) + from_x[span].astype(F32)
            term, gain_term = norm_back(grad_rows, residual[span].astype(F32), gains_all[0:1])
            input_grad[span] += term
            gain_sum[...] += gain_term[:8] + gain_term[8:]

        loop(rows, 16, body, 4)
        for i in range(dp):
            gain_to[i, 0:8] = gain_sum[:, i * block : (i + 1) * block]
            gain_to[i, 8:16] = ffn_sum[:, i * block : (i + 1) * block]
        for k in range(1, dp):
            to = (me + k) % dp
            net.send(gain_to.at[to], gain_from.at[me], back_gain_sems.at[me], (to, x))

    def sum_gains():
        total = gain_to[me]
        for k in range(1, dp):
            source = (me + k) % dp
            net.recv(gain_from.at[source], back_gain_sems.at[source])
            total = total + gain_from[source]
        gain_x[0] = total
        net.send(gain_x.at[0], gain_x.at[1], x_sems.at[4], net.device(x=1 - x))

    def block_rows():
        adds.finish()

        def body(r):
            span = pl.ds(r, 16)
            block_out[span] = (mixed[span] + adds.part(net.z, x)[span].astype(F32)).astype(BF16)

        loop(rows, 16, body, 4)

    qkv.start()
    turn_weights()
    out.start()
    send_gains()
    qkv.step(1)
    out.step(1)
    qkv.step(2)
    qkv.cross_step(0)
    out.cross_step(0)
    ffn[0].start()
    mask_grads()
    out.step(2)
    norm()
    grads.start()
    ffn[2].start()
    qkv.cross_step(1)
    qkv.step(3)
    qkv.cross_step(2)
    ffn_step(0, 3)
    out.cross_step(1)
    out.step(3)
    ffn_step(0, 2)
    qkv.cross_step(3)
    project(0)
    ffn_step(0, 1)
    grads.step(1)
    project(1)
    project(2)
    out.cross_step(2)
    project(3)
    ffn[1].start()
    attend()
    out.cross_step(3)
    join()
    mix()
    ffn_rows.start()
    grads.step(2)
    ffn_step(2, 1)
    ffn_step(2, 3)
    ffn_step(1, 1)
    ffn_step(1, 3)
    ffn_step(1, 2)
    ffn_step(2, 2)
    ffn_rows.step(1)
    load_rows(3)
    ffn_cross(1)
    ffn_cross(0)
    grads.step(3)
    ffn_cross(2)
    load_ffn(0)
    load_ffn(2)
    load_rows(2)
    ffn_rows.step(2)
    load_ffn(1)
    forward(3)
    forward(2)
    ffn_rows.step(3)
    load_rows(1)
    forward(1)
    backward(2)
    load_rows(0)
    forward(0)
    ffn_item()
    backward(0)
    red.step_c()
    backward(1)
    ffn_item()
    red.step_y()
    backs.step_x(2)
    ffn_item()
    red.step_c()
    backs.step_x(0)
    backs.step_z(0)
    red.step_c()
    ffn_item()
    ffn_item()
    backward(3)
    red.step_c()
    backs.step_x(1)
    backs.step_z(1)
    backs.step_z(2)
    red.step_c()
    ffn_item()
    ffn_item()
    red.step_y()
    red.step_y()
    red.step_c()
    red.step_c()
    ffn_item()
    ffn_item()
    red.step_c()
    backs.step_x(3)
    red.step_y()
    ffn_item()
    red.step_y()
    mix_grads()
    red.step_c()
    red.step_c()
    for _ in range(3):
        red.step_y()
    ffn_item()
    ffn_item()
    red.step_y()
    add_chunk(0)
    add_chunk(1)
    red.step_c()
    add_chunk(2)
    load_out()
    add_chunk(3)
    load_rest()
    red.step_y()
    attended_back()
    heads()
    red.step_c()
    attention_item()
    adds.step_x(adds.done_x)
    red.step_y()
    red.step_c()
    step_adds()
    attention_item()
    red.step_c()
    attention_item()
    adds.step_x(adds.done_x)
    for _ in range(3):
        attention_item()
    red.step_c()
    red.step_y()
    attention_item()
    red.step_c()
    attention_item()
    pl.semaphore_wait(free.at[4], beside)
    step_adds()
    red.step_c()
    red.step_y()
    red.step_z()
    red.step_c()
    red.step_c()
    attention_item()
    normed_back()
    red.step_y()
    red.step_z()
    red.step_c()
    red.step_y()
    adds.step_x(adds.done_x)
    attention_item()
    step_adds()
    red.step_y()
    red.step_z()
    red.step_c()
    red.step_y()
    attention_item()
    red.step_y()
    red.step_y()
    red.step_z()
    input_back()
    red.step_y()
    red.step_z()
    red.step_c()
    attention_item()
    red.step_c()
    red.step_z()
    red.step_y()
    adds.step_x(adds.done_x)
    red.step_z()
    red.step_y()
    red.step_c()
    attention_item()
    red.step_c()
    red.step_z()
    red.step_y()
    sum_gains()
    red.step_z()
    attention_item()
    red.step_c()
    attention_item()
    red.step_z()
    red.step_z()
    red.step_y()
    attention_item()
    red.step_z()
    red.step_y()
    red.step_c()
    red.step_z()
    step_adds()
    red.step_c()
    red.step_y()
    red.step_y()
    red.step_z()
    red.step_z()
    red.step_y()
    block_rows()
    red.step_z()
    assert red.done_y == red.done_z == red.total and adds.done_z == n and backs.done_x == n
    net.recv(gain_x.at[1], x_sems.at[4])
    gain_out[...] = gain_x[0] + gain_x[1]
    red.finish()
    net.drain()


def finish_kernel(ffn, attention, gains, qkv_grad, out_grad, gate_up_grad, down_grad, gain_sums):
    q, n = pl.program_id(0), pl.num_programs(0)
    z = lax.axis_index("dp") // 4
    gate_up_grad[...] = ffn[0:2, 0].astype(F32)
    down_grad[...] = ffn[2, 0].astype(F32).T
    total = attention[0, 2].astype(F32)
    total += jnp.where(z > 0, attention[0, 0].astype(F32), 0.0)
    total += jnp.where(z < n - 1, attention[0, 1].astype(F32), 0.0)

    @pl.when(q < 3)
    def _():
        qkv_grad[0] = total

    @pl.when(q == 3)
    def _():
        out_grad[...] = total.T

    gain_sums[0:1] = jnp.sum(gains[0:8], axis=0, keepdims=True)
    gain_sums[1:2] = jnp.sum(gains[8:16], axis=0, keepdims=True)


def call(kernel, collective_id, sends, locals_, vmem, outs, out_specs, scratch, sems, flags=0):
    def typed(entry):
        return (entry[:-1], F32) if entry[-1] is F32 else (entry, BF16)

    dma = pltpu.SemaphoreType.DMA
    return lambda in_specs, *args: pl.pallas_call(
        kernel,
        out_shape=[jax.ShapeDtypeStruct(*typed(entry)) for entry in outs],
        in_specs=in_specs,
        out_specs=out_specs,
        scratch_shapes=[pltpu.VMEM(*typed(entry)) for entry in scratch] + [dma((sends,)), dma((locals_,))] + [dma(entry) for entry in sems] + [pltpu.SemaphoreType.REGULAR((flags,))] * (flags > 0),
        compiler_params=pltpu.CompilerParams(collective_id=collective_id, has_side_effects=True, vmem_limit_bytes=vmem),
    )(*args)


def shards(dp, residual, seg_ids, attn_gain, w_qkv, w_out, ffn_gain, w_gate_up, w_down, cotangent):
    n = dp // 4
    rows, width = residual.shape
    group = seg_ids.shape[0]
    block, cols = w_qkv.shape[1:]
    part = w_gate_up.shape[2] // n
    pairs = jnp.arange(LANES, dtype=jnp.int32) % (HD // 2)
    freq = (ROPE_BASE ** (-(pairs.astype(F32) * 2.0 / HD)))[None]

    every = n * 2 * rows
    slots = SLOTS
    layer = call(
        functools.partial(layer_kernel, dp), 1, 320, 112, LIMIT,
        [
            (3, n, block, part), (4, 3, block, cols), (4, width, cols), (3, width, part), (n, 2, rows, width),
            (group, width), (group, cols), (3, group, cols), (rows, width), (rows, width, F32), (16, block, F32),
        ],
        [ANY] * 8 + [VM] * 3,
        [
            (4, width, cols), (every, width), (every, part), (every, 2 * part),
            (n, 2, rows, width), (n, rows, width), (n + 1, rows, width),
            (slots, 2, 2, block, part), (slots, 2, block, part), (slots, block, part),
            (group, width), (rows, width), (group, 3 * cols, F32), (rows, width, F32), (2, group, LANES, F32),
            (group, group, F32), (16, block, F32), (dp, 16, block, F32), (16, width, F32),
            (8, width, F32), (8, width, F32), (dp, 16, block, F32), (dp, 16, block, F32), (2, 16, block, F32),
        ],
        [
            (dp,), (4, n), (4, n), (3, 4, n), (2, n), (2, n), (5,),
            (n,), (n + 1,), (slots,), (slots,), (3, n), (4, n + 2), (dp,),
        ],
        5,
    )
    outputs = layer(
        [VM] * 7 + [ANY] * 3, residual, seg_ids[None], attn_gain[None], ffn_gain[None], freq, w_out, w_down, w_qkv,
        w_gate_up, cotangent,
    )
    result, totals, block_out, input_grad, gain_grads = outputs[0], outputs[1], outputs[8], outputs[9], outputs[10]
    qkv_grad, out_grad, gate_up_grad, down_grad, gain_sums = pl.pallas_call(
        finish_kernel,
        grid=(n,),
        out_shape=[
            jax.ShapeDtypeStruct(entry, F32)
            for entry in ((3, block, cols), (cols, block), (2, block, n * part), (n * part, block), (2, block))
        ],
        in_specs=[
            pl.BlockSpec((3, 1, block, part), lambda q: (0, q, 0, 0)),
            pl.BlockSpec((1, 3, block, cols), lambda q: (q, 0, 0, 0)),
            pl.BlockSpec((16, block), lambda q: (0, 0)),
        ],
        out_specs=[
            pl.BlockSpec((1, block, cols), lambda q: (jnp.minimum(q, 2), 0, 0)),
            pl.BlockSpec((cols, block), lambda q: (0, 0)),
            pl.BlockSpec((2, block, part), lambda q: (0, 0, q)),
            pl.BlockSpec((part, block), lambda q: (q, 0)),
            pl.BlockSpec((2, block), lambda q: (0, 0)),
        ],
        compiler_params=pltpu.CompilerParams(vmem_limit_bytes=LIMIT),
    )(result, totals, gain_grads)
    return block_out, input_grad, gain_sums[0], qkv_grad, out_grad, gain_sums[1], gate_up_grad, down_grad


def positions(segments):
    row_index = jnp.arange(segments.shape[1], dtype=jnp.int32)[None, :]
    previous = jnp.concatenate([segments[:, :1] - 1, segments[:, :-1]], axis=1)
    run_start = lax.cummax(jnp.where(segments != previous, row_index, 0), axis=1)
    return row_index - run_start


def rope_tables(places, head_dim):
    half_dim = head_dim // 2
    frequency = ROPE_BASE ** (-(jnp.arange(half_dim, dtype=jnp.float32) * 2.0 / head_dim))
    angles = places.astype(jnp.float32)[:, None, None] * frequency[None, None, :]
    return (jnp.cos(angles), jnp.sin(angles))


def rotate(field, cosine, sine_table):
    half_dim = field.shape[-1] // 2
    lower_half = field[..., :half_dim]
    upper_half = field[..., half_dim:]
    return jnp.concatenate(
        [
            lower_half * cosine - upper_half * sine_table,
            upper_half * cosine + lower_half * sine_table,
        ],
        axis=-1,
    )


def unrotate(field, cosine, sine_table):
    half_dim = field.shape[-1] // 2
    lower_half = field[..., :half_dim]
    upper_half = field[..., half_dim:]
    return jnp.concatenate(
        [
            lower_half * cosine + upper_half * sine_table,
            upper_half * cosine - lower_half * sine_table,
        ],
        axis=-1,
    )


def attention_scores(queries, key_rows, allowed):
    scores = jnp.einsum(
        "qhd,khd->hqk", queries, key_rows, preferred_element_type=jnp.float32
    ) * queries.shape[-1] ** (-0.5)
    return jnp.where(allowed[None], scores, -1e30)


def plain_shards(residual_in, seg_ids, attn_gain, w_qkv, w_out, ffn_gain, w_gate_up, w_down, cotangent):
    rows_local = residual_in.shape[0]
    group_rows = seg_ids.shape[0]
    offset = lax.axis_index("tensor") * rows_local
    live_rows = (lax.dynamic_slice_in_dim(seg_ids, offset, rows_local) >= 0).astype(jnp.float32)
    residual = residual_in.astype(jnp.float32)
    contract_rows = (((0,), (0,)), ((), ()))
    contract_cols = (((1,), (1,)), ((), ()))
    gain_attn, qkv_full, out_full = (
        lax.all_gather(attn_gain, "dp", axis=0, tiled=True),
        lax.all_gather(w_qkv, "dp", axis=1, tiled=True),
        lax.all_gather(w_out, "dp", axis=1, tiled=True),
    )
    norm_attn = lax.rsqrt(jnp.mean(residual * residual, axis=-1, keepdims=True) + EPSILON)
    unit_attn = residual * norm_attn
    normed = (unit_attn * gain_attn.astype(jnp.float32)).astype(jnp.bfloat16)
    normed_all = lax.all_gather(normed, "tensor", axis=0, tiled=True)
    projected = jnp.einsum("rd,cde->cre", normed_all, qkv_full, preferred_element_type=jnp.float32)
    head_count = qkv_full.shape[2] // HD
    head_shape = (group_rows, head_count, HD)
    cosine, sine_table = rope_tables(positions(seg_ids[None, :])[0], HD)
    queries = rotate(projected[0].reshape(head_shape), cosine, sine_table).astype(jnp.bfloat16)
    key_rows = rotate(projected[1].reshape(head_shape), cosine, sine_table).astype(jnp.bfloat16)
    value_rows = projected[2].reshape(head_shape).astype(jnp.bfloat16)
    row_index = jnp.arange(group_rows)
    allowed = (seg_ids[:, None] == seg_ids[None, :]) & (row_index[:, None] >= row_index[None, :])
    scores = attention_scores(queries, key_rows, allowed)
    row_top = jnp.max(scores, axis=-1, keepdims=True)
    log_total = row_top + jnp.log(jnp.sum(jnp.exp(scores - row_top), axis=-1, keepdims=True))
    weights = jnp.exp(scores - log_total).astype(jnp.bfloat16)
    attended = jnp.einsum("hqk,khd->qhd", weights, value_rows, preferred_element_type=jnp.float32)
    attended = attended.reshape(group_rows, head_count * HD).astype(jnp.bfloat16)
    mixed = residual + lax.psum_scatter(
        jnp.dot(attended, out_full, preferred_element_type=jnp.float32),
        "tensor",
        scatter_dimension=0,
        tiled=True,
    )
    gain_ffn, gate_up_full, down_full = (
        lax.all_gather(ffn_gain, "dp", axis=0, tiled=True),
        lax.all_gather(w_gate_up, "dp", axis=1, tiled=True),
        lax.all_gather(w_down, "dp", axis=1, tiled=True),
    )
    norm_ffn = lax.rsqrt(jnp.mean(mixed * mixed, axis=-1, keepdims=True) + EPSILON)
    unit_ffn = mixed * norm_ffn
    normed_ffn = (unit_ffn * gain_ffn.astype(jnp.float32)).astype(jnp.bfloat16)
    normed_ffn_all = lax.all_gather(normed_ffn, "tensor", axis=0, tiled=True)
    gate_up = jnp.einsum(
        "rd,cde->cre", normed_ffn_all, gate_up_full, preferred_element_type=jnp.float32
    )
    gate_pre = gate_up[0]
    up_pre = gate_up[1]
    sigmoid_gate = jax.nn.sigmoid(gate_pre)
    activated = gate_pre * sigmoid_gate
    hidden = (activated * up_pre).astype(jnp.bfloat16)
    output = mixed + lax.psum_scatter(
        jnp.dot(hidden, down_full, preferred_element_type=jnp.float32).astype(jnp.bfloat16),
        "tensor",
        scatter_dimension=0,
        tiled=True,
    ).astype(jnp.float32)
    grad_out = cotangent.astype(jnp.float32) * live_rows[:, None]
    grad_all = lax.all_gather(grad_out.astype(jnp.bfloat16), "tensor", axis=0, tiled=True)
    down_grad = lax.dot_general(hidden, grad_all, contract_rows, preferred_element_type=jnp.float32)
    hidden_grad = lax.dot_general(
        grad_all, down_full, contract_cols, preferred_element_type=jnp.float32
    )
    gate_grads = jnp.stack(
        [
            hidden_grad * up_pre * sigmoid_gate * (1.0 + gate_pre * (1.0 - sigmoid_gate)),
            hidden_grad * activated,
        ]
    ).astype(jnp.bfloat16)
    gate_up_grad = jnp.einsum(
        "rd,cre->cde", normed_ffn_all, gate_grads, preferred_element_type=jnp.float32
    )
    normed_ffn_grad = lax.psum_scatter(
        jnp.einsum("cre,cde->rd", gate_grads, gate_up_full, preferred_element_type=jnp.float32),
        "tensor",
        scatter_dimension=0,
        tiled=True,
    )
    ffn_gain_part = jnp.sum(normed_ffn_grad * unit_ffn, axis=0)
    scaled_ffn = normed_ffn_grad * gain_ffn.astype(jnp.float32)
    mixed_grad = grad_out + norm_ffn * (
        scaled_ffn - unit_ffn * jnp.mean(scaled_ffn * unit_ffn, axis=-1, keepdims=True)
    )
    mixed_all = lax.all_gather(mixed_grad.astype(jnp.bfloat16), "tensor", axis=0, tiled=True)
    out_grad = lax.dot_general(
        attended, mixed_all, contract_rows, preferred_element_type=jnp.float32
    )
    attended_grad = lax.dot_general(
        mixed_all, out_full, contract_cols, preferred_element_type=jnp.float32
    )
    attended_grad = attended_grad.astype(jnp.bfloat16).reshape(head_shape)
    probabilities = jnp.exp(attention_scores(queries, key_rows, allowed) - log_total)
    value_grad = jnp.einsum(
        "hqk,qhd->khd",
        probabilities.astype(jnp.bfloat16),
        attended_grad,
        preferred_element_type=jnp.float32,
    )
    prob_grad = jnp.einsum(
        "qhd,khd->hqk", attended_grad, value_rows, preferred_element_type=jnp.float32
    )
    score_grad = (
        probabilities * (prob_grad - jnp.sum(probabilities * prob_grad, axis=-1, keepdims=True))
    ).astype(jnp.bfloat16)
    scale_factor = HD ** (-0.5)
    query_grad = (
        jnp.einsum("hqk,khd->qhd", score_grad, key_rows, preferred_element_type=jnp.float32)
        * scale_factor
    )
    key_grad = (
        jnp.einsum("hqk,qhd->khd", score_grad, queries, preferred_element_type=jnp.float32)
        * scale_factor
    )
    qkv_grads = jnp.stack(
        [
            unrotate(query_grad, cosine, sine_table),
            unrotate(key_grad, cosine, sine_table),
            value_grad,
        ]
    )
    qkv_grads = qkv_grads.reshape(3, group_rows, head_count * HD).astype(jnp.bfloat16)
    qkv_grad = jnp.einsum("rd,cre->cde", normed_all, qkv_grads, preferred_element_type=jnp.float32)
    normed_grad = lax.psum_scatter(
        jnp.einsum("cre,cde->rd", qkv_grads, qkv_full, preferred_element_type=jnp.float32),
        "tensor",
        scatter_dimension=0,
        tiled=True,
    )
    attn_gain_part = jnp.sum(normed_grad * unit_attn, axis=0)
    scaled_attn = normed_grad * gain_attn.astype(jnp.float32)
    input_grad = mixed_grad + norm_attn * (
        scaled_attn - unit_attn * jnp.mean(scaled_attn * unit_attn, axis=-1, keepdims=True)
    )
    (
        query_total,
        key_total,
        value_total,
        out_total,
        attn_gain_total,
        gate_total,
        up_total,
        down_total,
        ffn_gain_total,
    ) = (
        lax.psum_scatter(qkv_grad[0], "dp", scatter_dimension=0, tiled=True),
        lax.psum_scatter(qkv_grad[1], "dp", scatter_dimension=0, tiled=True),
        lax.psum_scatter(qkv_grad[2], "dp", scatter_dimension=0, tiled=True),
        lax.psum_scatter(out_grad, "dp", scatter_dimension=1, tiled=True),
        lax.psum_scatter(attn_gain_part, "dp", scatter_dimension=0, tiled=True),
        lax.psum_scatter(gate_up_grad[0], "dp", scatter_dimension=0, tiled=True),
        lax.psum_scatter(gate_up_grad[1], "dp", scatter_dimension=0, tiled=True),
        lax.psum_scatter(down_grad, "dp", scatter_dimension=1, tiled=True),
        lax.psum_scatter(ffn_gain_part, "dp", scatter_dimension=0, tiled=True),
    )
    gate_up_total = jnp.stack([gate_total, up_total])
    qkv_total = jnp.stack([query_total, key_total, value_total])
    attn_gain_sum, ffn_gain_sum = lax.psum((attn_gain_total, ffn_gain_total), "tensor")
    return (
        output.astype(jnp.bfloat16),
        input_grad,
        attn_gain_sum,
        qkv_total,
        out_total,
        ffn_gain_sum,
        gate_up_total,
        down_total,
    )


def solution(mesh):
    in_specs = (
        P(("dp", "tensor"), None),
        P("dp"),
        P("dp"),
        P(None, "dp", "tensor"),
        P("tensor", "dp"),
        P("dp"),
        P(None, "dp", "tensor"),
        P("tensor", "dp"),
        P(("dp", "tensor"), None),
    )
    out_specs = (
        P(("dp", "tensor"), None),
        P(("dp", "tensor"), None),
        P("dp"),
        P(None, "dp", "tensor"),
        P("tensor", "dp"),
        P("dp"),
        P(None, "dp", "tensor"),
        P("tensor", "dp"),
    )
    dp = mesh.shape["dp"]
    local = functools.partial(shards, dp) if dp == 16 else plain_shards
    return jax.shard_map(local, mesh=mesh, in_specs=in_specs, out_specs=out_specs, check_vma=False)
```

```python
import functools

import jax
import jax.numpy as jnp
import numpy as np
from jax import lax
from jax.experimental import pallas as pl
from jax.experimental.pallas import tpu as pltpu
from jax.sharding import PartitionSpec as P

HD = 64
EPSILON = 1e-05
ROPE_BASE = 130000.0
MESH = pl.DeviceIdType.MESH
ANY = pl.BlockSpec(memory_space=pl.ANY)
VM = pl.BlockSpec(memory_space=pltpu.VMEM)
F32 = jnp.float32
BF16 = jnp.bfloat16
LANES = 128
SLOTS = 9
LIMIT = 66977792
NT = (((1,), (1,)), ((), ()))
TN = (((0,), (0,)), ((), ()))
NN = (((1,), (0,)), ((), ()))


def dot(a, b, dims=NN):
    return lax.dot_general(a, b, dims, preferred_element_type=F32)


def when(cond, action):
    if cond is None:
        action()
    else:
        pl.when(cond)(action)


class Net:
    def __init__(self, dp, send_sems, local_sems):
        self.n = dp // 4
        self.dp_index = lax.axis_index("dp")
        self.x = lax.axis_index("tensor")
        self.z = self.dp_index // 4
        self.y = (self.dp_index // 2) % 2
        self.c = self.dp_index % 2
        self.send_sems = send_sems
        self.local_sems = local_sems
        self.sent = 0
        self.moved = 0
        self.pending = []
        self.kept = []
        self.tags = {}

    def place(self, z, y, c):
        return (z * 2 + y) * 2 + c

    def device(self, z=None, y=None, c=None, x=None):
        z = self.z if z is None else z
        y = self.y if y is None else y
        c = self.c if c is None else c
        x = self.x if x is None else x
        return (self.place(z, y, c), x)

    def greet(self, devices):
        barrier = pltpu.get_barrier_semaphore()
        for device in devices:
            pl.semaphore_signal(barrier, inc=1, device_id=device, device_id_type=MESH)
        pl.semaphore_wait(barrier, len(devices))

    def send(self, src, dst, recv_sem, device, cond=None):
        sem = self.send_sems.at[self.sent]
        self.sent += 1
        copy = pltpu.make_async_remote_copy(
            src_ref=src, dst_ref=dst, send_sem=sem, recv_sem=recv_sem, device_id=device, device_id_type=MESH
        )
        when(cond, copy.start)
        self.pending.append((cond, copy))
        return self.pending[-1]

    def recv(self, dst, recv_sem):
        pltpu.make_async_remote_copy(
            src_ref=dst, dst_ref=dst, send_sem=self.send_sems.at[0], recv_sem=recv_sem,
            device_id=self.device(c=1 - self.c), device_id_type=MESH,
        ).wait_recv()

    def local(self, src, dst, cond=None):
        sem = self.local_sems.at[self.moved]
        self.moved += 1
        copy = pltpu.make_async_copy(src, dst, sem)
        when(cond, copy.start)
        self.kept.append((cond, copy))
        return self.kept[-1]

    def settle(self, entry):
        for entries, wait in ((self.kept, "wait"), (self.pending, "wait_send")):
            for k, known in enumerate(entries):
                if known is entry:
                    when(entry[0], getattr(entry[1], wait))
                    del entries[k]
                    return

    def tag(self, name, entries):
        self.tags.setdefault(name, []).extend(entries)

    def settle_tag(self, *names):
        for name in names:
            for entry in self.tags.pop(name, ()):
                self.settle(entry)

    def drain(self):
        assert self.sent <= self.send_sems.shape[0] and self.moved <= self.local_sems.shape[0]
        for cond, copy in self.pending:
            when(cond, copy.wait_send)
        for cond, copy in self.kept:
            when(cond, copy.wait)


class Gather:
    def __init__(self, net, own, at, sems, tag):
        self.net, self.own, self.at, self.tag = net, own, at, tag
        self.sems = sems

    def spread(self, block, src, ysend=True):
        net = self.net
        here = net.place(block, net.y, net.c)
        net.tag(self.tag, [net.send(src, self.at(here), self.sems.at[1, block], net.device(y=1 - net.y))])
        net.tag(self.tag, [net.send(src, self.at(here), self.sems.at[2 + net.y, block], net.device(c=1 - net.c))])

    def start(self):
        net = self.net
        here = self.at(net.dp_index)
        net.tag(self.tag, [net.send(self.own, here, self.sems.at[0, net.z], net.device(z=net.z + 1), net.z < net.n - 1)])
        net.tag(self.tag, [net.send(self.own, here, self.sems.at[0, net.z], net.device(z=net.z - 1), net.z > 0)])
        self.spread(net.z, self.own)
        self.kept = net.local(self.own, here)

    def step(self, s):
        net = self.net
        for sign in (1, -1):
            block = net.z - s * sign
            valid = jnp.logical_and(block >= 0, block < net.n)
            nxt = net.z + sign
            more = jnp.logical_and(nxt >= 0, nxt < net.n)
            here = self.at(net.place(block, net.y, net.c))

            @pl.when(valid)
            def _():
                net.recv(here, self.sems.at[0, block])

            net.tag(self.tag, [net.send(here, here, self.sems.at[0, block], net.device(z=nxt), jnp.logical_and(valid, more))])
            net.tag(self.tag, [net.send(here, here, self.sems.at[1, block], net.device(y=1 - net.y), valid)])
            net.tag(self.tag, [net.send(here, here, self.sems.at[2 + net.y, block], net.device(c=1 - net.c), valid)])

    def cross(self, block):
        net = self.net
        there = self.at(net.place(block, 1 - net.y, net.c))
        net.recv(there, self.sems.at[1, block])
        net.tag(self.tag, [net.send(there, there, self.sems.at[3 - net.y, block], net.device(c=1 - net.c))])

    def cross_step(self, s):
        net = self.net
        if s == 0:
            self.cross(net.z)
            return
        for sign in (1, -1):
            block = net.z - s * sign
            valid = jnp.logical_and(block >= 0, block < net.n)
            there = self.at(net.place(block, 1 - net.y, net.c))

            @pl.when(valid)
            def _():
                net.recv(there, self.sems.at[1, block])

            net.tag(self.tag, [net.send(there, there, self.sems.at[3 - net.y, block], net.device(c=1 - net.c), valid)])

    def finish(self, block):
        net = self.net
        for y in (0, 1):
            net.recv(self.at(net.place(block, y, 1 - net.c)), self.sems.at[2 + y, block])


class Exchange:
    def __init__(self, net, part, at, sems, tag):
        self.net, self.part, self.at, self.tag = net, part, at, tag
        self.sems = sems

    def start(self):
        net = self.net
        here = self.at(net.dp_index)
        for d in list(range(1, net.n)):
            to = (net.z + d) % net.n
            net.tag(self.tag, [net.send(self.part(to), here, self.sems.at[0, net.z], net.device(z=to))])
        own = self.part(net.z)
        net.tag(self.tag, [net.send(own, here, self.sems.at[1, net.z], net.device(y=1 - net.y))])
        net.tag(self.tag, [net.send(own, here, self.sems.at[2 + net.y, net.z], net.device(c=1 - net.c))])
        self.kept = net.local(own, here)

    def step(self, block):
        net = self.net
        here = self.at(net.place(block, net.y, net.c))
        net.recv(here, self.sems.at[0, block])
        net.send(here, here, self.sems.at[1, block], net.device(y=1 - net.y))
        net.send(here, here, self.sems.at[2 + net.y, block], net.device(c=1 - net.c))

    def cross(self, block):
        net = self.net
        there = self.at(net.place(block, 1 - net.y, net.c))
        net.recv(there, self.sems.at[1, block])
        net.send(there, there, self.sems.at[3 - net.y, block], net.device(c=1 - net.c))

    finish = Gather.finish


class Rows:
    def __init__(self, net, own, at, sems, tag):
        self.net, self.own, self.at, self.tag = net, own, at, tag
        self.sems = sems

    def start(self):
        net = self.net
        here = self.at(net.z, net.x)
        own = here if self.own is None else self.own
        net.tag(self.tag, [net.send(own, here, self.sems.at[0, net.z], net.device(z=net.z + 1), net.z < net.n - 1)])
        net.tag(self.tag, [net.send(own, here, self.sems.at[0, net.z], net.device(z=net.z - 1), net.z > 0)])
        net.tag(self.tag, [net.send(own, here, self.sems.at[1, net.z], net.device(x=1 - net.x))])
        if self.own is not None:
            net.tag(self.tag + "_kept", [net.local(own, here)])

    def step(self, s):
        net = self.net
        forwarded = []
        for sign in (1, -1):
            block = net.z - s * sign
            valid = jnp.logical_and(block >= 0, block < net.n)
            nxt = net.z + sign
            more = jnp.logical_and(nxt >= 0, nxt < net.n)
            here = self.at(block, net.x)

            @pl.when(valid)
            def _():
                net.recv(here, self.sems.at[0, block])

            forwarded.append(net.send(here, here, self.sems.at[0, block], net.device(z=nxt), jnp.logical_and(valid, more)))
            forwarded.append(net.send(here, here, self.sems.at[1, block], net.device(x=1 - net.x), valid))
        if self.own is None:
            net.tag(self.tag, forwarded)

    def finish(self, block):
        net = self.net
        net.recv(self.at(block, 1 - net.x), self.sems.at[1, block])


class Reduce:
    def __init__(self, net, part, from_c, from_y, result, line, sems, total):
        self.net, self.part, self.from_c, self.from_y = net, part, from_c, from_y
        self.result, self.totals = result
        self.line = line
        self.cs, self.ys, self.zs, self.ls, self.free = sems
        self.slots = part.shape[0]
        self.total = total
        self.items = []
        self.out = {}
        self.done_c = self.done_y = self.done_z = 0

    def add(self, total, term):
        def body(r):
            span = pl.ds(r, 16)
            total[span] = (total[span].astype(F32) + term[span].astype(F32)).astype(BF16)

        loop(total.shape[0], 16, body, 8)

    def credit(self, which, device):
        pl.semaphore_signal(self.free.at[which], inc=1, device_id=device, device_id_type=MESH)

    def item(self, matrix, to, left, right, depth, block):
        net = self.net
        i = len(self.items)
        slot = i % self.slots
        self.items.append((matrix, to))
        assert self.done_z > i - self.slots
        for entry in self.out.pop(i - self.slots, ()):
            net.settle(entry)

        def body(col):
            term = dot(left, right[:, pl.ds(col, 256)], TN).astype(BF16)
            for y in (0, 1):
                for c in (0, 1):
                    at = (y * 2 + c) * block
                    self.part[slot, c, y, :, pl.ds(col, 256)] = term[at : at + block]

        loop(right.shape[1], 256, body, 4)
        if i >= self.slots:
            pl.semaphore_wait(self.free.at[0], 1)
        self.out[i] = [
            net.send(self.part.at[slot, 1 - net.c], self.from_c.at[slot], self.cs.at[slot], net.device(c=1 - net.c))
        ]

    def step_c(self):
        net = self.net
        i = self.done_c
        self.done_c += 1
        slot = i % self.slots
        net.recv(self.from_c.at[slot], self.cs.at[slot])
        for y in (0, 1):
            self.add(self.part.at[slot, net.c, y], self.from_c.at[slot, y])
        if i + self.slots < self.total:
            self.credit(0, net.device(c=1 - net.c))
        if i >= self.slots:
            pl.semaphore_wait(self.free.at[1], 1)
        self.out[i].append(
            net.send(self.part.at[slot, net.c, 1 - net.y], self.from_y.at[slot], self.ys.at[slot], net.device(y=1 - net.y))
        )

    def step_y(self):
        net = self.net
        i = self.done_y
        self.done_y += 1
        slot = i % self.slots
        matrix, to = self.items[i]
        net.recv(self.from_y.at[slot], self.ys.at[slot])
        self.add(self.part.at[slot, net.c, net.y], self.from_y.at[slot])
        if i + self.slots < self.total:
            self.credit(1, net.device(y=1 - net.y))
        matrices = self.result.shape[0]
        if matrix >= matrices:
            return
        src = self.part.at[slot, net.c, net.y]
        dst = self.result.at[matrix, net.z]
        away = to != net.z
        self.out[i].append(net.send(src, dst, self.zs.at[matrix, net.z], net.device(z=to), away))
        self.out[i].append(net.local(src, dst, jnp.logical_not(away)))
        self.done_z += 1

    def step_z(self):
        net = self.net
        i = self.done_z
        self.done_z += 1
        assert i < self.done_y
        matrix, to = self.items[i]
        m = matrix - self.result.shape[0]
        total = self.part.at[i % self.slots, net.c, net.y]
        behind = jnp.where(to > net.z, net.z > 0, net.z < net.n - 1)
        place = self.line(m, to)

        @pl.when(jnp.logical_and(to != net.z, behind))
        def _():
            net.recv(place, self.ls.at[m, to])
            self.add(total, place)

        side = jnp.where(to > net.z, 0, 1)
        nxt = jnp.where(to > net.z, net.z + 1, net.z - 1)
        there = net.device(z=nxt)
        last = jnp.logical_and(to != net.z, to == nxt)
        self.out[i].append(net.send(total, place, self.ls.at[m, to], there, jnp.logical_and(to != net.z, to != nxt)))
        self.out[i].append(net.send(total, self.totals.at[m, side], self.ls.at[m, net.n + side], there, last))
        self.out[i].append(net.local(total, self.totals.at[m, 2], to == net.z))

    def finish(self):
        net = self.net
        for matrix in range(self.result.shape[0]):
            for d in range(1, net.n):
                block = (net.z + d) % net.n
                net.recv(self.result.at[matrix, block], self.zs.at[matrix, block])
        for m in range(self.totals.shape[0]):
            for side, cond in ((0, net.z > 0), (1, net.z < net.n - 1)):

                @pl.when(cond)
                def _():
                    net.recv(self.totals.at[m, side], self.ls.at[m, net.n + side])


def loop(total, step, body, unroll):
    @pl.loop(0, total // step, unroll=unroll)
    def _(i):
        body(pl.multiple_of(i * step, step))


def turn(field, cosine, sine, lane):
    half = HD // 2
    partner = jnp.where(lane % HD < half, pltpu.roll(field, LANES - half, 1), pltpu.roll(field, half, 1))
    return field * cosine + partner * sine


def head_masks():
    lane = lax.broadcasted_iota(jnp.int32, (1, LANES), 1)
    return (lane < HD).astype(BF16), (lane >= HD).astype(BF16)


def both(field, masks):
    return jnp.concatenate([field * masks[0], field * masks[1]], axis=0)


def pick(stacked, rows):
    lane = lax.broadcasted_iota(jnp.int32, (1, LANES), 1)
    return jnp.where(lane < HD, stacked[:rows], stacked[rows:])


def softmax(queries2, key_rows, allowed):
    scores = dot(queries2, key_rows, NT) * HD ** (-0.5)
    scores = jnp.where(allowed > 0, scores, -1e30)
    raised = jnp.exp(scores - jnp.max(scores, axis=-1, keepdims=True))
    return raised / jnp.sum(raised, axis=-1, keepdims=True)


def far_first(net):
    n = net.n
    table = [sorted(range(n), key=lambda b: (-abs(b - z), -b)) for z in range(n)]
    return [sum(jnp.where(net.z == z, table[z][k], 0) for z in range(n)) for k in range(n)]


class RowSum:
    def __init__(self, net, order, part, from_x, from_z, sems):
        self.net, self.order, self.part, self.from_x, self.from_z = net, order, part, from_x, from_z
        self.xs, self.zs = sems
        self.sent = []
        self.done_x = self.done_z = 0

    def start(self, b):
        net = self.net
        self.sent.append(
            net.send(self.part(b, 1 - net.x), self.from_x.at[b], self.xs.at[b], net.device(x=1 - net.x))
        )

    def add(self, total, term):
        def body(r):
            span = pl.ds(r, 16)
            total[span] = (total[span].astype(F32) + term[span].astype(F32)).astype(BF16)

        loop(total.shape[0], 16, body, 8)

    def step_x(self, k):
        net = self.net
        b = self.order[k]
        self.done_x += 1
        net.recv(self.from_x.at[b], self.xs.at[b])
        self.add(self.part(b, net.x), self.from_x.at[b])

    def step_z(self, k):
        net = self.net
        b = self.order[k]
        self.done_z += 1
        total = self.part(b, net.x)
        behind = jnp.where(b > net.z, net.z > 0, net.z < net.n - 1)

        @pl.when(jnp.logical_and(b != net.z, behind))
        def _():
            net.recv(self.from_z.at[b], self.zs.at[b])
            self.add(total, self.from_z.at[b])

        slot = jnp.where(b == net.z - 1, net.n, b)
        to = jnp.where(b > net.z, net.z + 1, net.z - 1)
        self.sent.append(net.send(total, self.from_z.at[slot], self.zs.at[slot], net.device(z=to), b != net.z))

    def finish(self):
        net = self.net
        total = self.part(net.z, net.x)
        for slot, cond in ((net.z, net.z > 0), (net.n, net.z < net.n - 1)):

            @pl.when(cond)
            def _():
                net.recv(self.from_z.at[slot], self.zs.at[slot])
                self.add(total, self.from_z.at[slot])


def norm_back(grad, value, gain):
    scale = lax.rsqrt(jnp.mean(value * value, axis=-1, keepdims=True) + EPSILON)
    unit = value * scale
    scaled = grad * gain
    back = scale * (scaled - unit * jnp.mean(scaled * unit, axis=-1, keepdims=True))
    return back, grad * unit


def layer_kernel(
    dp,
    residual, seg, attn_gain, ffn_gain, freq, w_out, w_down, w_qkv, w_gate_up, cotangent,
    result, totals, wa_out, wf_out, normed_ffn_out, normed_out, attended_out, qkv_out, block_out, input_grad, gain_out,
    weights, grad, hidden, gate_up_grad, back, back_x, back_z, part, from_c, from_y,
    mixed_all, from_x, pre, mixed, tables, allowed, gains, all_gains, gains_all, gain_sum, ffn_sum, gain_to,
    gain_from, gain_x,
    send_sems, local_sems, gain_sems, q_sems, o_sems, f_sems, g_sems, n_sems, x_sems,
    bx_sems, bz_sems, rc_sems, ry_sems, rz_sems, rl_sems, back_gain_sems, free,
):
    net = Net(dp, send_sems, local_sems)
    n, me, x = net.n, net.dp_index, net.x
    rows, width = residual.shape
    block, cols = w_qkv.shape[1:]
    group = pair = 2 * rows
    every = grad.shape[0]
    depth = width // n
    assert w_gate_up.shape[2] == n * cols and width == 2 * cols and width == 2 * every and width == dp * block
    lane = lax.broadcasted_iota(jnp.int32, (group, LANES), 1)
    live = gain_to
    assert gain_to.shape == (group // 16, 16, LANES)
    order = far_first(net)
    beside = jnp.where(net.z > 0, 1, 0) + jnp.where(net.z < n - 1, 1, 0)
    net.greet([((me + k) % dp, x) for k in range(1, dp)] + [(me, 1 - x)])

    def block_rows_of(z, half):
        return pl.ds(pl.multiple_of((z * 2 + half) * rows, rows), rows)

    normed_all = back.at[0]
    ffn_own, to_x = back.at[1, 0], back.at[1, 1]
    down_own = hidden.at[pl.ds(0, n * block)]
    out_own = hidden.at[pl.ds(n * block, block)]
    early_qkv = [
        gate_up_grad.at[pl.ds(0, group), pl.ds(0, cols)],
        gate_up_grad.at[pl.ds(0, group), pl.ds(cols, cols)],
        gate_up_grad.at[pl.ds(group, group), pl.ds(0, cols)],
    ]
    early_attended = gate_up_grad.at[pl.ds(group, group), pl.ds(cols, cols)]

    def at_weights(first, count):
        return lambda index: weights.at[pl.ds(first, count), pl.ds(pl.multiple_of(index * block, block), block)]

    def at_out(index):
        return weights.at[3, pl.ds(pl.multiple_of(index * block, block), block)]

    def ffn_part(m):
        def own(to):
            if m == 2:
                return down_own.at[pl.ds(pl.multiple_of(to * block, block), block)]
            return w_gate_up.at[m, :, pl.ds(pl.multiple_of(to * cols, cols), cols)]

        return own

    def ffn_place(m):
        return lambda index: wf_out.at[m, pl.ds(pl.multiple_of(index * block, block), block)]

    qkv = Gather(net, w_qkv, at_weights(0, 3), q_sems, "qkv")
    out = Gather(net, out_own, at_out, o_sems, "out")
    ffn = [Exchange(net, ffn_part(m), ffn_place(m), f_sems.at[m], "ffn") for m in range(3)]
    grads = Rows(net, None, lambda z, half: grad.at[block_rows_of(z, half)], g_sems, "grads")
    ffn_rows = Rows(net, ffn_own, lambda z, half: normed_ffn_out.at[z, half], n_sems, "rows")
    load_grad = net.local(cotangent, grad.at[block_rows_of(net.z, x)])

    def send_gains():
        gains[0:8] = jnp.broadcast_to(attn_gain[...].astype(F32), (8, block))
        gains[8:16] = jnp.broadcast_to(ffn_gain[...].astype(F32), (8, block))
        for k in range(1, dp):
            net.send(gains, all_gains.at[me], gain_sems.at[me], ((me + k) % dp, x))
        all_gains[me] = gains[...]

    def turn_weights():
        out_own[...] = w_out[...].T
        for q in range(n):
            down_own[q * block : (q + 1) * block] = w_down[q * cols : (q + 1) * cols].T

    def mask_grads():
        seg_rows = jnp.broadcast_to(seg[...].astype(F32), (LANES, group))
        seg_cols = seg_rows.T
        alive = (seg_cols >= 0).astype(F32)
        for i in range(group // 16):
            live[i] = alive[i * 16 : (i + 1) * 16]
        row_id = lax.broadcasted_iota(jnp.int32, (group, group), 0)
        col_id = lax.broadcasted_iota(jnp.int32, (group, group), 1)
        same = jnp.concatenate([seg_cols] * (group // LANES), axis=1) == jnp.concatenate([seg_rows] * (group // LANES), axis=0)
        mask = jnp.logical_and(same, row_id >= col_id).astype(F32)
        allowed[...] = mask
        angles = (jnp.sum(mask, axis=1, keepdims=True) - 1.0) * freq[...]
        tables[0] = jnp.cos(angles)
        tables[1] = jnp.where(lane % HD < HD // 2, -jnp.sin(angles), jnp.sin(angles))

        net.settle(load_grad)

        def body(r):
            span = pl.ds(pl.multiple_of((net.z * 2 + x) * rows + r, 16), 16)
            grad[span] = (grad[span].astype(F32) * live[(x * rows + r) // 16, :, 0:1]).astype(BF16)

        loop(rows, 16, body, 4)

    def norm():
        for k in range(1, dp):
            source = (me + k) % dp
            net.recv(all_gains.at[source], gain_sems.at[source])
        for i in range(dp):
            gains_all[:, i * block : (i + 1) * block] = all_gains[i]

        def body(r):
            value = residual[pl.ds(r, 16)].astype(F32)
            unit = value * lax.rsqrt(jnp.mean(value * value, axis=-1, keepdims=True) + EPSILON)
            normed_all[x, pl.ds(r, 16)] = (unit * gains_all[0:1]).astype(BF16)

        loop(rows, 16, body, 4)
        net.tag("normed", [net.send(normed_all.at[x], normed_all.at[x], x_sems.at[0], net.device(x=1 - x))])

    def project(k):
        if k == 0:
            net.recv(normed_all.at[1 - x], x_sems.at[0])
            net.settle(qkv.kept)
            net.tag("normed", [net.local(normed_all.at[half], normed_out.at[pl.ds(half * rows, rows)]) for half in (0, 1)])
        b = (net.z + k) % n
        qkv.finish(b)
        base = pl.multiple_of(b * depth, depth)

        def body(col):
            left = jnp.concatenate([normed_all[0, :, pl.ds(base, depth)], normed_all[1, :, pl.ds(base, depth)]], axis=0)
            for m in range(3):
                term = dot(left, weights[m, pl.ds(base, depth), pl.ds(col, 256)])
                to = pl.ds(pl.multiple_of(m * cols + col, 256), 256)
                pre[:, to] = term if k == 0 else pre[:, to] + term

        loop(cols, 256, body, 4)
        if k == n - 1:
            net.tag("save", [net.local(weights.at[pl.ds(0, 3)], wa_out.at[pl.ds(0, 3)])])

    def attend():
        masks = head_masks()

        def body(col):
            cosine, sine = tables[0], tables[1]
            queries = turn(pre[:, pl.ds(col, LANES)], cosine, sine, lane).astype(BF16)
            key_rows = turn(pre[:, pl.ds(pl.multiple_of(cols + col, LANES), LANES)], cosine, sine, lane).astype(BF16)
            value_rows = pre[:, pl.ds(pl.multiple_of(2 * cols + col, LANES), LANES)].astype(BF16)
            early_qkv[0][:, pl.ds(col, LANES)] = queries
            early_qkv[1][:, pl.ds(col, LANES)] = key_rows
            early_qkv[2][:, pl.ds(col, LANES)] = value_rows
            may = jnp.concatenate([allowed[...], allowed[...]], axis=0)
            probs = softmax(both(queries, masks), key_rows, may).astype(BF16)
            early_attended[:, pl.ds(col, LANES)] = pick(dot(probs, value_rows), group).astype(BF16)

        loop(cols, LANES, body, 4)
        net.tag("early", [net.local(early_qkv[m], qkv_out.at[m]) for m in range(3)])
        net.tag("early", [net.local(early_attended, attended_out)])

    def join():
        for k in range(n):
            out.finish((net.z + k) % n)
        net.settle(out.kept)
        net.tag("save_out", [net.local(weights.at[3], wa_out.at[3])])

        def body(col):
            span = pl.ds(col, 256)
            term = dot(early_attended[...], weights[3, span, :], NT)
            low, high = term[:rows], term[rows:]
            input_grad[:, span] = jnp.where(x == 0, low, high)
            to_x[:, span] = jnp.where(x == 0, high, low).astype(BF16)

        loop(width, 256, body, 4)
        net.tag("to_x", [net.send(to_x, from_x, x_sems.at[1], net.device(x=1 - x))])

    def mix():
        net.recv(from_x, x_sems.at[1])

        def body(r):
            span = pl.ds(r, 16)
            value = residual[span].astype(F32) + input_grad[span] + from_x[span].astype(F32)
            mixed[span] = value
            unit = value * lax.rsqrt(jnp.mean(value * value, axis=-1, keepdims=True) + EPSILON)
            ffn_own[span] = (unit * gains_all[8:9]).astype(BF16)

        loop(rows, 16, body, 4)

    def load_ffn(m):
        for k in range(n):
            ffn[m].finish((net.z + k) % n)
        net.settle(ffn[m].kept)
        net.settle_tag("qkv", "save")
        net.tag("weights", [net.local(wf_out.at[m], weights.at[m])])

    def load_rows(k):
        net.settle_tag("out", "save_out", "rows_kept")
        b = order[k]
        ffn_rows.finish(b)
        for x_half in (0, 1):
            for half in (0, 1):
                there = pl.ds(pl.multiple_of(half * every + (b * 2 + x_half) * rows, rows), rows)
                src = normed_ffn_out.at[b, x_half, :, pl.ds(half * cols, cols)]
                net.tag("load%d" % k, [net.local(src, weights.at[3, there])])

    def ffn_step(m, k):
        ffn[m].step((net.z + k) % n)

    def ffn_cross(m):
        for k in range(n):
            ffn[m].cross((net.z + k) % n)


    def features(half):
        return weights.at[3, pl.ds(half * every, every)]

    gate_grad, up_grad = gate_up_grad.at[:, pl.ds(0, cols)], gate_up_grad.at[:, pl.ds(cols, cols)]
    add = gate_up_grad
    backs = RowSum(net, order, lambda b, half: back.at[b, half], back_x, back_z, (bx_sems, bz_sems))
    adds = RowSum(
        net, order, lambda b, half: add.at[pl.ds(pl.multiple_of((b * 2 + half) * rows, rows), rows)],
        back_x, back_z, (bx_sems, bz_sems),
    )
    red = Reduce(
        net, part, from_c, from_y, (result, totals),
        lambda m, to: weights.at[3, pl.ds(pl.multiple_of((m * n + to) * block, block), block)],
        (rc_sems, ry_sems, rz_sems, rl_sems, free), 7 * n,
    )
    def rows_of(b):
        return pl.ds(pl.multiple_of(b * pair, pair), pair)

    def forward(k):
        net.settle_tag("load%d" % k, "weights", "ffn", "early")
        grads.finish(order[k])
        here = rows_of(order[k])

        def body(col):
            span = pl.ds(col, 256)

            def project(m):
                return dot(features(0)[here], weights[m, pl.ds(0, cols), span]) + dot(
                    features(1)[here], weights[m, pl.ds(cols, cols), span]
                )

            gate, up = project(0), project(1)
            hidden_grad = dot(grad[here], weights[2, :, span])
            sigmoid = 1.0 / (1.0 + jnp.exp(-gate))
            active = gate * sigmoid
            hidden[here, span] = (active * up).astype(BF16)
            gate_grad[here, span] = (hidden_grad * up * sigmoid * (1.0 + gate * (1.0 - sigmoid))).astype(BF16)
            up_grad[here, span] = (hidden_grad * active).astype(BF16)

        loop(cols, 256, body, 4)

    def backward(k):
        net.settle_tag("normed", "to_x", "rows")
        b = order[k]
        here = rows_of(b)

        def body(col):
            span = pl.ds(col, 256)
            term = dot(gate_grad[here], weights[0, span, :], NT) + dot(up_grad[here], weights[1, span, :], NT)
            term = term.astype(BF16)
            back[b, 0, :, span] = term[:rows]
            back[b, 1, :, span] = term[rows:]

        loop(width, 256, body, 4)
        backs.start(b)

    def add_chunk(k):
        here = rows_of(order[k])

        def body(col):
            span = pl.ds(col, 256)
            add[here, span] = dot(hidden[here], weights[2, span, :], NT).astype(BF16)

        loop(width, 256, body, 4)
        if k == 0:
            pl.semaphore_wait(free.at[2], 1)
        adds.start(order[k])

    ffn_items = [(2, k) for k in range(n)] + [(m, k) for k in range(n) for m in (0, 1)]
    attention_items = [(3, k) for k in range(n)] + [(m, k) for k in range(n) for m in range(3)]

    def ffn_item():
        m, k = ffn_items[len(red.items)]
        b = order[k]
        base = b * depth
        if m == 2:
            left = grad[:, pl.ds(pl.multiple_of(base, depth), depth)]
        else:
            row = pl.ds(pl.multiple_of(base // cols * every, every), every)
            left = weights[3, row, pl.ds(pl.multiple_of(base % cols, depth), depth)]
        red.item(m, b, left, (gate_grad, up_grad, hidden)[m], depth, block)

    def attention_item():
        m, k = attention_items[len(red.items) - len(ffn_items)]
        base = pl.ds(pl.multiple_of(order[k] * depth, depth), depth)
        left, right = (mixed_all, attended) if m == 3 else (normed, grads_of[m])
        red.item(3 + m, order[k], left[:, base], right, depth, block)

    queries_of, keys_of, values_of = [hidden.at[pl.ds(m * pair, pair)] for m in range(3)]
    attended = hidden.at[pl.ds(3 * pair, pair)]
    normed = grad.at[pl.ds(0, pair)]
    grads_of = [
        grad.at[pl.ds(2 * pair, pair), pl.ds(0, cols)],
        grad.at[pl.ds(2 * pair, pair), pl.ds(cols, cols)],
        grad.at[pl.ds(3 * pair, pair), pl.ds(0, cols)],
    ]
    attended_grad = grad.at[pl.ds(3 * pair, pair), pl.ds(cols, cols)]
    own_rows = mixed_all.at[pl.ds(pl.multiple_of(x * rows, rows), rows)]
    other_rows = mixed_all.at[pl.ds(pl.multiple_of((1 - x) * rows, rows), rows)]
    late = {}

    def tell_beside(which):
        for cond, z in ((net.z > 0, net.z - 1), (net.z < n - 1, net.z + 1)):

            @pl.when(cond)
            def _():
                pl.semaphore_signal(free.at[which], inc=1, device_id=net.device(z=z), device_id_type=MESH)

    def mix_grads():
        backs.finish()
        ffn_sum[...] = jnp.zeros_like(ffn_sum)

        def body(r):
            span = pl.ds(r, 16)
            own = pl.ds(pl.multiple_of((net.z * 2 + x) * rows + r, 16), 16)
            term, gain_term = norm_back(back[net.z, x, span].astype(F32), mixed[span], gains_all[8:9])
            value = grad[own].astype(F32) + term
            input_grad[span] = value
            mixed_all[pl.ds(pl.multiple_of(x * rows + r, 16), 16)] = value.astype(BF16)
            ffn_sum[...] += gain_term[:8] + gain_term[8:]

        loop(rows, 16, body, 4)
        net.send(own_rows, own_rows, x_sems.at[2], net.device(x=1 - x))
        pl.semaphore_signal(free.at[2], inc=1, device_id=net.device(x=1 - x), device_id_type=MESH)
        tell_beside(3)

    def load_out():
        late["out"] = net.local(wa_out.at[3], weights.at[3])

    def load_rest():
        net.settle_tag("grads")
        late["normed"] = net.local(normed_out, normed)
        late["qkv"] = net.local(wa_out.at[pl.ds(0, 3)], weights.at[pl.ds(0, 3)])
        late["parts"] = [net.local(qkv_out.at[m], hidden.at[pl.ds(m * pair, pair)]) for m in range(3)]
        late["attended"] = net.local(attended_out, attended)

    def step_adds():
        if adds.done_z == 0:
            pl.semaphore_wait(free.at[3], beside)
        adds.step_z(adds.done_z)

    def attended_back():
        net.settle(late["out"])
        net.recv(other_rows, x_sems.at[2])

        def body(col):
            span = pl.ds(col, 256)
            attended_grad[:, span] = dot(mixed_all[...], weights[3, :, span]).astype(BF16)

        loop(cols, 256, body, 4)
        tell_beside(4)
        net.settle(late["attended"])

    def heads():
        for load in late["parts"]:
            net.settle(load)
        masks = head_masks()

        def body(col):
            span = pl.ds(col, LANES)
            cosine, sine = tables[0], tables[1]
            queries, key_rows, value_rows = queries_of[:, span], keys_of[:, span], values_of[:, span]
            out_grad = attended_grad[:, span]
            queries2, out_grad2 = both(queries, masks), both(out_grad, masks)
            may = jnp.concatenate([allowed[...], allowed[...]], axis=0)
            probs = softmax(queries2, key_rows, may)
            value_grad = dot(probs.astype(BF16), out_grad2, TN)
            prob_grad = dot(out_grad2, value_rows, NT)
            score_grad = probs * (prob_grad - jnp.sum(probs * prob_grad, axis=-1, keepdims=True))
            score_grad = score_grad.astype(BF16)
            query_grad = pick(dot(score_grad, key_rows), pair) * HD ** (-0.5)
            key_grad = dot(score_grad, queries2, TN) * HD ** (-0.5)
            grads_of[0][:, span] = turn(query_grad, cosine, -sine, lane).astype(BF16)
            grads_of[1][:, span] = turn(key_grad, cosine, -sine, lane).astype(BF16)
            grads_of[2][:, span] = value_grad.astype(BF16)

        loop(cols, LANES, body, 4)
        net.settle(late["normed"])

    def normed_back():
        net.settle(late["qkv"])
        for entry in backs.sent:
            net.settle(entry)

        def body(col):
            span = pl.ds(col, 256)
            term = dot(grads_of[0][...], weights[0, span, :], NT)
            term += dot(grads_of[1][...], weights[1, span, :], NT)
            term += dot(grads_of[2][...], weights[2, span, :], NT)
            back[0, 0, :, span] = term[:rows].astype(BF16)
            back[0, 1, :, span] = term[rows:].astype(BF16)

        loop(width, 256, body, 4)
        net.send(back.at[0, 1 - x], from_x, x_sems.at[3], net.device(x=1 - x))

    def input_back():
        net.recv(from_x, x_sems.at[3])
        gain_sum[...] = jnp.zeros_like(gain_sum)

        def body(r):
            span = pl.ds(r, 16)
            grad_rows = back[0, x, span].astype(F32) + from_x[span].astype(F32)
            term, gain_term = norm_back(grad_rows, residual[span].astype(F32), gains_all[0:1])
            input_grad[span] += term
            gain_sum[...] += gain_term[:8] + gain_term[8:]

        loop(rows, 16, body, 4)
        for i in range(dp):
            gain_to[i, 0:8] = gain_sum[:, i * block : (i + 1) * block]
            gain_to[i, 8:16] = ffn_sum[:, i * block : (i + 1) * block]
        for k in range(1, dp):
            to = (me + k) % dp
            net.send(gain_to.at[to], gain_from.at[me], back_gain_sems.at[me], (to, x))

    def sum_gains():
        total = gain_to[me]
        for k in range(1, dp):
            source = (me + k) % dp
            net.recv(gain_from.at[source], back_gain_sems.at[source])
            total = total + gain_from[source]
        gain_x[0] = total
        net.send(gain_x.at[0], gain_x.at[1], x_sems.at[4], net.device(x=1 - x))

    def block_rows():
        adds.finish()

        def body(r):
            span = pl.ds(r, 16)
            block_out[span] = (mixed[span] + adds.part(net.z, x)[span].astype(F32)).astype(BF16)

        loop(rows, 16, body, 4)

    qkv.start()
    turn_weights()
    out.start()
    send_gains()
    qkv.step(1)
    mask_grads()
    norm()
    qkv.cross_step(0)
    out.step(1)
    qkv.step(2)
    ffn[2].start()
    out.step(2)
    qkv.cross_step(1)
    grads.start()
    qkv.step(3)
    ffn_step(2, 3)
    qkv.cross_step(2)
    out.step(3)
    ffn[0].start()
    qkv.cross_step(3)
    out.cross_step(0)
    project(0)
    grads.step(1)
    project(1)
    project(2)
    out.cross_step(1)
    out.cross_step(2)
    out.cross_step(3)
    ffn_step(2, 2)
    project(3)
    ffn[1].start()
    ffn_step(2, 1)
    attend()
    join()
    ffn_step(0, 2)
    grads.step(2)
    ffn_step(0, 1)
    ffn_cross(2)
    mix()
    ffn_rows.start()
    load_ffn(2)
    ffn_step(0, 3)
    ffn_step(1, 2)
    ffn_step(1, 3)
    grads.step(3)
    ffn_cross(0)
    load_rows(3)
    ffn_step(1, 1)
    ffn_rows.step(1)
    ffn_cross(1)
    ffn_rows.step(2)
    load_rows(2)
    load_ffn(1)
    load_ffn(0)
    ffn_rows.step(3)
    forward(3)
    forward(2)
    load_rows(1)
    backward(2)
    forward(1)
    load_rows(0)
    forward(0)
    ffn_item()
    backward(0)
    red.step_c()
    ffn_item()
    ffn_item()
    red.step_c()
    red.step_y()
    backward(1)
    red.step_c()
    backs.step_x(0)
    backs.step_z(0)
    red.step_y()
    ffn_item()
    ffn_item()
    red.step_c()
    red.step_c()
    backs.step_x(2)
    backs.step_x(1)
    backs.step_z(1)
    backs.step_z(2)
    ffn_item()
    red.step_c()
    ffn_item()
    ffn_item()
    red.step_y()
    backward(3)
    red.step_c()
    backs.step_x(3)
    ffn_item()
    red.step_c()
    ffn_item()
    red.step_c()
    red.step_y()
    ffn_item()
    mix_grads()
    red.step_y()
    red.step_c()
    ffn_item()
    add_chunk(0)
    load_out()
    red.step_y()
    red.step_y()
    add_chunk(1)
    add_chunk(2)
    red.step_y()
    red.step_c()
    red.step_c()
    add_chunk(3)
    load_rest()
    red.step_y()
    attended_back()
    attention_item()
    heads()
    red.step_c()
    for _ in range(3):
        red.step_y()
    attention_item()
    attention_item()
    red.step_c()
    pl.semaphore_wait(free.at[4], beside)
    attention_item()
    red.step_y()
    red.step_z()
    attention_item()
    red.step_y()
    red.step_c()
    red.step_c()
    adds.step_x(adds.done_x)
    red.step_c()
    red.step_z()
    attention_item()
    step_adds()
    normed_back()
    red.step_y()
    attention_item()
    red.step_z()
    attention_item()
    attention_item()
    red.step_c()
    attention_item()
    red.step_y()
    red.step_y()
    red.step_c()
    adds.step_x(adds.done_x)
    attention_item()
    red.step_c()
    red.step_c()
    red.step_y()
    step_adds()
    red.step_c()
    attention_item()
    red.step_c()
    adds.step_x(adds.done_x)
    red.step_z()
    red.step_c()
    red.step_z()
    step_adds()
    red.step_z()
    adds.step_x(adds.done_x)
    attention_item()
    red.step_y()
    red.step_y()
    red.step_z()
    red.step_y()
    red.step_c()
    attention_item()
    red.step_y()
    attention_item()
    input_back()
    red.step_z()
    red.step_z()
    red.step_y()
    red.step_c()
    red.step_c()
    step_adds()
    block_rows()
    attention_item()
    red.step_y()
    red.step_y()
    for _ in range(3):
        red.step_z()
    red.step_c()
    red.step_z()
    red.step_y()
    red.step_y()
    sum_gains()
    red.step_y()
    for _ in range(3):
        red.step_z()
    assert red.done_y == red.done_z == red.total and adds.done_z == n and backs.done_x == n
    net.recv(gain_x.at[1], x_sems.at[4])
    gain_out[...] = gain_x[0] + gain_x[1]
    red.finish()
    net.drain()


def finish_kernel(
    ffn, attention, gains, block_rows, input_rows,
    qkv_grad, out_grad, gate_up_grad, down_grad, attn_gain_grad, ffn_gain_grad, block_out, input_grad,
):
    q, n = pl.program_id(0), pl.num_programs(0)
    z = lax.axis_index("dp") // 4
    gate_up_grad[...] = ffn[0:2, 0].astype(F32)
    down_grad[...] = ffn[2, 0].astype(F32).T
    total = attention[0, 2].astype(F32)
    total += jnp.where(z > 0, attention[0, 0].astype(F32), 0.0)
    total += jnp.where(z < n - 1, attention[0, 1].astype(F32), 0.0)

    @pl.when(q < 3)
    def _():
        qkv_grad[0] = total

    @pl.when(q == 3)
    def _():
        out_grad[...] = total.T

    attn_gain_grad[...] = jnp.sum(gains[0:8], axis=0, keepdims=True)
    ffn_gain_grad[...] = jnp.sum(gains[8:16], axis=0, keepdims=True)
    block_out[...] = block_rows[...]
    input_grad[...] = input_rows[...]


def call(kernel, collective_id, sends, locals_, vmem, outs, out_specs, scratch, sems, flags=0):
    def typed(entry):
        return (entry[:-1], F32) if entry[-1] is F32 else (entry, BF16)

    dma = pltpu.SemaphoreType.DMA
    return lambda in_specs, *args: pl.pallas_call(
        kernel,
        out_shape=[jax.ShapeDtypeStruct(*typed(entry)) for entry in outs],
        in_specs=in_specs,
        out_specs=out_specs,
        scratch_shapes=[pltpu.VMEM(*typed(entry)) for entry in scratch] + [dma((sends,)), dma((locals_,))] + [dma(entry) for entry in sems] + [pltpu.SemaphoreType.REGULAR((flags,))] * (flags > 0),
        compiler_params=pltpu.CompilerParams(collective_id=collective_id, has_side_effects=True, vmem_limit_bytes=vmem),
    )(*args)


def shards(dp, residual, seg_ids, attn_gain, w_qkv, w_out, ffn_gain, w_gate_up, w_down, cotangent):
    n = dp // 4
    rows, width = residual.shape
    group = seg_ids.shape[0]
    block, cols = w_qkv.shape[1:]
    part = w_gate_up.shape[2] // n
    pairs = np.arange(LANES) % (HD // 2)
    freq = jnp.asarray(ROPE_BASE ** (-2.0 * pairs / HD), F32)[None]
    every = n * 2 * rows
    slots = SLOTS
    layer = call(
        functools.partial(layer_kernel, dp), 1, 320, 112, LIMIT,
        [
            (3, n, block, part), (4, 3, block, cols), (4, width, cols), (3, width, part), (n, 2, rows, width),
            (group, width), (group, cols), (3, group, cols), (rows, width), (rows, width, F32), (16, block, F32),
        ],
        [ANY] * 8 + [VM] * 3,
        [
            (4, width, cols), (every, width), (every, part), (every, 2 * part),
            (n, 2, rows, width), (n, rows, width), (n + 1, rows, width),
            (slots, 2, 2, block, part), (slots, 2, block, part), (slots, block, part),
            (group, width), (rows, width), (group, 3 * cols, F32), (rows, width, F32), (2, group, LANES, F32),
            (group, group, F32), (16, block, F32), (dp, 16, block, F32), (16, width, F32),
            (8, width, F32), (8, width, F32), (dp, 16, block, F32), (dp, 16, block, F32), (2, 16, block, F32),
        ],
        [
            (dp,), (4, n), (4, n), (3, 4, n), (2, n), (2, n), (5,),
            (n,), (n + 1,), (slots,), (slots,), (3, n), (4, n + 2), (dp,),
        ],
        5,
    )
    outputs = layer(
        [VM] * 7 + [ANY] * 3, residual, seg_ids[None], attn_gain[None], ffn_gain[None], freq, w_out, w_down, w_qkv,
        w_gate_up, cotangent,
    )
    result, totals, block_out, input_grad, gain_grads = outputs[0], outputs[1], outputs[8], outputs[9], outputs[10]
    qkv_grad, out_grad, gate_up_grad, down_grad, attn_gain_grad, ffn_gain_grad, block_out, input_grad = pl.pallas_call(
        finish_kernel,
        grid=(n,),
        out_shape=[
            jax.ShapeDtypeStruct(entry, F32)
            for entry in (
                (3, block, cols), (cols, block), (2, block, n * part), (n * part, block), (1, block), (1, block)
            )
        ] + [jax.ShapeDtypeStruct((rows, width), BF16), jax.ShapeDtypeStruct((rows, width), F32)],
        in_specs=[
            pl.BlockSpec((3, 1, block, part), lambda q: (0, q, 0, 0)),
            pl.BlockSpec((1, 3, block, cols), lambda q: (q, 0, 0, 0)),
            pl.BlockSpec((16, block), lambda q: (0, 0)),
            pl.BlockSpec((rows // n, width), lambda q: (q, 0)),
            pl.BlockSpec((rows // n, width), lambda q: (q, 0)),
        ],
        out_specs=[
            pl.BlockSpec((1, block, cols), lambda q: (jnp.minimum(q, 2), 0, 0)),
            pl.BlockSpec((cols, block), lambda q: (0, 0)),
            pl.BlockSpec((2, block, part), lambda q: (0, 0, q)),
            pl.BlockSpec((part, block), lambda q: (q, 0)),
            pl.BlockSpec((1, block), lambda q: (0, 0)),
            pl.BlockSpec((1, block), lambda q: (0, 0)),
            pl.BlockSpec((rows // n, width), lambda q: (q, 0)),
            pl.BlockSpec((rows // n, width), lambda q: (q, 0)),
        ],
        compiler_params=pltpu.CompilerParams(vmem_limit_bytes=LIMIT),
    )(result, totals, gain_grads, block_out, input_grad)
    return (
        block_out, input_grad, attn_gain_grad.reshape(block), qkv_grad, out_grad, ffn_gain_grad.reshape(block),
        gate_up_grad, down_grad,
    )


def positions(segments):
    row_index = jnp.arange(segments.shape[1], dtype=jnp.int32)[None, :]
    previous = jnp.concatenate([segments[:, :1] - 1, segments[:, :-1]], axis=1)
    run_start = lax.cummax(jnp.where(segments != previous, row_index, 0), axis=1)
    return row_index - run_start


def rope_tables(places, head_dim):
    half_dim = head_dim // 2
    frequency = ROPE_BASE ** (-(jnp.arange(half_dim, dtype=jnp.float32) * 2.0 / head_dim))
    angles = places.astype(jnp.float32)[:, None, None] * frequency[None, None, :]
    return (jnp.cos(angles), jnp.sin(angles))


def rotate(field, cosine, sine_table):
    half_dim = field.shape[-1] // 2
    lower_half = field[..., :half_dim]
    upper_half = field[..., half_dim:]
    return jnp.concatenate(
        [
            lower_half * cosine - upper_half * sine_table,
            upper_half * cosine + lower_half * sine_table,
        ],
        axis=-1,
    )


def unrotate(field, cosine, sine_table):
    half_dim = field.shape[-1] // 2
    lower_half = field[..., :half_dim]
    upper_half = field[..., half_dim:]
    return jnp.concatenate(
        [
            lower_half * cosine + upper_half * sine_table,
            upper_half * cosine - lower_half * sine_table,
        ],
        axis=-1,
    )


def attention_scores(queries, key_rows, allowed):
    scores = jnp.einsum(
        "qhd,khd->hqk", queries, key_rows, preferred_element_type=jnp.float32
    ) * queries.shape[-1] ** (-0.5)
    return jnp.where(allowed[None], scores, -1e30)


def plain_shards(residual_in, seg_ids, attn_gain, w_qkv, w_out, ffn_gain, w_gate_up, w_down, cotangent):
    rows_local = residual_in.shape[0]
    group_rows = seg_ids.shape[0]
    offset = lax.axis_index("tensor") * rows_local
    live_rows = (lax.dynamic_slice_in_dim(seg_ids, offset, rows_local) >= 0).astype(jnp.float32)
    residual = residual_in.astype(jnp.float32)
    contract_rows = (((0,), (0,)), ((), ()))
    contract_cols = (((1,), (1,)), ((), ()))
    gain_attn, qkv_full, out_full = (
        lax.all_gather(attn_gain, "dp", axis=0, tiled=True),
        lax.all_gather(w_qkv, "dp", axis=1, tiled=True),
        lax.all_gather(w_out, "dp", axis=1, tiled=True),
    )
    norm_attn = lax.rsqrt(jnp.mean(residual * residual, axis=-1, keepdims=True) + EPSILON)
    unit_attn = residual * norm_attn
    normed = (unit_attn * gain_attn.astype(jnp.float32)).astype(jnp.bfloat16)
    normed_all = lax.all_gather(normed, "tensor", axis=0, tiled=True)
    projected = jnp.einsum("rd,cde->cre", normed_all, qkv_full, preferred_element_type=jnp.float32)
    head_count = qkv_full.shape[2] // HD
    head_shape = (group_rows, head_count, HD)
    cosine, sine_table = rope_tables(positions(seg_ids[None, :])[0], HD)
    queries = rotate(projected[0].reshape(head_shape), cosine, sine_table).astype(jnp.bfloat16)
    key_rows = rotate(projected[1].reshape(head_shape), cosine, sine_table).astype(jnp.bfloat16)
    value_rows = projected[2].reshape(head_shape).astype(jnp.bfloat16)
    row_index = jnp.arange(group_rows)
    allowed = (seg_ids[:, None] == seg_ids[None, :]) & (row_index[:, None] >= row_index[None, :])
    scores = attention_scores(queries, key_rows, allowed)
    row_top = jnp.max(scores, axis=-1, keepdims=True)
    log_total = row_top + jnp.log(jnp.sum(jnp.exp(scores - row_top), axis=-1, keepdims=True))
    weights = jnp.exp(scores - log_total).astype(jnp.bfloat16)
    attended = jnp.einsum("hqk,khd->qhd", weights, value_rows, preferred_element_type=jnp.float32)
    attended = attended.reshape(group_rows, head_count * HD).astype(jnp.bfloat16)
    mixed = residual + lax.psum_scatter(
        jnp.dot(attended, out_full, preferred_element_type=jnp.float32),
        "tensor",
        scatter_dimension=0,
        tiled=True,
    )
    gain_ffn, gate_up_full, down_full = (
        lax.all_gather(ffn_gain, "dp", axis=0, tiled=True),
        lax.all_gather(w_gate_up, "dp", axis=1, tiled=True),
        lax.all_gather(w_down, "dp", axis=1, tiled=True),
    )
    norm_ffn = lax.rsqrt(jnp.mean(mixed * mixed, axis=-1, keepdims=True) + EPSILON)
    unit_ffn = mixed * norm_ffn
    normed_ffn = (unit_ffn * gain_ffn.astype(jnp.float32)).astype(jnp.bfloat16)
    normed_ffn_all = lax.all_gather(normed_ffn, "tensor", axis=0, tiled=True)
    gate_up = jnp.einsum(
        "rd,cde->cre", normed_ffn_all, gate_up_full, preferred_element_type=jnp.float32
    )
    gate_pre = gate_up[0]
    up_pre = gate_up[1]
    sigmoid_gate = jax.nn.sigmoid(gate_pre)
    activated = gate_pre * sigmoid_gate
    hidden = (activated * up_pre).astype(jnp.bfloat16)
    output = mixed + lax.psum_scatter(
        jnp.dot(hidden, down_full, preferred_element_type=jnp.float32).astype(jnp.bfloat16),
        "tensor",
        scatter_dimension=0,
        tiled=True,
    ).astype(jnp.float32)
    grad_out = cotangent.astype(jnp.float32) * live_rows[:, None]
    grad_all = lax.all_gather(grad_out.astype(jnp.bfloat16), "tensor", axis=0, tiled=True)
    down_grad = lax.dot_general(hidden, grad_all, contract_rows, preferred_element_type=jnp.float32)
    hidden_grad = lax.dot_general(
        grad_all, down_full, contract_cols, preferred_element_type=jnp.float32
    )
    gate_grads = jnp.stack(
        [
            hidden_grad * up_pre * sigmoid_gate * (1.0 + gate_pre * (1.0 - sigmoid_gate)),
            hidden_grad * activated,
        ]
    ).astype(jnp.bfloat16)
    gate_up_grad = jnp.einsum(
        "rd,cre->cde", normed_ffn_all, gate_grads, preferred_element_type=jnp.float32
    )
    normed_ffn_grad = lax.psum_scatter(
        jnp.einsum("cre,cde->rd", gate_grads, gate_up_full, preferred_element_type=jnp.float32),
        "tensor",
        scatter_dimension=0,
        tiled=True,
    )
    ffn_gain_part = jnp.sum(normed_ffn_grad * unit_ffn, axis=0)
    scaled_ffn = normed_ffn_grad * gain_ffn.astype(jnp.float32)
    mixed_grad = grad_out + norm_ffn * (
        scaled_ffn - unit_ffn * jnp.mean(scaled_ffn * unit_ffn, axis=-1, keepdims=True)
    )
    mixed_all = lax.all_gather(mixed_grad.astype(jnp.bfloat16), "tensor", axis=0, tiled=True)
    out_grad = lax.dot_general(
        attended, mixed_all, contract_rows, preferred_element_type=jnp.float32
    )
    attended_grad = lax.dot_general(
        mixed_all, out_full, contract_cols, preferred_element_type=jnp.float32
    )
    attended_grad = attended_grad.astype(jnp.bfloat16).reshape(head_shape)
    probabilities = jnp.exp(attention_scores(queries, key_rows, allowed) - log_total)
    value_grad = jnp.einsum(
        "hqk,qhd->khd",
        probabilities.astype(jnp.bfloat16),
        attended_grad,
        preferred_element_type=jnp.float32,
    )
    prob_grad = jnp.einsum(
        "qhd,khd->hqk", attended_grad, value_rows, preferred_element_type=jnp.float32
    )
    score_grad = (
        probabilities * (prob_grad - jnp.sum(probabilities * prob_grad, axis=-1, keepdims=True))
    ).astype(jnp.bfloat16)
    scale_factor = HD ** (-0.5)
    query_grad = (
        jnp.einsum("hqk,khd->qhd", score_grad, key_rows, preferred_element_type=jnp.float32)
        * scale_factor
    )
    key_grad = (
        jnp.einsum("hqk,qhd->khd", score_grad, queries, preferred_element_type=jnp.float32)
        * scale_factor
    )
    qkv_grads = jnp.stack(
        [
            unrotate(query_grad, cosine, sine_table),
            unrotate(key_grad, cosine, sine_table),
            value_grad,
        ]
    )
    qkv_grads = qkv_grads.reshape(3, group_rows, head_count * HD).astype(jnp.bfloat16)
    qkv_grad = jnp.einsum("rd,cre->cde", normed_all, qkv_grads, preferred_element_type=jnp.float32)
    normed_grad = lax.psum_scatter(
        jnp.einsum("cre,cde->rd", qkv_grads, qkv_full, preferred_element_type=jnp.float32),
        "tensor",
        scatter_dimension=0,
        tiled=True,
    )
    attn_gain_part = jnp.sum(normed_grad * unit_attn, axis=0)
    scaled_attn = normed_grad * gain_attn.astype(jnp.float32)
    input_grad = mixed_grad + norm_attn * (
        scaled_attn - unit_attn * jnp.mean(scaled_attn * unit_attn, axis=-1, keepdims=True)
    )
    (
        query_total,
        key_total,
        value_total,
        out_total,
        attn_gain_total,
        gate_total,
        up_total,
        down_total,
        ffn_gain_total,
    ) = (
        lax.psum_scatter(qkv_grad[0], "dp", scatter_dimension=0, tiled=True),
        lax.psum_scatter(qkv_grad[1], "dp", scatter_dimension=0, tiled=True),
        lax.psum_scatter(qkv_grad[2], "dp", scatter_dimension=0, tiled=True),
        lax.psum_scatter(out_grad, "dp", scatter_dimension=1, tiled=True),
        lax.psum_scatter(attn_gain_part, "dp", scatter_dimension=0, tiled=True),
        lax.psum_scatter(gate_up_grad[0], "dp", scatter_dimension=0, tiled=True),
        lax.psum_scatter(gate_up_grad[1], "dp", scatter_dimension=0, tiled=True),
        lax.psum_scatter(down_grad, "dp", scatter_dimension=1, tiled=True),
        lax.psum_scatter(ffn_gain_part, "dp", scatter_dimension=0, tiled=True),
    )
    gate_up_total = jnp.stack([gate_total, up_total])
    qkv_total = jnp.stack([query_total, key_total, value_total])
    attn_gain_sum, ffn_gain_sum = lax.psum((attn_gain_total, ffn_gain_total), "tensor")
    return (
        output.astype(jnp.bfloat16),
        input_grad,
        attn_gain_sum,
        qkv_total,
        out_total,
        ffn_gain_sum,
        gate_up_total,
        down_total,
    )


def solution(mesh):
    in_specs = (
        P(("dp", "tensor"), None),
        P("dp"),
        P("dp"),
        P(None, "dp", "tensor"),
        P("tensor", "dp"),
        P("dp"),
        P(None, "dp", "tensor"),
        P("tensor", "dp"),
        P(("dp", "tensor"), None),
    )
    out_specs = (
        P(("dp", "tensor"), None),
        P(("dp", "tensor"), None),
        P("dp"),
        P(None, "dp", "tensor"),
        P("tensor", "dp"),
        P("dp"),
        P(None, "dp", "tensor"),
        P("tensor", "dp"),
    )
    dp = mesh.shape["dp"]
    local = functools.partial(shards, dp) if dp == 16 else plain_shards
    return jax.shard_map(local, mesh=mesh, in_specs=in_specs, out_specs=out_specs, check_vma=False)
```

```python
import functools

import jax
import jax.numpy as jnp
import numpy as np
from jax import lax
from jax.experimental import pallas as pl
from jax.experimental.pallas import tpu as pltpu
from jax.sharding import PartitionSpec as P

HD = 64
EPSILON = 1e-05
ROPE_BASE = 130000.0
MESH = pl.DeviceIdType.MESH
ANY = pl.BlockSpec(memory_space=pl.ANY)
VM = pl.BlockSpec(memory_space=pltpu.VMEM)
F32 = jnp.float32
BF16 = jnp.bfloat16
LANES = 128
SLOTS = 9
LIMIT = 66977792
NT = (((1,), (1,)), ((), ()))
TN = (((0,), (0,)), ((), ()))
NN = (((1,), (0,)), ((), ()))


def dot(a, b, dims=NN):
    return lax.dot_general(a, b, dims, preferred_element_type=F32)


def when(cond, action):
    if cond is None:
        action()
    else:
        pl.when(cond)(action)


class Net:
    def __init__(self, dp, send_sems, local_sems):
        self.n = dp // 4
        self.dp_index = lax.axis_index("dp")
        self.x = lax.axis_index("tensor")
        self.z = self.dp_index // 4
        self.y = (self.dp_index // 2) % 2
        self.c = self.dp_index % 2
        self.send_sems = send_sems
        self.local_sems = local_sems
        self.sent = 0
        self.moved = 0
        self.pending = []
        self.kept = []
        self.tags = {}

    def place(self, z, y, c):
        return (z * 2 + y) * 2 + c

    def device(self, z=None, y=None, c=None, x=None):
        z = self.z if z is None else z
        y = self.y if y is None else y
        c = self.c if c is None else c
        x = self.x if x is None else x
        return (self.place(z, y, c), x)

    def greet(self, devices):
        barrier = pltpu.get_barrier_semaphore()
        for device in devices:
            pl.semaphore_signal(barrier, inc=1, device_id=device, device_id_type=MESH)
        pl.semaphore_wait(barrier, len(devices))

    def send(self, src, dst, recv_sem, device, cond=None):
        sem = self.send_sems.at[self.sent]
        self.sent += 1
        copy = pltpu.make_async_remote_copy(
            src_ref=src, dst_ref=dst, send_sem=sem, recv_sem=recv_sem, device_id=device, device_id_type=MESH
        )
        when(cond, copy.start)
        self.pending.append((cond, copy))
        return self.pending[-1]

    def recv(self, dst, recv_sem):
        pltpu.make_async_remote_copy(
            src_ref=dst, dst_ref=dst, send_sem=self.send_sems.at[0], recv_sem=recv_sem,
            device_id=self.device(c=1 - self.c), device_id_type=MESH,
        ).wait_recv()

    def local(self, src, dst, cond=None):
        sem = self.local_sems.at[self.moved]
        self.moved += 1
        copy = pltpu.make_async_copy(src, dst, sem)
        when(cond, copy.start)
        self.kept.append((cond, copy))
        return self.kept[-1]

    def settle(self, entry):
        for entries, wait in ((self.kept, "wait"), (self.pending, "wait_send")):
            for k, known in enumerate(entries):
                if known is entry:
                    when(entry[0], getattr(entry[1], wait))
                    del entries[k]
                    return

    def tag(self, name, entries):
        self.tags.setdefault(name, []).extend(entries)

    def settle_tag(self, *names):
        for name in names:
            for entry in self.tags.pop(name, ()):
                self.settle(entry)

    def drain(self):
        assert self.sent <= self.send_sems.shape[0] and self.moved <= self.local_sems.shape[0]
        for cond, copy in self.pending:
            when(cond, copy.wait_send)
        for cond, copy in self.kept:
            when(cond, copy.wait)


class Gather:
    def __init__(self, net, own, at, sems, tag):
        self.net, self.own, self.at, self.tag = net, own, at, tag
        self.sems = sems

    def spread(self, block, src, ysend=True):
        net = self.net
        here = net.place(block, net.y, net.c)
        net.tag(self.tag, [net.send(src, self.at(here), self.sems.at[1, block], net.device(y=1 - net.y))])
        net.tag(self.tag, [net.send(src, self.at(here), self.sems.at[2 + net.y, block], net.device(c=1 - net.c))])

    def start(self):
        net = self.net
        here = self.at(net.dp_index)
        net.tag(self.tag, [net.send(self.own, here, self.sems.at[0, net.z], net.device(z=net.z + 1), net.z < net.n - 1)])
        net.tag(self.tag, [net.send(self.own, here, self.sems.at[0, net.z], net.device(z=net.z - 1), net.z > 0)])
        self.spread(net.z, self.own)
        self.kept = net.local(self.own, here)

    def step(self, s):
        net = self.net
        for sign in (1, -1):
            block = net.z - s * sign
            valid = jnp.logical_and(block >= 0, block < net.n)
            block = jnp.where(valid, block, net.z)
            nxt = net.z + sign
            more = jnp.logical_and(nxt >= 0, nxt < net.n)
            nxt = jnp.where(more, nxt, net.z)
            here = self.at(net.place(block, net.y, net.c))

            @pl.when(valid)
            def _():
                net.recv(here, self.sems.at[0, block])

            net.tag(self.tag, [net.send(here, here, self.sems.at[0, block], net.device(z=nxt), jnp.logical_and(valid, more))])
            net.tag(self.tag, [net.send(here, here, self.sems.at[1, block], net.device(y=1 - net.y), valid)])
            net.tag(self.tag, [net.send(here, here, self.sems.at[2 + net.y, block], net.device(c=1 - net.c), valid)])

    def cross(self, block):
        net = self.net
        there = self.at(net.place(block, 1 - net.y, net.c))
        net.recv(there, self.sems.at[1, block])
        net.tag(self.tag, [net.send(there, there, self.sems.at[3 - net.y, block], net.device(c=1 - net.c))])

    def cross_step(self, s):
        net = self.net
        if s == 0:
            self.cross(net.z)
            return
        for sign in (1, -1):
            block = net.z - s * sign
            valid = jnp.logical_and(block >= 0, block < net.n)
            block = jnp.where(valid, block, net.z)
            there = self.at(net.place(block, 1 - net.y, net.c))

            @pl.when(valid)
            def _():
                net.recv(there, self.sems.at[1, block])

            net.tag(self.tag, [net.send(there, there, self.sems.at[3 - net.y, block], net.device(c=1 - net.c), valid)])

    def finish(self, block):
        net = self.net
        for y in (0, 1):
            net.recv(self.at(net.place(block, y, 1 - net.c)), self.sems.at[2 + y, block])


class Exchange:
    def __init__(self, net, part, at, sems, tag):
        self.net, self.part, self.at, self.tag = net, part, at, tag
        self.sems = sems

    def start(self):
        net = self.net
        here = self.at(net.dp_index)
        for d in list(range(1, net.n)):
            to = (net.z + d) % net.n
            net.tag(self.tag, [net.send(self.part(to), here, self.sems.at[0, net.z], net.device(z=to))])
        own = self.part(net.z)
        net.tag(self.tag, [net.send(own, here, self.sems.at[1, net.z], net.device(y=1 - net.y))])
        net.tag(self.tag, [net.send(own, here, self.sems.at[2 + net.y, net.z], net.device(c=1 - net.c))])
        self.kept = net.local(own, here)

    def step(self, block):
        net = self.net
        here = self.at(net.place(block, net.y, net.c))
        net.recv(here, self.sems.at[0, block])
        net.send(here, here, self.sems.at[1, block], net.device(y=1 - net.y))
        net.send(here, here, self.sems.at[2 + net.y, block], net.device(c=1 - net.c))

    def cross(self, block):
        net = self.net
        there = self.at(net.place(block, 1 - net.y, net.c))
        net.recv(there, self.sems.at[1, block])
        net.send(there, there, self.sems.at[3 - net.y, block], net.device(c=1 - net.c))

    finish = Gather.finish


class Rows:
    def __init__(self, net, own, at, sems, tag):
        self.net, self.own, self.at, self.tag = net, own, at, tag
        self.sems = sems

    def start(self):
        net = self.net
        here = self.at(net.z, net.x)
        own = here if self.own is None else self.own
        net.tag(self.tag, [net.send(own, here, self.sems.at[0, net.z], net.device(z=net.z + 1), net.z < net.n - 1)])
        net.tag(self.tag, [net.send(own, here, self.sems.at[0, net.z], net.device(z=net.z - 1), net.z > 0)])
        net.tag(self.tag, [net.send(own, here, self.sems.at[1, net.z], net.device(x=1 - net.x))])
        if self.own is not None:
            net.tag(self.tag + "_kept", [net.local(own, here)])

    def step(self, s):
        net = self.net
        forwarded = []
        for sign in (1, -1):
            block = net.z - s * sign
            valid = jnp.logical_and(block >= 0, block < net.n)
            block = jnp.where(valid, block, net.z)
            nxt = net.z + sign
            more = jnp.logical_and(nxt >= 0, nxt < net.n)
            nxt = jnp.where(more, nxt, net.z)
            here = self.at(block, net.x)

            @pl.when(valid)
            def _():
                net.recv(here, self.sems.at[0, block])

            forwarded.append(net.send(here, here, self.sems.at[0, block], net.device(z=nxt), jnp.logical_and(valid, more)))
            forwarded.append(net.send(here, here, self.sems.at[1, block], net.device(x=1 - net.x), valid))
        if self.own is None:
            net.tag(self.tag, forwarded)

    def finish(self, block):
        net = self.net
        net.recv(self.at(block, 1 - net.x), self.sems.at[1, block])


class Reduce:
    def __init__(self, net, part, from_c, from_y, result, line, sems, total):
        self.net, self.part, self.from_c, self.from_y = net, part, from_c, from_y
        self.result, self.totals = result
        self.line = line
        self.cs, self.ys, self.zs, self.ls, self.free = sems
        self.slots = part.shape[0]
        self.total = total
        self.items = []
        self.out = {}
        self.done_c = self.done_y = self.done_z = 0

    def add(self, total, term):
        def body(r):
            span = pl.ds(r, 16)
            total[span] = (total[span].astype(F32) + term[span].astype(F32)).astype(BF16)

        loop(total.shape[0], 16, body, 8)

    def credit(self, which, device):
        pl.semaphore_signal(self.free.at[which], inc=1, device_id=device, device_id_type=MESH)

    def item(self, matrix, to, left, right, depth, block):
        net = self.net
        i = len(self.items)
        slot = i % self.slots
        self.items.append((matrix, to))
        assert self.done_z > i - self.slots
        for entry in self.out.pop(i - self.slots, ()):
            net.settle(entry)

        def body(col):
            term = dot(left, right[:, pl.ds(col, 256)], TN).astype(BF16)
            for y in (0, 1):
                for c in (0, 1):
                    at = (y * 2 + c) * block
                    self.part[slot, c, y, :, pl.ds(col, 256)] = term[at : at + block]

        loop(right.shape[1], 256, body, 4)
        if i >= self.slots:
            pl.semaphore_wait(self.free.at[0], 1)
        self.out[i] = [
            net.send(self.part.at[slot, 1 - net.c], self.from_c.at[slot], self.cs.at[slot], net.device(c=1 - net.c))
        ]

    def step_c(self):
        net = self.net
        i = self.done_c
        self.done_c += 1
        slot = i % self.slots
        net.recv(self.from_c.at[slot], self.cs.at[slot])
        for y in (0, 1):
            self.add(self.part.at[slot, net.c, y], self.from_c.at[slot, y])
        if i + self.slots < self.total:
            self.credit(0, net.device(c=1 - net.c))
        if i >= self.slots:
            pl.semaphore_wait(self.free.at[1], 1)
        self.out[i].append(
            net.send(self.part.at[slot, net.c, 1 - net.y], self.from_y.at[slot], self.ys.at[slot], net.device(y=1 - net.y))
        )

    def step_y(self):
        net = self.net
        i = self.done_y
        self.done_y += 1
        slot = i % self.slots
        matrix, to = self.items[i]
        net.recv(self.from_y.at[slot], self.ys.at[slot])
        self.add(self.part.at[slot, net.c, net.y], self.from_y.at[slot])
        if i + self.slots < self.total:
            self.credit(1, net.device(y=1 - net.y))
        matrices = self.result.shape[0]
        if matrix >= matrices:
            return
        src = self.part.at[slot, net.c, net.y]
        dst = self.result.at[matrix, net.z]
        away = to != net.z
        self.out[i].append(net.send(src, dst, self.zs.at[matrix, net.z], net.device(z=to), away))
        self.out[i].append(net.local(src, dst, jnp.logical_not(away)))
        self.done_z += 1

    def step_z(self):
        net = self.net
        i = self.done_z
        self.done_z += 1
        assert i < self.done_y
        matrix, to = self.items[i]
        m = matrix - self.result.shape[0]
        total = self.part.at[i % self.slots, net.c, net.y]
        behind = jnp.where(to > net.z, net.z > 0, net.z < net.n - 1)
        place = self.line(m, to)

        @pl.when(jnp.logical_and(to != net.z, behind))
        def _():
            net.recv(place, self.ls.at[m, to])
            self.add(total, place)

        side = jnp.where(to > net.z, 0, 1)
        nxt = jnp.where(to > net.z, net.z + 1, net.z - 1)
        there = net.device(z=nxt)
        last = jnp.logical_and(to != net.z, to == nxt)
        self.out[i].append(net.send(total, place, self.ls.at[m, to], there, jnp.logical_and(to != net.z, to != nxt)))
        self.out[i].append(net.send(total, self.totals.at[m, side], self.ls.at[m, net.n + side], there, last))
        self.out[i].append(net.local(total, self.totals.at[m, 2], to == net.z))

    def finish(self):
        net = self.net
        for matrix in range(self.result.shape[0]):
            for d in range(1, net.n):
                block = (net.z + d) % net.n
                net.recv(self.result.at[matrix, block], self.zs.at[matrix, block])
        for m in range(self.totals.shape[0]):
            for side, cond in ((0, net.z > 0), (1, net.z < net.n - 1)):

                @pl.when(cond)
                def _():
                    net.recv(self.totals.at[m, side], self.ls.at[m, net.n + side])


def loop(total, step, body, unroll):
    @pl.loop(0, total // step, unroll=unroll)
    def _(i):
        body(pl.multiple_of(i * step, step))


def turn(field, cosine, sine, lane):
    half = HD // 2
    partner = jnp.where(lane % HD < half, pltpu.roll(field, LANES - half, 1), pltpu.roll(field, half, 1))
    return field * cosine + partner * sine


def head_masks():
    lane = lax.broadcasted_iota(jnp.int32, (1, LANES), 1)
    return (lane < HD).astype(BF16), (lane >= HD).astype(BF16)


def both(field, masks):
    return jnp.concatenate([field * masks[0], field * masks[1]], axis=0)


def pick(stacked, rows):
    lane = lax.broadcasted_iota(jnp.int32, (1, LANES), 1)
    return jnp.where(lane < HD, stacked[:rows], stacked[rows:])


def softmax(queries2, key_rows, allowed):
    scores = dot(queries2, key_rows, NT) * HD ** (-0.5)
    scores = jnp.where(allowed > 0, scores, -1e30)
    raised = jnp.exp(scores - jnp.max(scores, axis=-1, keepdims=True))
    return raised / jnp.sum(raised, axis=-1, keepdims=True)


def far_first(net):
    n = net.n
    table = [sorted(range(n), key=lambda b: (-abs(b - z), -b)) for z in range(n)]
    return [sum(jnp.where(net.z == z, table[z][k], 0) for z in range(n)) for k in range(n)]


class RowSum:
    def __init__(self, net, order, part, from_x, from_z, sems):
        self.net, self.order, self.part, self.from_x, self.from_z = net, order, part, from_x, from_z
        self.xs, self.zs = sems
        self.sent = []
        self.done_x = self.done_z = 0

    def start(self, b):
        net = self.net
        self.sent.append(
            net.send(self.part(b, 1 - net.x), self.from_x.at[b], self.xs.at[b], net.device(x=1 - net.x))
        )

    def add(self, total, term):
        def body(r):
            span = pl.ds(r, 16)
            total[span] = (total[span].astype(F32) + term[span].astype(F32)).astype(BF16)

        loop(total.shape[0], 16, body, 8)

    def step_x(self, k):
        net = self.net
        b = self.order[k]
        self.done_x += 1
        net.recv(self.from_x.at[b], self.xs.at[b])
        self.add(self.part(b, net.x), self.from_x.at[b])

    def step_z(self, k):
        net = self.net
        b = self.order[k]
        self.done_z += 1
        total = self.part(b, net.x)
        behind = jnp.where(b > net.z, net.z > 0, net.z < net.n - 1)

        @pl.when(jnp.logical_and(b != net.z, behind))
        def _():
            net.recv(self.from_z.at[b], self.zs.at[b])
            self.add(total, self.from_z.at[b])

        slot = jnp.where(b == net.z - 1, net.n, b)
        to = jnp.where(b > net.z, net.z + 1, net.z - 1)
        self.sent.append(net.send(total, self.from_z.at[slot], self.zs.at[slot], net.device(z=to), b != net.z))

    def finish(self):
        net = self.net
        total = self.part(net.z, net.x)
        for slot, cond in ((net.z, net.z > 0), (net.n, net.z < net.n - 1)):

            @pl.when(cond)
            def _():
                net.recv(self.from_z.at[slot], self.zs.at[slot])
                self.add(total, self.from_z.at[slot])


def norm_back(grad, value, gain):
    scale = lax.rsqrt(jnp.mean(value * value, axis=-1, keepdims=True) + EPSILON)
    unit = value * scale
    scaled = grad * gain
    back = scale * (scaled - unit * jnp.mean(scaled * unit, axis=-1, keepdims=True))
    return back, grad * unit


def layer_kernel(
    dp,
    residual, seg, attn_gain, ffn_gain, freq, w_out, w_down, w_qkv, w_gate_up, cotangent,
    result, totals, wa_out, wf_out, normed_ffn_out, normed_out, attended_out, qkv_out, block_out, input_grad, gain_out,
    weights, grad, hidden, gate_up_grad, back, back_x, back_z, part, from_c, from_y,
    mixed_all, from_x, pre, mixed, tables, allowed, gains, all_gains, gains_all, gain_sum, ffn_sum, gain_to,
    gain_from, gain_x,
    send_sems, local_sems, gain_sems, q_sems, o_sems, f_sems, g_sems, n_sems, x_sems,
    bx_sems, bz_sems, rc_sems, ry_sems, rz_sems, rl_sems, back_gain_sems, free,
):
    net = Net(dp, send_sems, local_sems)
    n, me, x = net.n, net.dp_index, net.x
    rows, width = residual.shape
    block, cols = w_qkv.shape[1:]
    group = pair = 2 * rows
    every = grad.shape[0]
    depth = width // n
    assert w_gate_up.shape[2] == n * cols and width == 2 * cols and width == 2 * every and width == dp * block
    lane = lax.broadcasted_iota(jnp.int32, (group, LANES), 1)
    live = gain_to
    assert gain_to.shape == (group // 16, 16, LANES)
    order = far_first(net)
    beside = jnp.where(net.z > 0, 1, 0) + jnp.where(net.z < n - 1, 1, 0)
    net.greet([((me + k) % dp, x) for k in range(1, dp)] + [(me, 1 - x)])

    def block_rows_of(z, half):
        return pl.ds(pl.multiple_of((z * 2 + half) * rows, rows), rows)

    normed_all = back.at[0]
    ffn_own, to_x = back.at[1, 0], back.at[1, 1]
    down_own = hidden.at[pl.ds(0, n * block)]
    out_own = hidden.at[pl.ds(n * block, block)]
    early_qkv = [
        gate_up_grad.at[pl.ds(0, group), pl.ds(0, cols)],
        gate_up_grad.at[pl.ds(0, group), pl.ds(cols, cols)],
        gate_up_grad.at[pl.ds(group, group), pl.ds(0, cols)],
    ]
    early_attended = gate_up_grad.at[pl.ds(group, group), pl.ds(cols, cols)]

    def at_weights(first, count):
        return lambda index: weights.at[pl.ds(first, count), pl.ds(pl.multiple_of(index * block, block), block)]

    def at_out(index):
        return weights.at[3, pl.ds(pl.multiple_of(index * block, block), block)]

    def ffn_part(m):
        def own(to):
            if m == 2:
                return down_own.at[pl.ds(pl.multiple_of(to * block, block), block)]
            return w_gate_up.at[m, :, pl.ds(pl.multiple_of(to * cols, cols), cols)]

        return own

    def ffn_place(m):
        return lambda index: wf_out.at[m, pl.ds(pl.multiple_of(index * block, block), block)]

    qkv = Gather(net, w_qkv, at_weights(0, 3), q_sems, "qkv")
    out = Gather(net, out_own, at_out, o_sems, "out")
    ffn = [Exchange(net, ffn_part(m), ffn_place(m), f_sems.at[m], "ffn") for m in range(3)]
    grads = Rows(net, None, lambda z, half: grad.at[block_rows_of(z, half)], g_sems, "grads")
    ffn_rows = Rows(net, ffn_own, lambda z, half: normed_ffn_out.at[z, half], n_sems, "rows")
    load_grad = net.local(cotangent, grad.at[block_rows_of(net.z, x)])

    def send_gains():
        gains[0:8] = jnp.broadcast_to(attn_gain[...].astype(F32), (8, block))
        gains[8:16] = jnp.broadcast_to(ffn_gain[...].astype(F32), (8, block))
        for k in range(1, dp):
            net.send(gains, all_gains.at[me], gain_sems.at[me], ((me + k) % dp, x))
        all_gains[me] = gains[...]

    def turn_weights():
        out_own[...] = w_out[...].T
        for q in range(n):
            down_own[q * block : (q + 1) * block] = w_down[q * cols : (q + 1) * cols].T

    def mask_grads():
        seg_rows = jnp.broadcast_to(seg[...].astype(F32), (LANES, group))
        seg_cols = seg_rows.T
        alive = (seg_cols >= 0).astype(F32)
        for i in range(group // 16):
            live[i] = alive[i * 16 : (i + 1) * 16]
        row_id = lax.broadcasted_iota(jnp.int32, (group, group), 0)
        col_id = lax.broadcasted_iota(jnp.int32, (group, group), 1)
        same = jnp.concatenate([seg_cols] * (group // LANES), axis=1) == jnp.concatenate([seg_rows] * (group // LANES), axis=0)
        mask = jnp.logical_and(same, row_id >= col_id).astype(F32)
        allowed[...] = mask
        angles = (jnp.sum(mask, axis=1, keepdims=True) - 1.0) * freq[...]
        tables[0] = jnp.cos(angles)
        tables[1] = jnp.where(lane % HD < HD // 2, -jnp.sin(angles), jnp.sin(angles))

        net.settle(load_grad)

        def body(r):
            span = pl.ds(pl.multiple_of((net.z * 2 + x) * rows + r, 16), 16)
            grad[span] = (grad[span].astype(F32) * live[(x * rows + r) // 16, :, 0:1]).astype(BF16)

        loop(rows, 16, body, 4)

    def norm():
        for k in range(1, dp):
            source = (me + k) % dp
            net.recv(all_gains.at[source], gain_sems.at[source])
        for i in range(dp):
            gains_all[:, i * block : (i + 1) * block] = all_gains[i]

        def body(r):
            value = residual[pl.ds(r, 16)].astype(F32)
            unit = value * lax.rsqrt(jnp.mean(value * value, axis=-1, keepdims=True) + EPSILON)
            normed_all[x, pl.ds(r, 16)] = (unit * gains_all[0:1]).astype(BF16)

        loop(rows, 16, body, 4)
        net.tag("normed", [net.send(normed_all.at[x], normed_all.at[x], x_sems.at[0], net.device(x=1 - x))])

    def project(k):
        if k == 0:
            net.recv(normed_all.at[1 - x], x_sems.at[0])
            net.settle(qkv.kept)
            net.tag("normed", [net.local(normed_all.at[half], normed_out.at[pl.ds(half * rows, rows)]) for half in (0, 1)])
        b = (net.z + k) % n
        qkv.finish(b)
        base = pl.multiple_of(b * depth, depth)

        def body(col):
            left = jnp.concatenate([normed_all[0, :, pl.ds(base, depth)], normed_all[1, :, pl.ds(base, depth)]], axis=0)
            for m in range(3):
                term = dot(left, weights[m, pl.ds(base, depth), pl.ds(col, 256)])
                to = pl.ds(pl.multiple_of(m * cols + col, 256), 256)
                pre[:, to] = term if k == 0 else pre[:, to] + term

        loop(cols, 256, body, 4)
        if k == n - 1:
            net.tag("save", [net.local(weights.at[pl.ds(0, 3)], wa_out.at[pl.ds(0, 3)])])

    def attend():
        masks = head_masks()

        def body(col):
            cosine, sine = tables[0], tables[1]
            queries = turn(pre[:, pl.ds(col, LANES)], cosine, sine, lane).astype(BF16)
            key_rows = turn(pre[:, pl.ds(pl.multiple_of(cols + col, LANES), LANES)], cosine, sine, lane).astype(BF16)
            value_rows = pre[:, pl.ds(pl.multiple_of(2 * cols + col, LANES), LANES)].astype(BF16)
            early_qkv[0][:, pl.ds(col, LANES)] = queries
            early_qkv[1][:, pl.ds(col, LANES)] = key_rows
            early_qkv[2][:, pl.ds(col, LANES)] = value_rows
            may = jnp.concatenate([allowed[...], allowed[...]], axis=0)
            probs = softmax(both(queries, masks), key_rows, may).astype(BF16)
            early_attended[:, pl.ds(col, LANES)] = pick(dot(probs, value_rows), group).astype(BF16)

        loop(cols, LANES, body, 4)
        net.tag("early", [net.local(early_qkv[m], qkv_out.at[m]) for m in range(3)])
        net.tag("early", [net.local(early_attended, attended_out)])

    def join():
        for k in range(n):
            out.finish((net.z + k) % n)
        net.settle(out.kept)
        net.tag("save_out", [net.local(weights.at[3], wa_out.at[3])])

        def body(col):
            span = pl.ds(col, 256)
            term = dot(early_attended[...], weights[3, span, :], NT)
            low, high = term[:rows], term[rows:]
            input_grad[:, span] = jnp.where(x == 0, low, high)
            to_x[:, span] = jnp.where(x == 0, high, low).astype(BF16)

        loop(width, 256, body, 4)
        net.tag("to_x", [net.send(to_x, from_x, x_sems.at[1], net.device(x=1 - x))])

    def mix():
        net.recv(from_x, x_sems.at[1])

        def body(r):
            span = pl.ds(r, 16)
            value = residual[span].astype(F32) + input_grad[span] + from_x[span].astype(F32)
            mixed[span] = value
            unit = value * lax.rsqrt(jnp.mean(value * value, axis=-1, keepdims=True) + EPSILON)
            ffn_own[span] = (unit * gains_all[8:9]).astype(BF16)

        loop(rows, 16, body, 4)

    def load_ffn(m):
        for k in range(n):
            ffn[m].finish((net.z + k) % n)
        net.settle(ffn[m].kept)
        net.settle_tag("qkv", "save")
        net.tag("weights", [net.local(wf_out.at[m], weights.at[m])])

    def load_rows(k):
        net.settle_tag("out", "save_out", "rows_kept")
        b = order[k]
        ffn_rows.finish(b)
        for x_half in (0, 1):
            for half in (0, 1):
                there = pl.ds(pl.multiple_of(half * every + (b * 2 + x_half) * rows, rows), rows)
                src = normed_ffn_out.at[b, x_half, :, pl.ds(half * cols, cols)]
                net.tag("load%d" % k, [net.local(src, weights.at[3, there])])

    def ffn_step(m, k):
        ffn[m].step((net.z + k) % n)

    def ffn_cross(m):
        for k in range(n):
            ffn[m].cross((net.z + k) % n)


    def features(half):
        return weights.at[3, pl.ds(half * every, every)]

    gate_grad, up_grad = gate_up_grad.at[:, pl.ds(0, cols)], gate_up_grad.at[:, pl.ds(cols, cols)]
    add = gate_up_grad
    backs = RowSum(net, order, lambda b, half: back.at[b, half], back_x, back_z, (bx_sems, bz_sems))
    adds = RowSum(
        net, order, lambda b, half: add.at[pl.ds(pl.multiple_of((b * 2 + half) * rows, rows), rows)],
        back_x, back_z, (bx_sems, bz_sems),
    )
    red = Reduce(
        net, part, from_c, from_y, (result, totals),
        lambda m, to: weights.at[3, pl.ds(pl.multiple_of((m * n + to) * block, block), block)],
        (rc_sems, ry_sems, rz_sems, rl_sems, free), 7 * n,
    )
    def rows_of(b):
        return pl.ds(pl.multiple_of(b * pair, pair), pair)

    def forward(k):
        net.settle_tag("load%d" % k, "weights", "ffn", "early")
        grads.finish(order[k])
        here = rows_of(order[k])

        def body(col):
            span = pl.ds(col, 256)

            def project(m):
                return dot(features(0)[here], weights[m, pl.ds(0, cols), span]) + dot(
                    features(1)[here], weights[m, pl.ds(cols, cols), span]
                )

            gate, up = project(0), project(1)
            hidden_grad = dot(grad[here], weights[2, :, span])
            sigmoid = 1.0 / (1.0 + jnp.exp(-gate))
            active = gate * sigmoid
            hidden[here, span] = (active * up).astype(BF16)
            gate_grad[here, span] = (hidden_grad * up * sigmoid * (1.0 + gate * (1.0 - sigmoid))).astype(BF16)
            up_grad[here, span] = (hidden_grad * active).astype(BF16)

        loop(cols, 256, body, 4)

    def backward(k):
        net.settle_tag("normed", "to_x", "rows")
        b = order[k]
        here = rows_of(b)

        def body(col):
            span = pl.ds(col, 256)
            term = dot(gate_grad[here], weights[0, span, :], NT) + dot(up_grad[here], weights[1, span, :], NT)
            term = term.astype(BF16)
            back[b, 0, :, span] = term[:rows]
            back[b, 1, :, span] = term[rows:]

        loop(width, 256, body, 4)
        backs.start(b)

    def add_chunk(k):
        here = rows_of(order[k])

        def body(col):
            span = pl.ds(col, 256)
            add[here, span] = dot(hidden[here], weights[2, span, :], NT).astype(BF16)

        loop(width, 256, body, 4)
        if k == 0:
            pl.semaphore_wait(free.at[2], 1)
        adds.start(order[k])

    ffn_items = [(2, k) for k in range(n)] + [(m, k) for k in range(n) for m in (0, 1)]
    attention_items = [(3, k) for k in range(n)] + [(m, k) for k in range(n) for m in range(3)]

    def ffn_item():
        m, k = ffn_items[len(red.items)]
        b = order[k]
        base = b * depth
        if m == 2:
            left = grad[:, pl.ds(pl.multiple_of(base, depth), depth)]
        else:
            row = pl.ds(pl.multiple_of(base // cols * every, every), every)
            left = weights[3, row, pl.ds(pl.multiple_of(base % cols, depth), depth)]
        red.item(m, b, left, (gate_grad, up_grad, hidden)[m], depth, block)

    def attention_item():
        m, k = attention_items[len(red.items) - len(ffn_items)]
        base = pl.ds(pl.multiple_of(order[k] * depth, depth), depth)
        left, right = (mixed_all, attended) if m == 3 else (normed, grads_of[m])
        red.item(3 + m, order[k], left[:, base], right, depth, block)

    queries_of, keys_of, values_of = [hidden.at[pl.ds(m * pair, pair)] for m in range(3)]
    attended = hidden.at[pl.ds(3 * pair, pair)]
    normed = grad.at[pl.ds(0, pair)]
    grads_of = [
        grad.at[pl.ds(2 * pair, pair), pl.ds(0, cols)],
        grad.at[pl.ds(2 * pair, pair), pl.ds(cols, cols)],
        grad.at[pl.ds(3 * pair, pair), pl.ds(0, cols)],
    ]
    attended_grad = grad.at[pl.ds(3 * pair, pair), pl.ds(cols, cols)]
    own_rows = mixed_all.at[pl.ds(pl.multiple_of(x * rows, rows), rows)]
    other_rows = mixed_all.at[pl.ds(pl.multiple_of((1 - x) * rows, rows), rows)]
    late = {}

    def tell_beside(which):
        for cond, z in ((net.z > 0, net.z - 1), (net.z < n - 1, net.z + 1)):

            @pl.when(cond)
            def _():
                pl.semaphore_signal(free.at[which], inc=1, device_id=net.device(z=z), device_id_type=MESH)

    def mix_grads():
        backs.finish()
        ffn_sum[...] = jnp.zeros_like(ffn_sum)

        def body(r):
            span = pl.ds(r, 16)
            own = pl.ds(pl.multiple_of((net.z * 2 + x) * rows + r, 16), 16)
            term, gain_term = norm_back(back[net.z, x, span].astype(F32), mixed[span], gains_all[8:9])
            value = grad[own].astype(F32) + term
            input_grad[span] = value
            mixed_all[pl.ds(pl.multiple_of(x * rows + r, 16), 16)] = value.astype(BF16)
            ffn_sum[...] += gain_term[:8] + gain_term[8:]

        loop(rows, 16, body, 4)
        net.send(own_rows, own_rows, x_sems.at[2], net.device(x=1 - x))
        pl.semaphore_signal(free.at[2], inc=1, device_id=net.device(x=1 - x), device_id_type=MESH)
        tell_beside(3)

    def load_out():
        late["out"] = net.local(wa_out.at[3], weights.at[3])

    def load_rest():
        net.settle_tag("grads")
        late["normed"] = net.local(normed_out, normed)
        late["qkv"] = net.local(wa_out.at[pl.ds(0, 3)], weights.at[pl.ds(0, 3)])
        late["parts"] = [net.local(qkv_out.at[m], hidden.at[pl.ds(m * pair, pair)]) for m in range(3)]
        late["attended"] = net.local(attended_out, attended)

    def step_adds():
        if adds.done_z == 0:
            pl.semaphore_wait(free.at[3], beside)
        adds.step_z(adds.done_z)

    def attended_back():
        net.settle(late["out"])
        net.recv(other_rows, x_sems.at[2])

        def body(col):
            span = pl.ds(col, 256)
            attended_grad[:, span] = dot(mixed_all[...], weights[3, :, span]).astype(BF16)

        loop(cols, 256, body, 4)
        tell_beside(4)
        net.settle(late["attended"])

    def heads():
        for load in late["parts"]:
            net.settle(load)
        masks = head_masks()

        def body(col):
            span = pl.ds(col, LANES)
            cosine, sine = tables[0], tables[1]
            queries, key_rows, value_rows = queries_of[:, span], keys_of[:, span], values_of[:, span]
            out_grad = attended_grad[:, span]
            queries2, out_grad2 = both(queries, masks), both(out_grad, masks)
            may = jnp.concatenate([allowed[...], allowed[...]], axis=0)
            probs = softmax(queries2, key_rows, may)
            value_grad = dot(probs.astype(BF16), out_grad2, TN)
            prob_grad = dot(out_grad2, value_rows, NT)
            score_grad = probs * (prob_grad - jnp.sum(probs * prob_grad, axis=-1, keepdims=True))
            score_grad = score_grad.astype(BF16)
            query_grad = pick(dot(score_grad, key_rows), pair) * HD ** (-0.5)
            key_grad = dot(score_grad, queries2, TN) * HD ** (-0.5)
            grads_of[0][:, span] = turn(query_grad, cosine, -sine, lane).astype(BF16)
            grads_of[1][:, span] = turn(key_grad, cosine, -sine, lane).astype(BF16)
            grads_of[2][:, span] = value_grad.astype(BF16)

        loop(cols, LANES, body, 4)
        net.settle(late["normed"])

    def normed_back():
        net.settle(late["qkv"])
        for entry in backs.sent:
            net.settle(entry)

        def body(col):
            span = pl.ds(col, 256)
            term = dot(grads_of[0][...], weights[0, span, :], NT)
            term += dot(grads_of[1][...], weights[1, span, :], NT)
            term += dot(grads_of[2][...], weights[2, span, :], NT)
            back[0, 0, :, span] = term[:rows].astype(BF16)
            back[0, 1, :, span] = term[rows:].astype(BF16)

        loop(width, 256, body, 4)
        net.send(back.at[0, 1 - x], from_x, x_sems.at[3], net.device(x=1 - x))

    def input_back():
        net.recv(from_x, x_sems.at[3])
        gain_sum[...] = jnp.zeros_like(gain_sum)

        def body(r):
            span = pl.ds(r, 16)
            grad_rows = back[0, x, span].astype(F32) + from_x[span].astype(F32)
            term, gain_term = norm_back(grad_rows, residual[span].astype(F32), gains_all[0:1])
            input_grad[span] += term
            gain_sum[...] += gain_term[:8] + gain_term[8:]

        loop(rows, 16, body, 4)
        for i in range(dp):
            gain_to[i, 0:8] = gain_sum[:, i * block : (i + 1) * block]
            gain_to[i, 8:16] = ffn_sum[:, i * block : (i + 1) * block]
        for k in range(1, dp):
            to = (me + k) % dp
            net.send(gain_to.at[to], gain_from.at[me], back_gain_sems.at[me], (to, x))

    def sum_gains():
        total = gain_to[me]
        for k in range(1, dp):
            source = (me + k) % dp
            net.recv(gain_from.at[source], back_gain_sems.at[source])
            total = total + gain_from[source]
        gain_x[0] = total
        net.send(gain_x.at[0], gain_x.at[1], x_sems.at[4], net.device(x=1 - x))

    def block_rows():
        adds.finish()

        def body(r):
            span = pl.ds(r, 16)
            block_out[span] = (mixed[span] + adds.part(net.z, x)[span].astype(F32)).astype(BF16)

        loop(rows, 16, body, 4)

    qkv.start()
    turn_weights()
    out.start()
    send_gains()
    qkv.step(1)
    mask_grads()
    norm()
    qkv.cross_step(0)
    out.step(1)
    qkv.step(2)
    ffn[2].start()
    out.step(2)
    qkv.cross_step(1)
    grads.start()
    qkv.step(3)
    ffn_step(2, 3)
    qkv.cross_step(2)
    out.step(3)
    ffn[0].start()
    qkv.cross_step(3)
    out.cross_step(0)
    project(0)
    grads.step(1)
    project(1)
    project(2)
    out.cross_step(1)
    out.cross_step(2)
    out.cross_step(3)
    ffn_step(2, 2)
    project(3)
    ffn[1].start()
    ffn_step(2, 1)
    attend()
    join()
    ffn_step(0, 2)
    grads.step(2)
    ffn_step(0, 1)
    ffn_cross(2)
    mix()
    ffn_rows.start()
    load_ffn(2)
    ffn_step(0, 3)
    ffn_step(1, 2)
    ffn_step(1, 3)
    grads.step(3)
    ffn_cross(0)
    load_rows(3)
    ffn_step(1, 1)
    ffn_rows.step(1)
    ffn_cross(1)
    ffn_rows.step(2)
    load_rows(2)
    load_ffn(1)
    load_ffn(0)
    ffn_rows.step(3)
    forward(3)
    forward(2)
    load_rows(1)
    backward(2)
    forward(1)
    load_rows(0)
    forward(0)
    ffn_item()
    backward(0)
    red.step_c()
    ffn_item()
    ffn_item()
    red.step_c()
    red.step_y()
    backward(1)
    red.step_c()
    backs.step_x(0)
    backs.step_z(0)
    red.step_y()
    ffn_item()
    ffn_item()
    red.step_c()
    red.step_c()
    backs.step_x(2)
    backs.step_x(1)
    backs.step_z(1)
    backs.step_z(2)
    ffn_item()
    red.step_c()
    ffn_item()
    ffn_item()
    red.step_y()
    backward(3)
    red.step_c()
    backs.step_x(3)
    ffn_item()
    red.step_c()
    ffn_item()
    red.step_c()
    red.step_y()
    ffn_item()
    mix_grads()
    red.step_y()
    red.step_c()
    ffn_item()
    add_chunk(0)
    load_out()
    red.step_y()
    red.step_y()
    add_chunk(1)
    add_chunk(2)
    red.step_y()
    red.step_c()
    red.step_c()
    add_chunk(3)
    load_rest()
    red.step_y()
    attended_back()
    attention_item()
    heads()
    red.step_c()
    for _ in range(3):
        red.step_y()
    attention_item()
    attention_item()
    red.step_c()
    pl.semaphore_wait(free.at[4], beside)
    attention_item()
    red.step_y()
    red.step_z()
    attention_item()
    red.step_y()
    red.step_c()
    red.step_c()
    adds.step_x(adds.done_x)
    red.step_c()
    red.step_z()
    attention_item()
    step_adds()
    normed_back()
    red.step_y()
    attention_item()
    red.step_z()
    attention_item()
    attention_item()
    red.step_c()
    attention_item()
    red.step_y()
    red.step_y()
    red.step_c()
    adds.step_x(adds.done_x)
    attention_item()
    red.step_c()
    red.step_c()
    red.step_y()
    step_adds()
    red.step_c()
    attention_item()
    red.step_c()
    adds.step_x(adds.done_x)
    red.step_z()
    red.step_c()
    red.step_z()
    step_adds()
    red.step_z()
    adds.step_x(adds.done_x)
    attention_item()
    red.step_y()
    red.step_y()
    red.step_z()
    red.step_y()
    red.step_c()
    attention_item()
    red.step_y()
    attention_item()
    input_back()
    red.step_z()
    red.step_z()
    red.step_y()
    red.step_c()
    red.step_c()
    step_adds()
    block_rows()
    attention_item()
    red.step_y()
    red.step_y()
    for _ in range(3):
        red.step_z()
    red.step_c()
    red.step_z()
    red.step_y()
    red.step_y()
    sum_gains()
    red.step_y()
    for _ in range(3):
        red.step_z()
    assert red.done_y == red.done_z == red.total and adds.done_z == n and backs.done_x == n
    net.recv(gain_x.at[1], x_sems.at[4])
    gain_out[...] = gain_x[0] + gain_x[1]
    red.finish()
    net.drain()


def finish_kernel(
    ffn, attention, gains, block_rows, input_rows,
    qkv_grad, out_grad, gate_up_grad, down_grad, attn_gain_grad, ffn_gain_grad, block_out, input_grad,
):
    q, n = pl.program_id(0), pl.num_programs(0)
    z = lax.axis_index("dp") // 4
    gate_up_grad[...] = ffn[0:2, 0].astype(F32)
    down_grad[...] = ffn[2, 0].astype(F32).T
    total = attention[0, 2].astype(F32)
    total += jnp.where(z > 0, attention[0, 0].astype(F32), 0.0)
    total += jnp.where(z < n - 1, attention[0, 1].astype(F32), 0.0)

    @pl.when(q < 3)
    def _():
        qkv_grad[0] = total

    @pl.when(q == 3)
    def _():
        out_grad[...] = total.T

    attn_gain_grad[...] = jnp.sum(gains[0:8], axis=0, keepdims=True)
    ffn_gain_grad[...] = jnp.sum(gains[8:16], axis=0, keepdims=True)
    block_out[...] = block_rows[...]
    input_grad[...] = input_rows[...]


def call(kernel, collective_id, sends, locals_, vmem, outs, out_specs, scratch, sems, flags=0):
    def typed(entry):
        return (entry[:-1], F32) if entry[-1] is F32 else (entry, BF16)

    dma = pltpu.SemaphoreType.DMA
    return lambda in_specs, *args: pl.pallas_call(
        kernel,
        out_shape=[jax.ShapeDtypeStruct(*typed(entry)) for entry in outs],
        in_specs=in_specs,
        out_specs=out_specs,
        scratch_shapes=[pltpu.VMEM(*typed(entry)) for entry in scratch] + [dma((sends,)), dma((locals_,))] + [dma(entry) for entry in sems] + [pltpu.SemaphoreType.REGULAR((flags,))] * (flags > 0),
        compiler_params=pltpu.CompilerParams(collective_id=collective_id, has_side_effects=True, vmem_limit_bytes=vmem),
    )(*args)


def shards(dp, residual, seg_ids, attn_gain, w_qkv, w_out, ffn_gain, w_gate_up, w_down, cotangent):
    n = dp // 4
    rows, width = residual.shape
    group = seg_ids.shape[0]
    block, cols = w_qkv.shape[1:]
    part = w_gate_up.shape[2] // n
    pairs = np.arange(LANES) % (HD // 2)
    freq = jnp.asarray(ROPE_BASE ** (-2.0 * pairs / HD), F32)[None]
    every = n * 2 * rows
    slots = SLOTS
    layer = call(
        functools.partial(layer_kernel, dp), 1, 320, 112, LIMIT,
        [
            (3, n, block, part), (4, 3, block, cols), (4, width, cols), (3, width, part), (n, 2, rows, width),
            (group, width), (group, cols), (3, group, cols), (rows, width), (rows, width, F32), (16, block, F32),
        ],
        [ANY] * 8 + [VM] * 3,
        [
            (4, width, cols), (every, width), (every, part), (every, 2 * part),
            (n, 2, rows, width), (n, rows, width), (n + 1, rows, width),
            (slots, 2, 2, block, part), (slots, 2, block, part), (slots, block, part),
            (group, width), (rows, width), (group, 3 * cols, F32), (rows, width, F32), (2, group, LANES, F32),
            (group, group, F32), (16, block, F32), (dp, 16, block, F32), (16, width, F32),
            (8, width, F32), (8, width, F32), (dp, 16, block, F32), (dp, 16, block, F32), (2, 16, block, F32),
        ],
        [
            (dp,), (4, n), (4, n), (3, 4, n), (2, n), (2, n), (5,),
            (n,), (n + 1,), (slots,), (slots,), (3, n), (4, n + 2), (dp,),
        ],
        5,
    )
    outputs = layer(
        [VM] * 7 + [ANY] * 3, residual, seg_ids[None], attn_gain[None], ffn_gain[None], freq, w_out, w_down, w_qkv,
        w_gate_up, cotangent,
    )
    result, totals, block_out, input_grad, gain_grads = outputs[0], outputs[1], outputs[8], outputs[9], outputs[10]
    qkv_grad, out_grad, gate_up_grad, down_grad, attn_gain_grad, ffn_gain_grad, block_out, input_grad = pl.pallas_call(
        finish_kernel,
        grid=(n,),
        out_shape=[
            jax.ShapeDtypeStruct(entry, F32)
            for entry in (
                (3, block, cols), (cols, block), (2, block, n * part), (n * part, block), (1, block), (1, block)
            )
        ] + [jax.ShapeDtypeStruct((rows, width), BF16), jax.ShapeDtypeStruct((rows, width), F32)],
        in_specs=[
            pl.BlockSpec((3, 1, block, part), lambda q: (0, q, 0, 0)),
            pl.BlockSpec((1, 3, block, cols), lambda q: (q, 0, 0, 0)),
            pl.BlockSpec((16, block), lambda q: (0, 0)),
            pl.BlockSpec((rows // n, width), lambda q: (q, 0)),
            pl.BlockSpec((rows // n, width), lambda q: (q, 0)),
        ],
        out_specs=[
            pl.BlockSpec((1, block, cols), lambda q: (jnp.minimum(q, 2), 0, 0)),
            pl.BlockSpec((cols, block), lambda q: (0, 0)),
            pl.BlockSpec((2, block, part), lambda q: (0, 0, q)),
            pl.BlockSpec((part, block), lambda q: (q, 0)),
            pl.BlockSpec((1, block), lambda q: (0, 0)),
            pl.BlockSpec((1, block), lambda q: (0, 0)),
            pl.BlockSpec((rows // n, width), lambda q: (q, 0)),
            pl.BlockSpec((rows // n, width), lambda q: (q, 0)),
        ],
        compiler_params=pltpu.CompilerParams(vmem_limit_bytes=LIMIT),
    )(result, totals, gain_grads, block_out, input_grad)
    return (
        block_out, input_grad, attn_gain_grad.reshape(block), qkv_grad, out_grad, ffn_gain_grad.reshape(block),
        gate_up_grad, down_grad,
    )


def positions(segments):
    row_index = jnp.arange(segments.shape[1], dtype=jnp.int32)[None, :]
    previous = jnp.concatenate([segments[:, :1] - 1, segments[:, :-1]], axis=1)
    run_start = lax.cummax(jnp.where(segments != previous, row_index, 0), axis=1)
    return row_index - run_start


def rope_tables(places, head_dim):
    half_dim = head_dim // 2
    frequency = ROPE_BASE ** (-(jnp.arange(half_dim, dtype=jnp.float32) * 2.0 / head_dim))
    angles = places.astype(jnp.float32)[:, None, None] * frequency[None, None, :]
    return (jnp.cos(angles), jnp.sin(angles))


def rotate(field, cosine, sine_table):
    half_dim = field.shape[-1] // 2
    lower_half = field[..., :half_dim]
    upper_half = field[..., half_dim:]
    return jnp.concatenate(
        [
            lower_half * cosine - upper_half * sine_table,
            upper_half * cosine + lower_half * sine_table,
        ],
        axis=-1,
    )


def unrotate(field, cosine, sine_table):
    half_dim = field.shape[-1] // 2
    lower_half = field[..., :half_dim]
    upper_half = field[..., half_dim:]
    return jnp.concatenate(
        [
            lower_half * cosine + upper_half * sine_table,
            upper_half * cosine - lower_half * sine_table,
        ],
        axis=-1,
    )


def attention_scores(queries, key_rows, allowed):
    scores = jnp.einsum(
        "qhd,khd->hqk", queries, key_rows, preferred_element_type=jnp.float32
    ) * queries.shape[-1] ** (-0.5)
    return jnp.where(allowed[None], scores, -1e30)


def plain_shards(residual_in, seg_ids, attn_gain, w_qkv, w_out, ffn_gain, w_gate_up, w_down, cotangent):
    rows_local = residual_in.shape[0]
    group_rows = seg_ids.shape[0]
    offset = lax.axis_index("tensor") * rows_local
    live_rows = (lax.dynamic_slice_in_dim(seg_ids, offset, rows_local) >= 0).astype(jnp.float32)
    residual = residual_in.astype(jnp.float32)
    contract_rows = (((0,), (0,)), ((), ()))
    contract_cols = (((1,), (1,)), ((), ()))
    gain_attn, qkv_full, out_full = (
        lax.all_gather(attn_gain, "dp", axis=0, tiled=True),
        lax.all_gather(w_qkv, "dp", axis=1, tiled=True),
        lax.all_gather(w_out, "dp", axis=1, tiled=True),
    )
    norm_attn = lax.rsqrt(jnp.mean(residual * residual, axis=-1, keepdims=True) + EPSILON)
    unit_attn = residual * norm_attn
    normed = (unit_attn * gain_attn.astype(jnp.float32)).astype(jnp.bfloat16)
    normed_all = lax.all_gather(normed, "tensor", axis=0, tiled=True)
    projected = jnp.einsum("rd,cde->cre", normed_all, qkv_full, preferred_element_type=jnp.float32)
    head_count = qkv_full.shape[2] // HD
    head_shape = (group_rows, head_count, HD)
    cosine, sine_table = rope_tables(positions(seg_ids[None, :])[0], HD)
    queries = rotate(projected[0].reshape(head_shape), cosine, sine_table).astype(jnp.bfloat16)
    key_rows = rotate(projected[1].reshape(head_shape), cosine, sine_table).astype(jnp.bfloat16)
    value_rows = projected[2].reshape(head_shape).astype(jnp.bfloat16)
    row_index = jnp.arange(group_rows)
    allowed = (seg_ids[:, None] == seg_ids[None, :]) & (row_index[:, None] >= row_index[None, :])
    scores = attention_scores(queries, key_rows, allowed)
    row_top = jnp.max(scores, axis=-1, keepdims=True)
    log_total = row_top + jnp.log(jnp.sum(jnp.exp(scores - row_top), axis=-1, keepdims=True))
    weights = jnp.exp(scores - log_total).astype(jnp.bfloat16)
    attended = jnp.einsum("hqk,khd->qhd", weights, value_rows, preferred_element_type=jnp.float32)
    attended = attended.reshape(group_rows, head_count * HD).astype(jnp.bfloat16)
    mixed = residual + lax.psum_scatter(
        jnp.dot(attended, out_full, preferred_element_type=jnp.float32),
        "tensor",
        scatter_dimension=0,
        tiled=True,
    )
    gain_ffn, gate_up_full, down_full = (
        lax.all_gather(ffn_gain, "dp", axis=0, tiled=True),
        lax.all_gather(w_gate_up, "dp", axis=1, tiled=True),
        lax.all_gather(w_down, "dp", axis=1, tiled=True),
    )
    norm_ffn = lax.rsqrt(jnp.mean(mixed * mixed, axis=-1, keepdims=True) + EPSILON)
    unit_ffn = mixed * norm_ffn
    normed_ffn = (unit_ffn * gain_ffn.astype(jnp.float32)).astype(jnp.bfloat16)
    normed_ffn_all = lax.all_gather(normed_ffn, "tensor", axis=0, tiled=True)
    gate_up = jnp.einsum(
        "rd,cde->cre", normed_ffn_all, gate_up_full, preferred_element_type=jnp.float32
    )
    gate_pre = gate_up[0]
    up_pre = gate_up[1]
    sigmoid_gate = jax.nn.sigmoid(gate_pre)
    activated = gate_pre * sigmoid_gate
    hidden = (activated * up_pre).astype(jnp.bfloat16)
    output = mixed + lax.psum_scatter(
        jnp.dot(hidden, down_full, preferred_element_type=jnp.float32).astype(jnp.bfloat16),
        "tensor",
        scatter_dimension=0,
        tiled=True,
    ).astype(jnp.float32)
    grad_out = cotangent.astype(jnp.float32) * live_rows[:, None]
    grad_all = lax.all_gather(grad_out.astype(jnp.bfloat16), "tensor", axis=0, tiled=True)
    down_grad = lax.dot_general(hidden, grad_all, contract_rows, preferred_element_type=jnp.float32)
    hidden_grad = lax.dot_general(
        grad_all, down_full, contract_cols, preferred_element_type=jnp.float32
    )
    gate_grads = jnp.stack(
        [
            hidden_grad * up_pre * sigmoid_gate * (1.0 + gate_pre * (1.0 - sigmoid_gate)),
            hidden_grad * activated,
        ]
    ).astype(jnp.bfloat16)
    gate_up_grad = jnp.einsum(
        "rd,cre->cde", normed_ffn_all, gate_grads, preferred_element_type=jnp.float32
    )
    normed_ffn_grad = lax.psum_scatter(
        jnp.einsum("cre,cde->rd", gate_grads, gate_up_full, preferred_element_type=jnp.float32),
        "tensor",
        scatter_dimension=0,
        tiled=True,
    )
    ffn_gain_part = jnp.sum(normed_ffn_grad * unit_ffn, axis=0)
    scaled_ffn = normed_ffn_grad * gain_ffn.astype(jnp.float32)
    mixed_grad = grad_out + norm_ffn * (
        scaled_ffn - unit_ffn * jnp.mean(scaled_ffn * unit_ffn, axis=-1, keepdims=True)
    )
    mixed_all = lax.all_gather(mixed_grad.astype(jnp.bfloat16), "tensor", axis=0, tiled=True)
    out_grad = lax.dot_general(
        attended, mixed_all, contract_rows, preferred_element_type=jnp.float32
    )
    attended_grad = lax.dot_general(
        mixed_all, out_full, contract_cols, preferred_element_type=jnp.float32
    )
    attended_grad = attended_grad.astype(jnp.bfloat16).reshape(head_shape)
    probabilities = jnp.exp(attention_scores(queries, key_rows, allowed) - log_total)
    value_grad = jnp.einsum(
        "hqk,qhd->khd",
        probabilities.astype(jnp.bfloat16),
        attended_grad,
        preferred_element_type=jnp.float32,
    )
    prob_grad = jnp.einsum(
        "qhd,khd->hqk", attended_grad, value_rows, preferred_element_type=jnp.float32
    )
    score_grad = (
        probabilities * (prob_grad - jnp.sum(probabilities * prob_grad, axis=-1, keepdims=True))
    ).astype(jnp.bfloat16)
    scale_factor = HD ** (-0.5)
    query_grad = (
        jnp.einsum("hqk,khd->qhd", score_grad, key_rows, preferred_element_type=jnp.float32)
        * scale_factor
    )
    key_grad = (
        jnp.einsum("hqk,qhd->khd", score_grad, queries, preferred_element_type=jnp.float32)
        * scale_factor
    )
    qkv_grads = jnp.stack(
        [
            unrotate(query_grad, cosine, sine_table),
            unrotate(key_grad, cosine, sine_table),
            value_grad,
        ]
    )
    qkv_grads = qkv_grads.reshape(3, group_rows, head_count * HD).astype(jnp.bfloat16)
    qkv_grad = jnp.einsum("rd,cre->cde", normed_all, qkv_grads, preferred_element_type=jnp.float32)
    normed_grad = lax.psum_scatter(
        jnp.einsum("cre,cde->rd", qkv_grads, qkv_full, preferred_element_type=jnp.float32),
        "tensor",
        scatter_dimension=0,
        tiled=True,
    )
    attn_gain_part = jnp.sum(normed_grad * unit_attn, axis=0)
    scaled_attn = normed_grad * gain_attn.astype(jnp.float32)
    input_grad = mixed_grad + norm_attn * (
        scaled_attn - unit_attn * jnp.mean(scaled_attn * unit_attn, axis=-1, keepdims=True)
    )
    (
        query_total,
        key_total,
        value_total,
        out_total,
        attn_gain_total,
        gate_total,
        up_total,
        down_total,
        ffn_gain_total,
    ) = (
        lax.psum_scatter(qkv_grad[0], "dp", scatter_dimension=0, tiled=True),
        lax.psum_scatter(qkv_grad[1], "dp", scatter_dimension=0, tiled=True),
        lax.psum_scatter(qkv_grad[2], "dp", scatter_dimension=0, tiled=True),
        lax.psum_scatter(out_grad, "dp", scatter_dimension=1, tiled=True),
        lax.psum_scatter(attn_gain_part, "dp", scatter_dimension=0, tiled=True),
        lax.psum_scatter(gate_up_grad[0], "dp", scatter_dimension=0, tiled=True),
        lax.psum_scatter(gate_up_grad[1], "dp", scatter_dimension=0, tiled=True),
        lax.psum_scatter(down_grad, "dp", scatter_dimension=1, tiled=True),
        lax.psum_scatter(ffn_gain_part, "dp", scatter_dimension=0, tiled=True),
    )
    gate_up_total = jnp.stack([gate_total, up_total])
    qkv_total = jnp.stack([query_total, key_total, value_total])
    attn_gain_sum, ffn_gain_sum = lax.psum((attn_gain_total, ffn_gain_total), "tensor")
    return (
        output.astype(jnp.bfloat16),
        input_grad,
        attn_gain_sum,
        qkv_total,
        out_total,
        ffn_gain_sum,
        gate_up_total,
        down_total,
    )


def solution(mesh):
    in_specs = (
        P(("dp", "tensor"), None),
        P("dp"),
        P("dp"),
        P(None, "dp", "tensor"),
        P("tensor", "dp"),
        P("dp"),
        P(None, "dp", "tensor"),
        P("tensor", "dp"),
        P(("dp", "tensor"), None),
    )
    out_specs = (
        P(("dp", "tensor"), None),
        P(("dp", "tensor"), None),
        P("dp"),
        P(None, "dp", "tensor"),
        P("tensor", "dp"),
        P("dp"),
        P(None, "dp", "tensor"),
        P("tensor", "dp"),
    )
    dp = mesh.shape["dp"]
    local = functools.partial(shards, dp) if dp == 16 else plain_shards
    return jax.shard_map(local, mesh=mesh, in_specs=in_specs, out_specs=out_specs, check_vma=False)
```
